32 devices in a mesh: dp: 16 (over z, x, core), tensor: 2 (over y).
Axes of the slice: x: 2, y: 2, z: 4, core: 2. Of those that a mesh axis runs over, the one named last changes fastest.
Arguments:
- context: bfloat16 [6144, 8192], P('dp', 'tensor'), may hold values from -6 to 6
- output_weight: bfloat16 [8192, 8192], P('tensor', 'dp'), may hold values from -0.0625 to 0.0625
- adapter_down_weight: bfloat16 [8192, 16], P('tensor'), may hold values from -0.0625 to 0.0625
- adapter_up_weight: bfloat16 [16, 8192], replicated, may hold values from -0.29882812 to 0.29882812
- residual: bfloat16 [6144, 8192], P('dp', 'tensor'), may hold values from -60 to 60
- frozen_residual_delta: bfloat16 [6144, 8192], P('dp', 'tensor'), may hold values from -6 to 6
- harmful_count: int32 [16], replicated, may hold values from 48 to 192
- retain_count: int32 [16], replicated, may hold values from 48 to 192
Outputs:
- adapted: bfloat16 [6144, 8192], P('dp', 'tensor')
- grad_a: float32 [8192, 16], P('tensor')
- grad_b: float32 [16, 8192], replicated
The draws below stay inside these ranges and needn't reach their ends.
All inputs are finite; a program needn't handle non-finite values.
Results may differ from the reference program's by a relative error of at most 0.005.
Values may be sent and summed in bfloat16 or wider, within the bound.
No kernel may reach another device: no remote copies, remote signals or barrier semaphores. Data moves between devices by JAX's collectives and lax.ppermute only.
A program may use at most 192 MiB of HBM per device.

```python
import math
import jax
import jax.numpy as jnp
from jax import lax

MODEL_WIDTH = 8192
ADAPTER_RANK = 16
LEN = 384
CONTEXT_WIDTH = 8192
TOKENS = 6144
N_DP = 16


def draw_residual(key, part):
    key_scale, key_base = jax.random.split(jax.random.fold_in(key, 11))
    row_scale = jnp.exp(jax.random.uniform(key_scale, (TOKENS, 1), jnp.float32, 0.0, math.log(10.0)))
    base = jnp.clip(jax.random.normal(key_base, (TOKENS, MODEL_WIDTH), jnp.float32), -6.0, 6.0)
    return (row_scale * base).astype(jnp.bfloat16)


def place_ends(entries, stream_key, least, high):
    shape = entries.shape
    spot = [jax.random.randint(jax.random.fold_in(stream_key, axis), (), 0, shape[axis]) for axis in range(len(shape))]
    entries = entries.at[tuple(spot)].set(least)
    longest = shape.index(max(shape))
    spot[longest] = (spot[longest] + 1) % shape[longest]
    return entries.at[tuple(spot)].set(high)


def steps_of(rng, extent, cuts, low, largest):
    def one(axis_at, parts):
        steps = jax.random.uniform(jax.random.fold_in(jax.random.fold_in(rng, 6), axis_at), (parts,), jnp.float32, low / len(cuts), largest / len(cuts))
        return jnp.repeat(jnp.exp(steps), extent[axis_at] // parts).reshape((-1,) + (1,) * (len(extent) - axis_at - 1))

    loudness = one(*cuts[0])
    for cut in cuts[1:]:
        loudness = loudness * one(*cut)
    return loudness


def bell_draw(key, dims, spread, limit, cuts=(), held_as=jnp.bfloat16):
    drawn = jax.random.normal(key, dims, jnp.float32) * spread
    if len(cuts) > 0:
        drawn = steps_of(key, dims, cuts, -0.22, 0.18) * drawn
    return jnp.clip(drawn, min=-limit, max=limit).astype(held_as)


def setup_inputs(seed: int = 0) -> dict:
    streams_of = jax.random.split(jax.random.key(seed), 9)
    return {
        "context": bell_draw(streams_of[0], (TOKENS, CONTEXT_WIDTH), 1.0, 6.0, ((0, 16), (1, 2))),
        "output_weight": bell_draw(streams_of[1], (CONTEXT_WIDTH, MODEL_WIDTH), CONTEXT_WIDTH ** -0.5, 0.0625, ((0, 2), (1, 16))),
        "adapter_down_weight": bell_draw(streams_of[2], (CONTEXT_WIDTH, ADAPTER_RANK), CONTEXT_WIDTH ** -0.5, 0.0625, ((0, 2),)),
        "adapter_up_weight": bell_draw(streams_of[3], (ADAPTER_RANK, MODEL_WIDTH), 0.05, 0.29882812),
        "residual": draw_residual(jax.random.fold_in(streams_of[8], 71), 0),
        "frozen_residual_delta": bell_draw(streams_of[5], (TOKENS, MODEL_WIDTH), 1.0, 6.0, ((0, 16), (1, 2))),
        "harmful_count": place_ends(jax.random.randint(streams_of[6], (N_DP,), LEN // 8, LEN // 2 + 1), jax.random.fold_in(streams_of[6], 1), LEN // 8, (LEN // 2 + 1) - 1).astype(jnp.int32),
        "retain_count": place_ends(jax.random.randint(streams_of[7], (N_DP,), LEN // 8, LEN // 2 + 1), jax.random.fold_in(streams_of[7], 1), LEN // 8, (LEN // 2 + 1) - 1).astype(jnp.int32),
    }


ADAPTER_SCALE = 2.0
NORM_EPS = 1e-06
REROUTE_WEIGHT = 65536.0
RETAIN_WEIGHT = 1024.0

def row_gradient(hidden_states, target, sq_state, sq_target, cross_term, gap_sq, harmful, retained, harm_total, keep_total):
    norm_h = jnp.sqrt(sq_state + NORM_EPS)
    norm_g = jnp.sqrt(sq_target + NORM_EPS)
    cosine = cross_term / (norm_h * norm_g)
    distance = jnp.sqrt(gap_sq + NORM_EPS)
    weight_harm = REROUTE_WEIGHT / harm_total * harmful
    weight_keep = RETAIN_WEIGHT / keep_total * retained
    first = (weight_harm / (norm_h * norm_g))[:, None] * target
    second = (weight_harm * cosine / (norm_h * norm_h))[:, None] * hidden_states
    third = (weight_keep / distance)[:, None] * (hidden_states - target)
    return first - second + third

def reference(context, output_weight, adapter_down_weight, adapter_up_weight, residual, frozen_residual_delta, harmful_count, retain_count):
    harm_total = jnp.sum(harmful_count).astype(jnp.float32)
    keep_total = jnp.sum(retain_count).astype(jnp.float32)
    up_weight_single = adapter_up_weight.astype(jnp.float32)
    ctx_all = context.reshape(N_DP, LEN, CONTEXT_WIDTH)
    res_all = residual.reshape(N_DP, LEN, MODEL_WIDTH)
    fro_all = frozen_residual_delta.reshape(N_DP, LEN, MODEL_WIDTH)
    positions = jnp.arange(LEN, dtype=jnp.int32)

    def per_sequence(carry, items):
        acc_a, up_gradient_total = carry
        context_rows, residual_rows, fro_rows, harm_here, keep_here = items
        attention_output = jnp.dot(context_rows, output_weight, preferred_element_type=jnp.float32)
        reduced_state = jnp.dot(context_rows, adapter_down_weight, preferred_element_type=jnp.float32)
        hidden_states = residual_rows.astype(jnp.float32) + attention_output + ADAPTER_SCALE * jnp.dot(reduced_state, up_weight_single, precision=lax.Precision.HIGHEST)
        target = residual_rows.astype(jnp.float32) + fro_rows.astype(jnp.float32)
        harmful = (positions < harm_here).astype(jnp.float32)
        retained = ((positions >= harm_here) & (positions < harm_here + keep_here)).astype(jnp.float32)
        gap = hidden_states - target
        output_gradient = row_gradient(hidden_states, target, lax.optimization_barrier(jnp.sum(hidden_states * hidden_states, axis=1)), lax.optimization_barrier(jnp.sum(target * target, axis=1)), lax.optimization_barrier(jnp.sum(hidden_states * target, axis=1)), lax.optimization_barrier(jnp.sum(gap * gap, axis=1)), harmful, retained, harm_total, keep_total)
        reduced_gradient = ADAPTER_SCALE * jnp.dot(output_gradient, up_weight_single.T, precision=lax.Precision.HIGHEST)
        acc_a = acc_a + jnp.dot(context_rows.astype(jnp.float32).T, reduced_gradient, precision=lax.Precision.HIGHEST)
        up_gradient_total = up_gradient_total + ADAPTER_SCALE * jnp.dot(reduced_state.T, output_gradient, precision=lax.Precision.HIGHEST)
        return ((acc_a, up_gradient_total), hidden_states.astype(jnp.bfloat16))
    start = (jnp.zeros((CONTEXT_WIDTH, ADAPTER_RANK), jnp.float32), jnp.zeros((ADAPTER_RANK, MODEL_WIDTH), jnp.float32))
    (grad_a, grad_b), adapted = lax.scan(per_sequence, start, (ctx_all, res_all, fro_all, harmful_count, retain_count))
    return (adapted.reshape(TOKENS, MODEL_WIDTH), grad_a, grad_b)
```

```python
import jax
import jax.numpy as jnp
from jax import lax
from jax.sharding import PartitionSpec as P

ADAPTER_SCALE = 2.0
NORM_EPS = 1e-06
REROUTE_WEIGHT = 65536.0
RETAIN_WEIGHT = 1024.0
INNER = 4
LAYERS = 4
LATE_CUTS = (256, 128, 128)
HIGHEST = lax.Precision.HIGHEST


def after(value, *earlier):
    return lax.optimization_barrier((value,) + earlier)[0]


def routes(step):
    pairs = []
    for z in range(LAYERS):
        for q in range(INNER):
            for t in range(2):
                to = step(z, q, t)
                if to is not None:
                    pairs.append(((z * INNER + q) * 2 + t, (to[0] * INNER + to[1]) * 2 + to[2]))
    return pairs


def send(value, step):
    return lax.ppermute(value, ("dp", "tensor"), routes(step))


def keeps_early(z, t):
    return (t == 0) == (z < 2)


def inward(z, q, t):
    return {0: (1, q, t), 3: (2, q, t)}.get(z)


def outward(z, q, t):
    return {1: (0, q, t), 2: (3, q, t)}.get(z)


def mid_swap(z, q, t):
    return {1: (2, q, t), 2: (1, q, t)}.get(z)


def inner_swap(bits, layers=range(LAYERS)):
    return lambda z, q, t: (z, q ^ bits, t) if z in layers else None


def to_early(z, q, t):
    return None if keeps_early(z, t) else (z, q, 1 - t)


def to_late(z, q, t):
    return (z, q, 1 - t) if keeps_early(z, t) else None


def among(early, bits):
    return lambda z, q, t: (z, q ^ bits, t) if keeps_early(z, t) == early else None


def dot_bf16(a, b):
    return jnp.dot(a, b, preferred_element_type=jnp.float32).astype(jnp.bfloat16)


def gather_rows(rows, layers):
    core = send(rows, inner_swap(1, layers))
    across = send(rows, inner_swap(2, layers))
    diagonal = send(across, inner_swap(1, layers))
    return jnp.concatenate([rows, core, across, diagonal], axis=0)


def add_bf16(a, b):
    return (a.astype(jnp.float32) + b.astype(jnp.float32)).astype(jnp.bfloat16)


def to_owners(block, early, rows):
    pieces = [block[:rows]]
    for bits in range(1, INNER):
        pieces.append(send(block[bits * rows : (bits + 1) * rows], among(early, bits)))
    return pieces


def line_attention(context, output_weight):
    rows = context.shape[0]
    cols = output_weight.shape[1]
    data_rank = lax.axis_index("dp")
    tensor_rank = lax.axis_index("tensor")
    layer = data_rank // INNER
    place = data_rank % INNER
    low = layer < 2
    at_end = (layer == 0) | (layer == LAYERS - 1)
    early = (tensor_rank == 0) == low

    guest_rows = send(context, inward)
    middle = send(output_weight, mid_swap)
    outer_end = send(output_weight, outward)
    own_all = gather_rows(context, range(LAYERS))

    cuts, start = [], 0
    for width in LATE_CUTS:
        cuts.append((start * cols // 512, (start + width) * cols // 512))
        start += width
    outer_mid, previous = [], guest_rows
    for lo, hi in cuts:
        previous = send(after(output_weight[:, lo:hi], previous), inward)
        outer_mid.append(previous)
    far, previous = [], middle
    for chunk in outer_mid:
        previous = send(after(chunk, previous), mid_swap)
        far.append(previous)
    guest_all = gather_rows(guest_rows, (1, 2))

    part_own = dot_bf16(own_all, output_weight)
    sum_own = add_bf16(part_own, send(part_own, to_early))
    own_pieces = to_owners(sum_own, True, rows)

    def late(chunk):
        back = send(dot_bf16(guest_all, chunk), outward)
        part = jnp.where(at_end, back, dot_bf16(own_all, chunk))
        total = add_bf16(part, send(part, to_late))
        return to_owners(total, False, rows)

    middle_pieces = late(middle)

    outer = jnp.where(at_end, outer_end, jnp.concatenate(outer_mid, axis=1))
    part_outer = dot_bf16(own_all, outer)
    sum_outer = add_bf16(part_outer, send(part_outer, to_early))
    outer_pieces = to_owners(sum_outer, True, rows)

    far_parts = [late(chunk) for chunk in far]
    far_pieces = [jnp.concatenate(group, axis=1) for group in zip(*far_parts)]

    first = [jnp.where(early, a, b) for a, b in zip(own_pieces, middle_pieces)]
    second = [jnp.where(early, a, b) for a, b in zip(outer_pieces, far_pieces)]
    stacked = jnp.stack(first + second)
    first_half = jnp.where(early, layer % 2, jnp.where(low, 0, 1))
    ordered = []
    for half in range(2):
        group = jnp.where(first_half == half, 0, INNER)
        for q in range(INNER):
            ordered.append(
                lax.dynamic_index_in_dim(stacked, group + (place ^ q), 0, keepdims=False)
            )
    return jnp.concatenate(ordered, axis=1)


def general_attention(context, output_weight):
    partial = dot_bf16(context, lax.all_gather(output_weight, "dp", axis=1, tiled=True))
    return lax.psum_scatter(partial, "tensor", scatter_dimension=1, tiled=True)


def line_swap(value, step):
    return send(value, step)


def line_sum_grads(grad_a_t, grad_b):
    data_rank = lax.axis_index("dp")
    tensor_rank = lax.axis_index("tensor")
    place = data_rank % INNER
    rank = grad_a_t.shape[0]
    both = jnp.concatenate([grad_a_t, grad_b], axis=0)
    for bits in (1, 2):
        half = both.shape[1] // 2
        upper = (place & bits) != 0
        low_part, high_part = both[:, :half], both[:, half:]
        keep = jnp.where(upper, high_part, low_part)
        give = jnp.where(upper, low_part, high_part)
        both = keep + send(give, inner_swap(bits))
    for bits in (1, 2):
        both = both + send(both, lambda z, q, t: (z ^ bits, q, t))
    other_b = send(both[rank:], lambda z, q, t: (z, q, 1 - t))
    both = jnp.concatenate([both, other_b], axis=0)
    for bits in (2, 1):
        upper = (place & bits) != 0
        got = send(both, inner_swap(bits))
        both = jnp.concatenate(
            [jnp.where(upper, got, both), jnp.where(upper, both, got)], axis=1
        )
    grad_a = both[:rank].T
    mine, other = both[rank : 2 * rank], both[2 * rank :]
    first = tensor_rank == 0
    grad_b = jnp.concatenate(
        [jnp.where(first, mine, other), jnp.where(first, other, mine)], axis=1
    )
    return grad_a, grad_b


def general_sum_grads(grad_a_t, grad_b):
    grad_a_t, grad_b = lax.psum((grad_a_t, grad_b), "dp")
    return grad_a_t.T, lax.all_gather(grad_b, "tensor", axis=1, tiled=True)


def solution(mesh):
    line = mesh.shape["dp"] == LAYERS * INNER and mesh.shape["tensor"] == 2

    def sum_tensor(value):
        if line:
            return value + send(value, lambda z, q, t: (z, q, 1 - t))
        return lax.psum(value, "tensor")

    def local(
        context,
        output_weight,
        adapter_down_weight,
        adapter_up_weight,
        residual,
        frozen_residual_delta,
        harmful_count,
        retain_count,
    ):
        seq_len = context.shape[0]
        tensor_rank = lax.axis_index("tensor")
        data_rank = lax.axis_index("dp")
        harm_total = jnp.sum(harmful_count).astype(jnp.float32)
        keep_total = jnp.sum(retain_count).astype(jnp.float32)
        harm_here = harmful_count[data_rank]
        keep_here = retain_count[data_rank]
        col_count = residual.shape[1]

        low_rank_t = sum_tensor(
            lax.dot_general(
                adapter_down_weight,
                context,
                (((0,), (1,)), ((), ())),
                preferred_element_type=jnp.float32,
            )
        )
        up_columns = lax.dynamic_slice_in_dim(
            adapter_up_weight, tensor_rank * col_count, col_count, 1
        ).astype(jnp.float32)
        low_up = ADAPTER_SCALE * lax.dot_general(
            low_rank_t, up_columns, (((0,), (0,)), ((), ())), precision=HIGHEST
        )
        target = residual.astype(jnp.float32) + frozen_residual_delta.astype(jnp.float32)

        attn = (line_attention if line else general_attention)(context, output_weight)
        states = residual.astype(jnp.float32) + attn.astype(jnp.float32) + low_up
        gap = states - target

        def on_up(values):
            return lax.dot_general(
                up_columns, values, (((1,), (1,)), ((), ())), precision=HIGHEST
            )

        sums = jnp.stack(
            [
                jnp.sum(states * states, axis=1),
                jnp.sum(target * target, axis=1),
                jnp.sum(states * target, axis=1),
                jnp.sum(gap * gap, axis=1),
            ]
        )
        rank = up_columns.shape[0]
        shared = sum_tensor(jnp.concatenate([on_up(states), on_up(target), sums], axis=0))
        states_up, target_up = shared[:rank], shared[rank : 2 * rank]
        sq_state, sq_target, cross_term, gap_sq = (shared[2 * rank + i] for i in range(4))

        positions = jnp.arange(seq_len, dtype=jnp.int32)
        harmful = (positions < harm_here).astype(jnp.float32)
        retained = (
            (positions >= harm_here) & (positions < harm_here + keep_here)
        ).astype(jnp.float32)
        norm_h = jnp.sqrt(sq_state + NORM_EPS)
        norm_g = jnp.sqrt(sq_target + NORM_EPS)
        cosine = cross_term / (norm_h * norm_g)
        distance = jnp.sqrt(gap_sq + NORM_EPS)
        weight_harm = REROUTE_WEIGHT / harm_total * harmful
        weight_keep = RETAIN_WEIGHT / keep_total * retained / distance
        on_target = weight_harm / (norm_h * norm_g) - weight_keep
        on_states = weight_keep - weight_harm * cosine / (norm_h * norm_h)

        cotangent = on_target[:, None] * target + on_states[:, None] * states
        low_cot_t = ADAPTER_SCALE * (on_target * target_up + on_states * states_up)
        grad_a_t = jnp.dot(low_cot_t, context.astype(jnp.float32), precision=HIGHEST)
        grad_b = ADAPTER_SCALE * jnp.dot(low_rank_t, cotangent, precision=HIGHEST)
        grad_a, grad_b = (line_sum_grads if line else general_sum_grads)(grad_a_t, grad_b)
        return states.astype(jnp.bfloat16), grad_a, grad_b

    return jax.shard_map(
        local,
        mesh=mesh,
        in_specs=(
            P("dp", "tensor"),
            P("tensor", "dp"),
            P("tensor", None),
            P(),
            P("dp", "tensor"),
            P("dp", "tensor"),
            P(),
            P(),
        ),
        out_specs=(P("dp", "tensor"), P("tensor", None), P()),
        check_vma=False,
    )
```

```python
import jax
import jax.numpy as jnp
from jax import lax
from jax.experimental import pallas as pl
from jax.experimental.pallas import tpu as pltpu
from jax.sharding import PartitionSpec as P

ADAPTER_SCALE = 2.0
NORM_EPS = 1e-06
REROUTE_WEIGHT = 65536.0
RETAIN_WEIGHT = 1024.0
INNER = 4
LAYERS = 4
HIGHEST = lax.Precision.HIGHEST


def after(value, *earlier):
    return lax.optimization_barrier((value,) + earlier)[0]


def routes(step):
    pairs = []
    for z in range(LAYERS):
        for q in range(INNER):
            for t in range(2):
                to = step(z, q, t)
                if to is not None:
                    pairs.append(((z * INNER + q) * 2 + t, (to[0] * INNER + to[1]) * 2 + to[2]))
    return pairs


def send(value, step):
    return lax.ppermute(value, ("dp", "tensor"), routes(step))


def keeps_early(z, t):
    return (t == 0) == (z < 2)


def inward(z, q, t):
    return {0: (1, q, t), 3: (2, q, t)}.get(z)


def outward(z, q, t):
    return {1: (0, q, t), 2: (3, q, t)}.get(z)


def mid_swap(z, q, t):
    return {1: (2, q, t), 2: (1, q, t)}.get(z)


def inner_swap(bits, layers=range(LAYERS)):
    return lambda z, q, t: (z, q ^ bits, t) if z in layers else None


def to_early(z, q, t):
    return None if keeps_early(z, t) else (z, q, 1 - t)


def to_late(z, q, t):
    return (z, q, 1 - t) if keeps_early(z, t) else None


def among(early, bits):
    return lambda z, q, t: (z, q ^ bits, t) if keeps_early(z, t) == early else None


def dot_bf16(a, b):
    return jnp.dot(a, b, preferred_element_type=jnp.float32).astype(jnp.bfloat16)


def at_end_layer():
    layer = lax.axis_index("dp") // INNER
    return (layer == 0) | (layer == LAYERS - 1)


def products(*jobs, light=False):
    operands = []

    def index(array):
        for i, known in enumerate(operands):
            if known is array:
                return i
        operands.append(array)
        return len(operands) - 1

    plan = []
    for layer, pieces, weights, ends in jobs:
        choices = [weights] if ends is None else [weights, ends]
        plan.append(
            (
                index(layer),
                pieces,
                [[(index(w), start, n) for w, start, n in choice] for choice in choices],
            )
        )
    depth = jobs[0][0].shape[1]
    rows = jobs[0][0].shape[0] // INNER
    widths = [sum(n for _, _, n in choices[0]) for _, _, choices in plan]
    steps = [(j, p) for j, (_, pieces, _) in enumerate(plan) for p in range(len(pieces))]
    columns = max(len(choice) for _, _, choices in plan for choice in choices)

    def kernel(*refs):
        inputs = refs[: len(operands)]
        outs = refs[len(operands) : len(operands) + len(plan)]
        a_buf, w_buf, a_sem, w_sem = refs[len(operands) + len(plan) :]
        ends = at_end_layer()

        place = lax.axis_index("dp") % INNER

        def rows_copy(step):
            j, p = steps[step]
            start = pl.multiple_of((place ^ plan[j][1][p]) * rows, rows)
            source = inputs[plan[j][0]].at[pl.ds(start, rows)]
            return pltpu.make_async_copy(source, a_buf.at[step % 2], a_sem.at[step % 2])

        def weight_copies(j, choice):
            at = 0
            for i, (k, start, n) in enumerate(plan[j][2][choice]):
                source = inputs[k]
                if source.shape[1] != n:
                    source = source.at[:, pl.ds(start, n)]
                yield pltpu.make_async_copy(
                    source, w_buf.at[j % 2, :, pl.ds(at, n)], w_sem.at[j % 2, i]
                )
                at += n

        def weights(j, action):
            if len(plan[j][2]) == 1:
                for copy in weight_copies(j, 0):
                    action(copy)
                return

            @pl.when(ends)
            def _():
                for copy in weight_copies(j, 1):
                    action(copy)

            @pl.when(jnp.logical_not(ends))
            def _():
                for copy in weight_copies(j, 0):
                    action(copy)

        def begin(copy):
            copy.start()

        def finish(copy):
            copy.wait()

        weights(0, begin)
        rows_copy(0).start()
        for step, (j, p) in enumerate(steps):
            if step + 1 < len(steps):
                rows_copy(step + 1).start()
            if p == 0:
                weights(j, finish)
                if j + 1 < len(plan):
                    weights(j + 1, begin)
            rows_copy(step).wait()
            outs[j][p * rows : (p + 1) * rows, :] = jnp.dot(
                a_buf[step % 2],
                w_buf[j % 2, :, : widths[j]],
                preferred_element_type=jnp.float32,
            ).astype(jnp.bfloat16)

    in_vmem = pl.BlockSpec(memory_space=pltpu.VMEM)
    return pl.pallas_call(
        kernel,
        out_shape=[
            jax.ShapeDtypeStruct((len(pieces) * rows, n), jnp.bfloat16)
            for (_, pieces, _), n in zip(plan, widths)
        ],
        in_specs=[pl.BlockSpec(memory_space=pl.ANY)] * len(operands),
        out_specs=[in_vmem] * len(plan),
        scratch_shapes=[
            pltpu.VMEM((2, rows, depth), jnp.bfloat16),
            pltpu.VMEM((2, depth, max(widths)), jnp.bfloat16),
            pltpu.SemaphoreType.DMA((2,)),
            pltpu.SemaphoreType.DMA((2, columns)),
        ],
        compiler_params=pltpu.CompilerParams(vmem_limit_bytes=56 * 1024 * 1024),
        cost_estimate=pl.CostEstimate(
            flops=1000 if light else 11_000_000_000, bytes_accessed=1000, transcendentals=0
        ),
    )(*operands)


def add_bf16(a, b):
    return (a.astype(jnp.float32) + b.astype(jnp.float32)).astype(jnp.bfloat16)


def to_owners(block, early, rows):
    pieces = [block[:rows]]
    for bits in range(1, INNER):
        pieces.append(send(block[bits * rows : (bits + 1) * rows], among(early, bits)))
    return pieces


def layer_rows(rows):
    groups = [[z * INNER + q for q in range(INNER)] for z in range(LAYERS)]
    return lax.all_gather(rows, "dp", axis_index_groups=groups, axis=0, tiled=True)


def line_pieces(context, output_weight, due):
    rows = context.shape[0]
    half = output_weight.shape[1] // 2
    quarter = half // 2
    at_end = at_end_layer()

    block = 2 * half
    every = range(INNER)

    def pin(*values):
        return lax.optimization_barrier(values)

    def y_early(part):
        return send(part, to_early)

    def y_late(part):
        return send(part, to_late)

    quarters = [output_weight[:, i * quarter : (i + 1) * quarter] for i in range(4)]
    wide = output_weight[:, : half + quarter]
    own = layer_rows(context)
    guest = send(context, inward)
    middle = [send(wide, mid_swap)]
    outer_end = [send(wide, outward)]
    guest, middle[0], outer_end[0], quarters, _ = pin(
        guest, middle[0], outer_end[0], quarters, due
    )
    mid_quarters = [middle[0][:, i * quarter : (i + 1) * quarter] for i in range(2)]

    near = [send(quarters[0], inward)]
    middle.append(send(quarters[3], mid_swap))
    outer_end.append(send(quarters[3], outward))
    guests = layer_rows(guest)
    part_own = products(
        (own, (0, 1), [(output_weight, 0, block)], None),
        (own, (2, 3), [(output_weight, 0, block)], None),
        light=True,
    )
    near[0], middle, outer_end, part_own, rest, mid_quarters = pin(
        near[0], middle, outer_end, part_own, quarters[1:], mid_quarters
    )

    def first_half(arrays):
        return [(arrays[0], 0, half)]

    def second_half(arrays):
        return [(arrays[0], half, quarter), (arrays[1], 0, quarter)]

    def narrow(arrays):
        return [(array, 0, quarter) for array in arrays]

    far = [send(near[0], mid_swap)]
    near.append(send(rest[0], inward))
    mid_end = [send(mid_quarters[0], outward)]
    got_own = [y_early(part_own[0])]
    (part_mid_b,) = products((own, every, second_half(middle), None))
    far[0], near[1], mid_end[0], got_own[0], part_mid_b, part_own, rest, mid_quarters = pin(
        far[0], near[1], mid_end[0], got_own[0], part_mid_b, part_own, rest, mid_quarters
    )

    far.append(send(near[1], mid_swap))
    near.append(send(rest[1], inward))
    mid_end.append(send(mid_quarters[1], outward))
    got_own.append(y_early(part_own[1]))
    (part_outer_a,) = products((own, every, narrow(near[:2]), first_half(outer_end)))
    far[1], near[2], mid_end[1], got_own[1], part_outer_a, part_own, rest = pin(
        far[1], near[2], mid_end[1], got_own[1], part_outer_a, part_own, rest
    )

    far.append(send(near[2], mid_swap))
    near.append(send(rest[2], inward))
    got_outer_a = y_early(part_outer_a)
    part_mid_a, lent_mid_b = products(
        (own, every, first_half(middle), narrow(mid_end)),
        (guests, every, second_half(middle), None),
    )
    far[2], near[3], got_outer_a, part_mid_a, lent_mid_b, part_own = pin(
        far[2], near[3], got_outer_a, part_mid_a, lent_mid_b, part_own
    )

    far.append(send(near[3], mid_swap))
    lent_mid_b = send(lent_mid_b, outward)
    got_mid_a = y_late(part_mid_a)
    sum_own = jnp.concatenate([add_bf16(a, b) for a, b in zip(part_own, got_own)], axis=0)
    early_block = jnp.concatenate([sum_own, add_bf16(part_outer_a, got_outer_a)], axis=1)
    early = to_owners(early_block, True, rows)
    lent_far_a, part_far_a = products(
        (guests, every, narrow(far[:2]), None), (own, every, narrow(far[:2]), None)
    )
    far[3], lent_mid_b, got_mid_a, early, lent_far_a, part_far_a, part_mid_b = pin(
        far[3], lent_mid_b, got_mid_a, early, lent_far_a, part_far_a, part_mid_b
    )

    lent_far_a = send(lent_far_a, outward)
    part_mid_b = jnp.where(at_end, lent_mid_b, part_mid_b)
    got_mid_b = y_late(part_mid_b)
    sum_mid_a = add_bf16(part_mid_a, got_mid_a)
    lent_far_b, part_far_b = products(
        (guests, every, narrow(far[2:]), None), (own, every, narrow(far[2:]), None)
    )
    lent_far_a, part_mid_b, got_mid_b, lent_far_b, part_far_b, part_far_a, sum_mid_a = pin(
        lent_far_a, part_mid_b, got_mid_b, lent_far_b, part_far_b, part_far_a, sum_mid_a
    )

    lent_far_b = send(lent_far_b, outward)
    part_far_a = jnp.where(at_end, lent_far_a, part_far_a)
    got_far_a = y_late(part_far_a)
    late_block = jnp.concatenate([sum_mid_a, add_bf16(part_mid_b, got_mid_b)], axis=1)
    late = to_owners(late_block, False, rows)
    (part_outer_b,) = products((own, every, narrow(near[2:]), second_half(outer_end)))
    lent_far_b, part_far_a, got_far_a, late, part_outer_b, part_far_b = pin(
        lent_far_b, part_far_a, got_far_a, late, part_outer_b, part_far_b
    )

    part_far_b = jnp.where(at_end, lent_far_b, part_far_b)
    got_far_b = y_late(part_far_b)
    got_outer_b = y_early(part_outer_b)
    late += to_owners(add_bf16(part_far_a, got_far_a), False, rows)
    got_far_b, got_outer_b, late, part_far_b, part_outer_b = pin(
        got_far_b, got_outer_b, late, part_far_b, part_outer_b
    )

    early += to_owners(add_bf16(part_outer_b, got_outer_b), True, rows)
    late += to_owners(add_bf16(part_far_b, got_far_b), False, rows)
    return early, late


def split3(value):
    parts = []
    for _ in range(3):
        parts.append(value.astype(jnp.bfloat16))
        value = value - parts[-1].astype(jnp.float32)
    return parts


def line_states(context, output_weight, residual, delta, up_weight, low_rank, due):
    early, late = line_pieces(context, output_weight, (low_rank, *due))
    pieces = early + late
    rows, cols = residual.shape
    rank = up_weight.shape[0]
    block = output_weight.shape[1]
    half = block // 2
    step = block

    def kernel(*refs):
        piece_refs = refs[: len(pieces)]
        res_ref, delta_ref, up_ref, low_ref = refs[len(pieces) : len(pieces) + 4]
        adapted_ref, states_ref, sums_ref = refs[len(pieces) + 4 : len(pieces) + 7]
        attn, sem = refs[len(pieces) + 7 :]
        data_rank = lax.axis_index("dp")
        tensor_rank = lax.axis_index("tensor")
        layer = data_rank // INNER
        place = data_rank % INNER
        low = layer < 2
        is_early = (tensor_rank == 0) == low
        first = jnp.where(is_early, layer % 2, jnp.where(low, 0, 1))

        def copies(names, cuts):
            for j in range(INNER):
                column = (place ^ j) * block
                one = first * (INNER * block) + column
                two = (1 - first) * (INNER * block) + column
                for group, start, at, width in cuts:
                    target = one + at if at < block else two + at - block
                    source = names[group * INNER + j]
                    if source.shape[1] != width:
                        source = source.at[:, pl.ds(start, width)]
                    yield source, pl.multiple_of(target, half), width

        def load(names, cuts):
            started = []
            for i, (source, column, width) in enumerate(copies(names, cuts)):
                copy = pltpu.make_async_copy(source, attn.at[:, pl.ds(column, width)], sem.at[i])
                copy.start()
                started.append(copy)
            for copy in started:
                copy.wait()

        @pl.when(is_early)
        def _():
            load(
                piece_refs[: len(early)],
                [(0, 0, 0, block), (0, block, block, half), (1, 0, block + half, half)],
            )

        @pl.when(jnp.logical_not(is_early))
        def _():
            load(
                piece_refs[len(early) :],
                [(0, 0, 0, block), (1, 0, block, half), (2, 0, block + half, half)],
            )

        low_parts = jnp.concatenate(split3(low_ref[...]), axis=1)
        sums_ref[...] = jnp.zeros_like(sums_ref)

        @pl.loop(0, cols // step)
        def _(i):
            here = pl.ds(pl.multiple_of(i * step, step), step)
            up = up_ref[:, here]
            res = res_ref[:, here].astype(jnp.float32)
            low_up = jnp.dot(
                low_parts,
                jnp.concatenate([up] * 3, axis=0),
                preferred_element_type=jnp.float32,
            )
            states = res + attn[:, here].astype(jnp.float32) + ADAPTER_SCALE * low_up
            target = res + delta_ref[:, here].astype(jnp.float32)
            gap = states - target
            adapted_ref[:, here] = states.astype(jnp.bfloat16)
            states_ref[:, here] = states
            on_up = 0
            for part in split3(states):
                on_up += lax.dot_general(
                    part, up, (((1,), (1,)), ((), ())), preferred_element_type=jnp.float32
                )
            sums_ref[:, :rank] += on_up
            for k, product in enumerate((states * states, states * target, gap * gap)):
                sums_ref[:, rank + k : rank + k + 1] += jnp.sum(product, axis=1, keepdims=True)

    anywhere = pl.BlockSpec(memory_space=pl.ANY)
    in_vmem = pl.BlockSpec(memory_space=pltpu.VMEM)
    return pl.pallas_call(
        kernel,
        out_shape=(
            jax.ShapeDtypeStruct((rows, cols), jnp.bfloat16),
            jax.ShapeDtypeStruct((rows, cols), jnp.float32),
            jax.ShapeDtypeStruct((rows, 128), jnp.float32),
        ),
        in_specs=[anywhere] * len(pieces) + [in_vmem] * 4,
        out_specs=(in_vmem,) * 3,
        scratch_shapes=[
            pltpu.VMEM((rows, cols), jnp.bfloat16),
            pltpu.SemaphoreType.DMA((3 * INNER,)),
        ],
        compiler_params=pltpu.CompilerParams(vmem_limit_bytes=48 * 1024 * 1024),
        cost_estimate=pl.CostEstimate(
            flops=rows * cols * 8, bytes_accessed=rows * cols * 4, transcendentals=0
        ),
    )(*pieces, residual, delta, up_weight, low_rank)


def general_attention(context, output_weight):
    partial = dot_bf16(context, lax.all_gather(output_weight, "dp", axis=1, tiled=True))
    return lax.psum_scatter(partial, "tensor", scatter_dimension=1, tiled=True)


def line_sum_grads(grad_a_t, grad_b):
    data_rank = lax.axis_index("dp")
    tensor_rank = lax.axis_index("tensor")
    place = data_rank % INNER
    rank = grad_a_t.shape[0]
    both = jnp.concatenate([grad_a_t, grad_b], axis=0)
    for bits in (1, 2):
        half = both.shape[1] // 2
        upper = (place & bits) != 0
        low_part, high_part = both[:, :half], both[:, half:]
        keep = jnp.where(upper, high_part, low_part)
        give = jnp.where(upper, low_part, high_part)
        both = keep + send(give, inner_swap(bits))
    for bits in (1, 2):
        both = both + send(both, lambda z, q, t: (z ^ bits, q, t))
    other_b = send(both[rank:], lambda z, q, t: (z, q, 1 - t))
    both = jnp.concatenate([both, other_b], axis=0)
    for bits in (2, 1):
        upper = (place & bits) != 0
        got = send(both, inner_swap(bits))
        both = jnp.concatenate(
            [jnp.where(upper, got, both), jnp.where(upper, both, got)], axis=1
        )
    grad_a = both[:rank].T
    mine, other = both[rank : 2 * rank], both[2 * rank :]
    first = tensor_rank == 0
    grad_b = jnp.concatenate(
        [jnp.where(first, mine, other), jnp.where(first, other, mine)], axis=1
    )
    return grad_a, grad_b


def general_sum_grads(grad_a_t, grad_b):
    grad_a_t, grad_b = lax.psum((grad_a_t, grad_b), "dp")
    return grad_a_t.T, lax.all_gather(grad_b, "tensor", axis=1, tiled=True)


def solution(mesh):
    line = mesh.shape["dp"] == LAYERS * INNER and mesh.shape["tensor"] == 2

    def sum_tensor(value):
        if line:
            return value + send(value, lambda z, q, t: (z, q, 1 - t))
        return lax.psum(value, "tensor")

    def local(
        context,
        output_weight,
        adapter_down_weight,
        adapter_up_weight,
        residual,
        frozen_residual_delta,
        harmful_count,
        retain_count,
    ):
        seq_len = context.shape[0]
        tensor_rank = lax.axis_index("tensor")
        data_rank = lax.axis_index("dp")
        harm_total = jnp.sum(harmful_count).astype(jnp.float32)
        keep_total = jnp.sum(retain_count).astype(jnp.float32)
        harm_here = harmful_count[data_rank]
        keep_here = retain_count[data_rank]
        col_count = residual.shape[1]

        low_rank_t = sum_tensor(
            lax.dot_general(
                adapter_down_weight,
                context,
                (((0,), (1,)), ((), ())),
                preferred_element_type=jnp.float32,
            )
        )
        up_narrow = lax.dynamic_slice_in_dim(
            adapter_up_weight, tensor_rank * col_count, col_count, 1
        )
        up_columns = up_narrow.astype(jnp.float32)
        target = residual.astype(jnp.float32) + frozen_residual_delta.astype(jnp.float32)

        def on_up(values):
            return lax.dot_general(
                up_columns, values, (((1,), (1,)), ((), ())), precision=HIGHEST
            )

        rank = up_columns.shape[0]
        early_sums = sum_tensor(
            jnp.concatenate([on_up(target), jnp.sum(target * target, axis=1)[None]], axis=0)
        )
        target_up, sq_target = early_sums[:rank], early_sums[rank]
        if line:
            adapted, states, sums = line_states(
                context,
                output_weight,
                residual,
                frozen_residual_delta,
                up_narrow,
                low_rank_t.T,
                (early_sums,),
            )
            sums = sums[:, : rank + 3].T
        else:
            low_up = ADAPTER_SCALE * lax.dot_general(
                low_rank_t, up_columns, (((0,), (0,)), ((), ())), precision=HIGHEST
            )
            attn = general_attention(context, output_weight).astype(jnp.float32)
            states = residual.astype(jnp.float32) + attn + low_up
            adapted = states.astype(jnp.bfloat16)
            gap = states - target
            products = [states * states, states * target, gap * gap]
            sums = jnp.stack([jnp.sum(product, axis=1) for product in products])
            sums = jnp.concatenate([on_up(states), sums], axis=0)
        shared = sum_tensor(sums)
        states_up = shared[:rank]
        sq_state, cross_term, gap_sq = (shared[rank + i] for i in range(3))

        positions = jnp.arange(seq_len, dtype=jnp.int32)
        harmful = (positions < harm_here).astype(jnp.float32)
        retained = (
            (positions >= harm_here) & (positions < harm_here + keep_here)
        ).astype(jnp.float32)
        norm_h = jnp.sqrt(sq_state + NORM_EPS)
        norm_g = jnp.sqrt(sq_target + NORM_EPS)
        cosine = cross_term / (norm_h * norm_g)
        distance = jnp.sqrt(gap_sq + NORM_EPS)
        weight_harm = REROUTE_WEIGHT / harm_total * harmful
        weight_keep = RETAIN_WEIGHT / keep_total * retained / distance
        on_target = weight_harm / (norm_h * norm_g) - weight_keep
        on_states = weight_keep - weight_harm * cosine / (norm_h * norm_h)

        cotangent = on_target[:, None] * target + on_states[:, None] * states
        low_cot_t = ADAPTER_SCALE * (on_target * target_up + on_states * states_up)
        grad_a_t = jnp.dot(low_cot_t, context.astype(jnp.float32), precision=HIGHEST)
        grad_b = ADAPTER_SCALE * jnp.dot(low_rank_t, cotangent, precision=HIGHEST)
        grad_a, grad_b = (line_sum_grads if line else general_sum_grads)(grad_a_t, grad_b)
        return adapted, grad_a, grad_b

    return jax.shard_map(
        local,
        mesh=mesh,
        in_specs=(
            P("dp", "tensor"),
            P("tensor", "dp"),
            P("tensor", None),
            P(),
            P("dp", "tensor"),
            P("dp", "tensor"),
            P(),
            P(),
        ),
        out_specs=(P("dp", "tensor"), P("tensor", None), P()),
        check_vma=False,
    )
```

```python
import jax
import jax.numpy as jnp
from jax import lax
from jax.experimental import pallas as pl
from jax.experimental.pallas import tpu as pltpu
from jax.sharding import PartitionSpec as P

ADAPTER_SCALE = 2.0
NORM_EPS = 1e-06
REROUTE_WEIGHT = 65536.0
RETAIN_WEIGHT = 1024.0
INNER = 4
LAYERS = 4
HIGHEST = lax.Precision.HIGHEST


def after(value, *earlier):
    return lax.optimization_barrier((value,) + earlier)[0]


def routes(step):
    pairs = []
    for z in range(LAYERS):
        for q in range(INNER):
            for t in range(2):
                to = step(z, q, t)
                if to is not None:
                    pairs.append(((z * INNER + q) * 2 + t, (to[0] * INNER + to[1]) * 2 + to[2]))
    return pairs


def send(value, step):
    return lax.ppermute(value, ("dp", "tensor"), routes(step))


def inward(z, q, t):
    return {0: (1, q, t), 3: (2, q, t)}.get(z)


def outward(z, q, t):
    return {1: (0, q, t), 2: (3, q, t)}.get(z)


def mid_swap(z, q, t):
    return {1: (2, q, t), 2: (1, q, t)}.get(z)


def inner_swap(bits, layers=range(LAYERS)):
    return lambda z, q, t: (z, q ^ bits, t) if z in layers else None


def other_tensor(z, q, t):
    return (z, q, 1 - t)


def dot_bf16(a, b):
    return jnp.dot(a, b, preferred_element_type=jnp.float32).astype(jnp.bfloat16)


def at_end_layer():
    layer = lax.axis_index("dp") // INNER
    return (layer == 0) | (layer == LAYERS - 1)


def products(half, *jobs):
    operands = []

    def index(array):
        for i, known in enumerate(operands):
            if known is array:
                return i
        operands.append(array)
        return len(operands) - 1

    plan = []
    for layer, weights, ends in jobs:
        choices = [weights] if ends is None else [weights, ends]
        plan.append(
            (
                index(layer),
                range(INNER),
                [[(index(w), start, n) for w, start, n in choice] for choice in choices],
            )
        )
    depth = jobs[0][0].shape[1]
    rows = jobs[0][0].shape[0] // INNER
    widths = [sum(n for _, _, n in choices[0]) for _, _, choices in plan]
    splits = [width // half for width in widths]
    out_count = sum(splits)
    steps = [(j, p) for j, (_, pieces, _) in enumerate(plan) for p in range(len(pieces))]
    columns = max(len(choice) for _, _, choices in plan for choice in choices)

    def kernel(*refs):
        inputs = refs[: len(operands)]
        outs = refs[len(operands) : len(operands) + out_count]
        a_buf, w_buf, a_sem, w_sem = refs[len(operands) + out_count :]
        ends = at_end_layer()

        place = lax.axis_index("dp") % INNER

        def rows_copy(step):
            j, p = steps[step]
            start = pl.multiple_of((place ^ plan[j][1][p]) * rows, rows)
            source = inputs[plan[j][0]].at[pl.ds(start, rows)]
            return pltpu.make_async_copy(source, a_buf.at[step % 2], a_sem.at[step % 2])

        def weight_copies(j, choice):
            at = 0
            for i, (k, start, n) in enumerate(plan[j][2][choice]):
                source = inputs[k]
                if source.shape[1] != n:
                    source = source.at[:, pl.ds(start, n)]
                yield pltpu.make_async_copy(
                    source, w_buf.at[j % 2, :, pl.ds(at, n)], w_sem.at[j % 2, i]
                )
                at += n

        def weights(j, action):
            if len(plan[j][2]) == 1:
                for copy in weight_copies(j, 0):
                    action(copy)
                return

            @pl.when(ends)
            def _():
                for copy in weight_copies(j, 1):
                    action(copy)

            @pl.when(jnp.logical_not(ends))
            def _():
                for copy in weight_copies(j, 0):
                    action(copy)

        def begin(copy):
            copy.start()

        def finish(copy):
            copy.wait()

        weights(0, begin)
        rows_copy(0).start()
        for step, (j, p) in enumerate(steps):
            if step + 1 < len(steps):
                rows_copy(step + 1).start()
            if p == 0:
                weights(j, finish)
                if j + 1 < len(plan):
                    weights(j + 1, begin)
            rows_copy(step).wait()
            result = jnp.dot(
                a_buf[step % 2],
                w_buf[j % 2, :, : widths[j]],
                preferred_element_type=jnp.float32,
            ).astype(jnp.bfloat16)
            for k in range(splits[j]):
                out = outs[sum(splits[:j]) + k]
                out[p * rows : (p + 1) * rows, :] = result[:, k * half : (k + 1) * half]

    in_vmem = pl.BlockSpec(memory_space=pltpu.VMEM)
    return pl.pallas_call(
        kernel,
        out_shape=[
            jax.ShapeDtypeStruct((INNER * rows, half), jnp.bfloat16) for _ in range(out_count)
        ],
        in_specs=[pl.BlockSpec(memory_space=pl.ANY)] * len(operands),
        out_specs=[in_vmem] * out_count,
        scratch_shapes=[
            pltpu.VMEM((2, rows, depth), jnp.bfloat16),
            pltpu.VMEM((2, depth, max(widths)), jnp.bfloat16),
            pltpu.SemaphoreType.DMA((2,)),
            pltpu.SemaphoreType.DMA((2, columns)),
        ],
        compiler_params=pltpu.CompilerParams(vmem_limit_bytes=56 * 1024 * 1024),
        cost_estimate=pl.CostEstimate(
            flops=11_000_000_000, bytes_accessed=1000, transcendentals=0
        ),
    )(*operands)


def add_bf16(a, b):
    return (a.astype(jnp.float32) + b.astype(jnp.float32)).astype(jnp.bfloat16)


def to_owners(block, rows):
    pieces = [block[:rows]]
    for bits in range(1, INNER):
        pieces.append(send(block[bits * rows : (bits + 1) * rows], inner_swap(bits)))
    return pieces


def layer_rows(rows):
    groups = [[z * INNER + q for q in range(INNER)] for z in range(LAYERS)]
    return lax.all_gather(rows, "dp", axis_index_groups=groups, axis=0, tiled=True)


def line_pieces(context, output_weight, due):
    rows = context.shape[0]
    half = output_weight.shape[1] // 2
    quarter = half // 2
    block = 2 * half
    layer = lax.axis_index("dp") // INNER
    at_end = at_end_layer()
    keeps_near = (lax.axis_index("tensor") == 0) == (layer < 2)

    def pin(*values):
        return lax.optimization_barrier(values)

    def swap(near_part, far_part):
        kept = jnp.where(keeps_near, near_part, far_part)
        return kept, send(jnp.where(keeps_near, far_part, near_part), other_tensor)

    def narrow(arrays):
        return [(array, 0, quarter) for array in arrays]

    quarters = [output_weight[:, i * quarter : (i + 1) * quarter] for i in range(4)]
    guest = send(context, inward)
    middle = send(output_weight, mid_swap)
    outer_end = send(output_weight, outward)
    own = layer_rows(context)
    near = [send(after(quarters[0], guest, due), inward)]
    guest, near[0], middle, outer_end, quarters = pin(
        guest, near[0], middle, outer_end, quarters
    )
    guests = layer_rows(guest)
    mid_quarters = [middle[:, i * quarter : (i + 1) * quarter] for i in range(2)]
    mid_a, mid_b = [(middle, 0, half)], [(middle, half, half)]

    far = [send(near[0], mid_swap)]
    near.append(send(quarters[1], inward))
    mid_end = [send(mid_quarters[0], outward)]
    part_own = products(half, (own, [(output_weight, 0, block)], None))
    far[0], near[1], mid_end[0], part_own, quarters, mid_quarters = pin(
        far[0], near[1], mid_end[0], part_own, quarters, mid_quarters
    )

    far.append(send(near[1], mid_swap))
    near.append(send(quarters[2], inward))
    mid_end.append(send(mid_quarters[1], outward))
    part_mid_b, part_outer_a = products(
        half, (own, mid_b + narrow(near[:2]), mid_b + [(outer_end, 0, half)])
    )
    far[1], near[2], mid_end[1], part_mid_b, part_outer_a, quarters = pin(
        far[1], near[2], mid_end[1], part_mid_b, part_outer_a, quarters
    )

    far.append(send(near[2], mid_swap))
    near.append(send(quarters[3], inward))
    (part_mid_a,) = products(half, (own, mid_a, narrow(mid_end)))
    (lent_mid_b,) = products(half, (guests, mid_b, None))
    far[2], near[3], part_mid_a, lent_mid_b = pin(far[2], near[3], part_mid_a, lent_mid_b)

    far.append(send(near[3], mid_swap))
    lent_mid_b = send(lent_mid_b, outward)
    kept_a, came_a = swap(part_own[0], part_mid_a)
    lent_far_a, part_far_a = products(
        half, (guests, narrow(far[:2]), None), (own, narrow(far[:2]), None)
    )
    far[3], lent_mid_b, kept_a, came_a, lent_far_a, part_far_a = pin(
        far[3], lent_mid_b, kept_a, came_a, lent_far_a, part_far_a
    )

    lent_far_a = send(lent_far_a, outward)
    kept_b, came_b = swap(part_own[1], jnp.where(at_end, lent_mid_b, part_mid_b))
    lent_far_b, part_far_b = products(
        half, (guests, narrow(far[2:]), None), (own, narrow(far[2:]), None)
    )
    lent_far_a, kept_a, kept_b, came_b, lent_far_b, part_far_b = pin(
        lent_far_a, add_bf16(kept_a, came_a), kept_b, came_b, lent_far_b, part_far_b
    )

    lent_far_b = send(lent_far_b, outward)
    kept_c, came_c = swap(part_outer_a, jnp.where(at_end, lent_far_a, part_far_a))
    first = to_owners(jnp.concatenate([kept_a, add_bf16(kept_b, came_b)], axis=1), rows)
    (part_outer_b,) = products(half, (own, narrow(near[2:]), [(outer_end, half, half)]))
    lent_far_b, kept_c, came_c, first, part_outer_b = pin(
        lent_far_b, kept_c, came_c, first, part_outer_b
    )

    kept_d, came_d = swap(part_outer_b, jnp.where(at_end, lent_far_b, part_far_b))
    second = to_owners(add_bf16(kept_c, came_c), rows)
    kept_d, came_d, second = pin(kept_d, came_d, second)
    return first, second, to_owners(add_bf16(kept_d, came_d), rows)


def split3(value):
    parts = []
    for _ in range(3):
        parts.append(value.astype(jnp.bfloat16))
        value = value - parts[-1].astype(jnp.float32)
    return parts


def line_states(context, output_weight, residual, delta, up_weight, low_rank, due):
    lists = line_pieces(context, output_weight, (low_rank, *due))
    pieces = [piece for group in lists for piece in group]
    rows, cols = residual.shape
    rank = up_weight.shape[0]
    block = output_weight.shape[1]
    half = block // 2
    step = block

    def kernel(*refs):
        piece_refs = refs[: len(pieces)]
        res_ref, delta_ref, up_ref, low_ref = refs[len(pieces) : len(pieces) + 4]
        adapted_ref, states_ref, sums_ref = refs[len(pieces) + 4 : len(pieces) + 7]
        attn, sem = refs[len(pieces) + 7 :]
        data_rank = lax.axis_index("dp")
        tensor_rank = lax.axis_index("tensor")
        layer = data_rank // INNER
        place = data_rank % INNER
        low = layer < 2
        is_early = (tensor_rank == 0) == low
        first = jnp.where(is_early, layer % 2, jnp.where(low, 0, 1))

        started = []
        for j in range(INNER):
            column = (place ^ j) * block
            one = first * (INNER * block) + column
            two = (1 - first) * (INNER * block) + column
            for k, (target, width) in enumerate(((one, block), (two, half), (two + half, half))):
                to = attn.at[:, pl.ds(pl.multiple_of(target, half), width)]
                copy = pltpu.make_async_copy(piece_refs[k * INNER + j], to, sem.at[len(started)])
                copy.start()
                started.append(copy)
        for copy in started:
            copy.wait()

        low_parts = jnp.concatenate(split3(low_ref[...]), axis=1)
        sums_ref[...] = jnp.zeros_like(sums_ref)

        @pl.loop(0, cols // step)
        def _(i):
            here = pl.ds(pl.multiple_of(i * step, step), step)
            up = up_ref[:, here]
            res = res_ref[:, here].astype(jnp.float32)
            low_up = jnp.dot(
                low_parts,
                jnp.concatenate([up] * 3, axis=0),
                preferred_element_type=jnp.float32,
            )
            states = res + attn[:, here].astype(jnp.float32) + ADAPTER_SCALE * low_up
            target = res + delta_ref[:, here].astype(jnp.float32)
            gap = states - target
            adapted_ref[:, here] = states.astype(jnp.bfloat16)
            states_ref[:, here] = states
            on_up = 0
            for part in split3(states):
                on_up += lax.dot_general(
                    part, up, (((1,), (1,)), ((), ())), preferred_element_type=jnp.float32
                )
            sums_ref[:, :rank] += on_up
            for k, product in enumerate((states * states, states * target, gap * gap)):
                sums_ref[:, rank + k : rank + k + 1] += jnp.sum(product, axis=1, keepdims=True)

    anywhere = pl.BlockSpec(memory_space=pl.ANY)
    in_vmem = pl.BlockSpec(memory_space=pltpu.VMEM)
    return pl.pallas_call(
        kernel,
        out_shape=(
            jax.ShapeDtypeStruct((rows, cols), jnp.bfloat16),
            jax.ShapeDtypeStruct((rows, cols), jnp.float32),
            jax.ShapeDtypeStruct((rows, 128), jnp.float32),
        ),
        in_specs=[anywhere] * len(pieces) + [in_vmem] * 4,
        out_specs=(in_vmem,) * 3,
        scratch_shapes=[
            pltpu.VMEM((rows, cols), jnp.bfloat16),
            pltpu.SemaphoreType.DMA((3 * INNER,)),
        ],
        compiler_params=pltpu.CompilerParams(vmem_limit_bytes=48 * 1024 * 1024),
        cost_estimate=pl.CostEstimate(
            flops=rows * cols * 8, bytes_accessed=rows * cols * 4, transcendentals=0
        ),
    )(*pieces, residual, delta, up_weight, low_rank)


def general_attention(context, output_weight):
    partial = dot_bf16(context, lax.all_gather(output_weight, "dp", axis=1, tiled=True))
    return lax.psum_scatter(partial, "tensor", scatter_dimension=1, tiled=True)


def line_sum_grads(grad_a_t, grad_b):
    data_rank = lax.axis_index("dp")
    tensor_rank = lax.axis_index("tensor")
    place = data_rank % INNER
    rank = grad_a_t.shape[0]
    both = jnp.concatenate([grad_a_t, grad_b], axis=0)
    for bits in (1, 2):
        half = both.shape[1] // 2
        upper = (place & bits) != 0
        low_part, high_part = both[:, :half], both[:, half:]
        keep = jnp.where(upper, high_part, low_part)
        give = jnp.where(upper, low_part, high_part)
        both = keep + send(give, inner_swap(bits))
    for bits in (1, 2):
        both = both + send(both, lambda z, q, t: (z ^ bits, q, t))
    other_b = send(both[rank:], other_tensor)
    both = jnp.concatenate([both, other_b], axis=0)
    for bits in (2, 1):
        upper = (place & bits) != 0
        got = send(both, inner_swap(bits))
        both = jnp.concatenate(
            [jnp.where(upper, got, both), jnp.where(upper, both, got)], axis=1
        )
    grad_a = both[:rank].T
    mine, other = both[rank : 2 * rank], both[2 * rank :]
    first = tensor_rank == 0
    grad_b = jnp.concatenate(
        [jnp.where(first, mine, other), jnp.where(first, other, mine)], axis=1
    )
    return grad_a, grad_b


def general_sum_grads(grad_a_t, grad_b):
    grad_a_t, grad_b = lax.psum((grad_a_t, grad_b), "dp")
    return grad_a_t.T, lax.all_gather(grad_b, "tensor", axis=1, tiled=True)


def solution(mesh):
    line = mesh.shape["dp"] == LAYERS * INNER and mesh.shape["tensor"] == 2

    def sum_tensor(value):
        if line:
            return value + send(value, other_tensor)
        return lax.psum(value, "tensor")

    def local(
        context,
        output_weight,
        adapter_down_weight,
        adapter_up_weight,
        residual,
        frozen_residual_delta,
        harmful_count,
        retain_count,
    ):
        seq_len = context.shape[0]
        tensor_rank = lax.axis_index("tensor")
        data_rank = lax.axis_index("dp")
        harm_total = jnp.sum(harmful_count).astype(jnp.float32)
        keep_total = jnp.sum(retain_count).astype(jnp.float32)
        harm_here = harmful_count[data_rank]
        keep_here = retain_count[data_rank]
        col_count = residual.shape[1]

        low_rank_t = sum_tensor(
            lax.dot_general(
                adapter_down_weight,
                context,
                (((0,), (1,)), ((), ())),
                preferred_element_type=jnp.float32,
            )
        )
        up_narrow = lax.dynamic_slice_in_dim(
            adapter_up_weight, tensor_rank * col_count, col_count, 1
        )
        up_columns = up_narrow.astype(jnp.float32)
        target = residual.astype(jnp.float32) + frozen_residual_delta.astype(jnp.float32)

        def on_up(values):
            return lax.dot_general(
                up_columns, values, (((1,), (1,)), ((), ())), precision=HIGHEST
            )

        rank = up_columns.shape[0]
        early_sums = sum_tensor(
            jnp.concatenate([on_up(target), jnp.sum(target * target, axis=1)[None]], axis=0)
        )
        target_up, sq_target = early_sums[:rank], early_sums[rank]
        if line:
            adapted, states, sums = line_states(
                context,
                output_weight,
                residual,
                frozen_residual_delta,
                up_narrow,
                low_rank_t.T,
                (early_sums,),
            )
            sums = sums[:, : rank + 3].T
        else:
            low_up = ADAPTER_SCALE * lax.dot_general(
                low_rank_t, up_columns, (((0,), (0,)), ((), ())), precision=HIGHEST
            )
            attn = general_attention(context, output_weight).astype(jnp.float32)
            states = residual.astype(jnp.float32) + attn + low_up
            adapted = states.astype(jnp.bfloat16)
            gap = states - target
            products = [states * states, states * target, gap * gap]
            sums = jnp.stack([jnp.sum(product, axis=1) for product in products])
            sums = jnp.concatenate([on_up(states), sums], axis=0)
        shared = sum_tensor(sums)
        states_up = shared[:rank]
        sq_state, cross_term, gap_sq = (shared[rank + i] for i in range(3))

        positions = jnp.arange(seq_len, dtype=jnp.int32)
        harmful = (positions < harm_here).astype(jnp.float32)
        retained = (
            (positions >= harm_here) & (positions < harm_here + keep_here)
        ).astype(jnp.float32)
        norm_h = jnp.sqrt(sq_state + NORM_EPS)
        norm_g = jnp.sqrt(sq_target + NORM_EPS)
        cosine = cross_term / (norm_h * norm_g)
        distance = jnp.sqrt(gap_sq + NORM_EPS)
        weight_harm = REROUTE_WEIGHT / harm_total * harmful
        weight_keep = RETAIN_WEIGHT / keep_total * retained / distance
        on_target = weight_harm / (norm_h * norm_g) - weight_keep
        on_states = weight_keep - weight_harm * cosine / (norm_h * norm_h)

        cotangent = on_target[:, None] * target + on_states[:, None] * states
        low_cot_t = ADAPTER_SCALE * (on_target * target_up + on_states * states_up)
        grad_a_t = jnp.dot(low_cot_t, context.astype(jnp.float32), precision=HIGHEST)
        grad_b = ADAPTER_SCALE * jnp.dot(low_rank_t, cotangent, precision=HIGHEST)
        grad_a, grad_b = (line_sum_grads if line else general_sum_grads)(grad_a_t, grad_b)
        return adapted, grad_a, grad_b

    return jax.shard_map(
        local,
        mesh=mesh,
        in_specs=(
            P("dp", "tensor"),
            P("tensor", "dp"),
            P("tensor", None),
            P(),
            P("dp", "tensor"),
            P("dp", "tensor"),
            P(),
            P(),
        ),
        out_specs=(P("dp", "tensor"), P("tensor", None), P()),
        check_vma=False,
    )
```

```python
import jax
import jax.numpy as jnp
from jax import lax
from jax.experimental import pallas as pl
from jax.experimental.pallas import tpu as pltpu
from jax.sharding import PartitionSpec as P

ADAPTER_SCALE = 2.0
NORM_EPS = 1e-06
REROUTE_WEIGHT = 65536.0
RETAIN_WEIGHT = 1024.0
INNER = 4
LAYERS = 4
HIGHEST = lax.Precision.HIGHEST


def after(value, *earlier):
    return lax.optimization_barrier((value,) + earlier)[0]


def routes(step):
    pairs = []
    for z in range(LAYERS):
        for q in range(INNER):
            for t in range(2):
                to = step(z, q, t)
                if to is not None:
                    pairs.append(((z * INNER + q) * 2 + t, (to[0] * INNER + to[1]) * 2 + to[2]))
    return pairs


def send(value, step):
    return lax.ppermute(value, ("dp", "tensor"), routes(step))


def inward(z, q, t):
    return {0: (1, q, t), 3: (2, q, t)}.get(z)


def outward(z, q, t):
    return {1: (0, q, t), 2: (3, q, t)}.get(z)


def mid_swap(z, q, t):
    return {1: (2, q, t), 2: (1, q, t)}.get(z)


def inner_swap(bits, layers=range(LAYERS)):
    return lambda z, q, t: (z, q ^ bits, t) if z in layers else None


def other_tensor(z, q, t):
    return (z, q, 1 - t)


def dot_bf16(a, b):
    return jnp.dot(a, b, preferred_element_type=jnp.float32).astype(jnp.bfloat16)


def at_end_layer():
    layer = lax.axis_index("dp") // INNER
    return (layer == 0) | (layer == LAYERS - 1)


def products(half, *jobs):
    operands = []

    def index(array):
        for i, known in enumerate(operands):
            if known is array:
                return i
        operands.append(array)
        return len(operands) - 1

    plan = []
    for layer, weights, ends in jobs:
        choices = [weights] if ends is None else [weights, ends]
        plan.append(
            (
                index(layer),
                range(INNER),
                [[(index(w), start, n) for w, start, n in choice] for choice in choices],
            )
        )
    depth = jobs[0][0].shape[1]
    rows = jobs[0][0].shape[0] // INNER
    widths = [sum(n for _, _, n in choices[0]) for _, _, choices in plan]
    splits = [width // half for width in widths]
    out_count = sum(splits)
    steps = [(j, p) for j, (_, pieces, _) in enumerate(plan) for p in range(len(pieces))]
    columns = max(len(choice) for _, _, choices in plan for choice in choices)

    def kernel(*refs):
        inputs = refs[: len(operands)]
        outs = refs[len(operands) : len(operands) + out_count]
        a_buf, w_buf, a_sem, w_sem = refs[len(operands) + out_count :]
        ends = at_end_layer()

        place = lax.axis_index("dp") % INNER

        def rows_copy(step):
            j, p = steps[step]
            start = pl.multiple_of((place ^ plan[j][1][p]) * rows, rows)
            source = inputs[plan[j][0]].at[pl.ds(start, rows)]
            return pltpu.make_async_copy(source, a_buf.at[step % 2], a_sem.at[step % 2])

        def weight_copies(j, choice):
            at = 0
            for i, (k, start, n) in enumerate(plan[j][2][choice]):
                source = inputs[k]
                if source.shape[1] != n:
                    source = source.at[:, pl.ds(start, n)]
                yield pltpu.make_async_copy(
                    source, w_buf.at[j % 2, :, pl.ds(at, n)], w_sem.at[j % 2, i]
                )
                at += n

        def weights(j, action):
            if len(plan[j][2]) == 1:
                for copy in weight_copies(j, 0):
                    action(copy)
                return

            @pl.when(ends)
            def _():
                for copy in weight_copies(j, 1):
                    action(copy)

            @pl.when(jnp.logical_not(ends))
            def _():
                for copy in weight_copies(j, 0):
                    action(copy)

        def begin(copy):
            copy.start()

        def finish(copy):
            copy.wait()

        weights(0, begin)
        rows_copy(0).start()
        for step, (j, p) in enumerate(steps):
            if step + 1 < len(steps):
                rows_copy(step + 1).start()
            if p == 0:
                weights(j, finish)
                if j + 1 < len(plan):
                    weights(j + 1, begin)
            rows_copy(step).wait()
            result = jnp.dot(
                a_buf[step % 2],
                w_buf[j % 2, :, : widths[j]],
                preferred_element_type=jnp.float32,
            ).astype(jnp.bfloat16)
            for k in range(splits[j]):
                out = outs[sum(splits[:j]) + k]
                out[p * rows : (p + 1) * rows, :] = result[:, k * half : (k + 1) * half]

    in_vmem = pl.BlockSpec(memory_space=pltpu.VMEM)
    return pl.pallas_call(
        kernel,
        out_shape=[
            jax.ShapeDtypeStruct((INNER * rows, half), jnp.bfloat16) for _ in range(out_count)
        ],
        in_specs=[pl.BlockSpec(memory_space=pl.ANY)] * len(operands),
        out_specs=[in_vmem] * out_count,
        scratch_shapes=[
            pltpu.VMEM((2, rows, depth), jnp.bfloat16),
            pltpu.VMEM((2, depth, max(widths)), jnp.bfloat16),
            pltpu.SemaphoreType.DMA((2,)),
            pltpu.SemaphoreType.DMA((2, columns)),
        ],
        compiler_params=pltpu.CompilerParams(vmem_limit_bytes=56 * 1024 * 1024),
        cost_estimate=pl.CostEstimate(
            flops=11_000_000_000, bytes_accessed=1000, transcendentals=0
        ),
    )(*operands)


def add_bf16(a, b):
    return (a.astype(jnp.float32) + b.astype(jnp.float32)).astype(jnp.bfloat16)


def to_owners(block, rows):
    pieces = [block[:rows]]
    for bits in range(1, INNER):
        pieces.append(send(block[bits * rows : (bits + 1) * rows], inner_swap(bits)))
    return pieces


def layer_rows(rows):
    groups = [[z * INNER + q for q in range(INNER)] for z in range(LAYERS)]
    return lax.all_gather(rows, "dp", axis_index_groups=groups, axis=0, tiled=True)


def line_pieces(context, output_weight, due, first_states):
    rows = context.shape[0]
    half = output_weight.shape[1] // 2
    quarter = half // 2
    block = 2 * half
    layer = lax.axis_index("dp") // INNER
    at_end = at_end_layer()
    keeps_near = (lax.axis_index("tensor") == 0) == (layer < 2)

    def pin(*values):
        return lax.optimization_barrier(values)

    def swap(near_part, far_part):
        kept = jnp.where(keeps_near, near_part, far_part)
        return kept, send(jnp.where(keeps_near, far_part, near_part), other_tensor)

    def narrow(arrays):
        return [(array, 0, quarter) for array in arrays]

    quarters = [output_weight[:, i * quarter : (i + 1) * quarter] for i in range(4)]
    guest = send(context, inward)
    middle = send(output_weight, mid_swap)
    outer_end = send(output_weight, outward)
    own = layer_rows(context)
    near = [send(after(quarters[0], guest, due), inward)]
    guest, near[0], middle, outer_end, quarters = pin(
        guest, near[0], middle, outer_end, quarters
    )
    guests = layer_rows(guest)
    mid_quarters = [middle[:, i * quarter : (i + 1) * quarter] for i in range(2)]
    mid_a, mid_b = [(middle, 0, half)], [(middle, half, half)]

    far = [send(near[0], mid_swap)]
    near.append(send(quarters[1], inward))
    mid_end = [send(mid_quarters[0], outward)]
    part_own = products(half, (own, [(output_weight, 0, block)], None))
    far[0], near[1], mid_end[0], part_own, quarters, mid_quarters = pin(
        far[0], near[1], mid_end[0], part_own, quarters, mid_quarters
    )

    far.append(send(near[1], mid_swap))
    near.append(send(quarters[2], inward))
    mid_end.append(send(mid_quarters[1], outward))
    part_mid_b, part_outer_a = products(
        half, (own, mid_b + narrow(near[:2]), mid_b + [(outer_end, 0, half)])
    )
    far[1], near[2], mid_end[1], part_mid_b, part_outer_a, quarters = pin(
        far[1], near[2], mid_end[1], part_mid_b, part_outer_a, quarters
    )

    far.append(send(near[2], mid_swap))
    near.append(send(quarters[3], inward))
    (part_mid_a,) = products(half, (own, mid_a, narrow(mid_end)))
    (lent_mid_b,) = products(half, (guests, mid_b, None))
    far[2], near[3], part_mid_a, lent_mid_b = pin(far[2], near[3], part_mid_a, lent_mid_b)

    far.append(send(near[3], mid_swap))
    lent_mid_b = send(lent_mid_b, outward)
    kept_a, came_a = swap(part_own[0], part_mid_a)
    lent_far_a, part_far_a = products(
        half, (guests, narrow(far[:2]), None), (own, narrow(far[:2]), None)
    )
    far[3], lent_mid_b, kept_a, came_a, lent_far_a, part_far_a = pin(
        far[3], lent_mid_b, kept_a, came_a, lent_far_a, part_far_a
    )

    lent_far_a = send(lent_far_a, outward)
    kept_b, came_b = swap(part_own[1], jnp.where(at_end, lent_mid_b, part_mid_b))
    lent_far_b, part_far_b = products(
        half, (guests, narrow(far[2:]), None), (own, narrow(far[2:]), None)
    )
    lent_far_a, kept_a, kept_b, came_b, lent_far_b, part_far_b = pin(
        lent_far_a, add_bf16(kept_a, came_a), kept_b, came_b, lent_far_b, part_far_b
    )

    lent_far_b = send(lent_far_b, outward)
    kept_c, came_c = swap(part_outer_a, jnp.where(at_end, lent_far_a, part_far_a))
    first = to_owners(jnp.concatenate([kept_a, add_bf16(kept_b, came_b)], axis=1), rows)
    (part_outer_b,) = products(half, (own, narrow(near[2:]), [(outer_end, half, half)]))
    lent_far_b, kept_c, came_c, first, part_outer_b = pin(
        lent_far_b, kept_c, came_c, first, part_outer_b
    )

    kept_d, came_d = swap(part_outer_b, jnp.where(at_end, lent_far_b, part_far_b))
    second = to_owners(add_bf16(kept_c, came_c), rows)
    half_done = first_states(first)
    kept_d, came_d, second, half_done = pin(kept_d, came_d, second, half_done)
    return second + to_owners(add_bf16(kept_d, came_d), rows), half_done


def split3(value):
    parts = []
    for _ in range(3):
        parts.append(value.astype(jnp.bfloat16))
        value = value - parts[-1].astype(jnp.float32)
    return parts


def half_states(second, pieces, residual, delta, up_weight, low_rank, before):
    rows, cols = residual.shape
    rank = up_weight.shape[0]
    width = cols // 2
    block = width // INNER
    thin = pieces[0].shape[1]
    count = len(pieces)

    def kernel(*refs):
        piece_refs = refs[:count]
        res_ref, delta_ref, up_ref, low_ref = refs[count : count + 4]
        prior_ref = refs[count + 6] if before else None
        adapted_ref, attn_ref, sums_ref = refs[-11:-8]
        attn, res, delta_v, adapted, up_v, sem, in_sem, out_sem = refs[-8:]
        data_rank = lax.axis_index("dp")
        layer = data_rank // INNER
        place = data_rank % INNER
        low = layer < 2
        keeps_near = (lax.axis_index("tensor") == 0) == low
        first = jnp.where(keeps_near, layer % 2, jnp.where(low, 0, 1))
        side = 1 - first if second else first
        here = pl.ds(pl.multiple_of(side * width, width), width)

        loads = [
            pltpu.make_async_copy(source.at[:, here], to, in_sem.at[i])
            for i, (source, to) in enumerate(((res_ref, res), (delta_ref, delta_v), (up_ref, up_v)))
        ]
        for i, piece in enumerate(piece_refs):
            at = (place ^ (i % INNER)) * block + (i // INNER) * thin
            to = attn.at[:, pl.ds(pl.multiple_of(at, thin), thin)]
            loads.append(pltpu.make_async_copy(piece, to, sem.at[i]))
        for copy in loads:
            copy.start()
        low_parts = jnp.concatenate(split3(ADAPTER_SCALE * low_ref[...]), axis=1)
        if before:
            sums_ref[...] = prior_ref[...]
        else:
            sums_ref[...] = jnp.zeros_like(sums_ref)
        for copy in loads:
            copy.wait()
        attn_out = pltpu.make_async_copy(attn, attn_ref.at[:, here], out_sem.at[0])
        attn_out.start()

        def on_up(values, up):
            return lax.dot_general(
                values, up, (((1,), (1,)), ((), ())), preferred_element_type=jnp.float32
            )

        @pl.loop(0, INNER)
        def _(i):
            part = pl.ds(pl.multiple_of(i * block, block), block)
            up = up_v[:, part]
            low_up = jnp.dot(
                low_parts,
                jnp.concatenate([up] * 3, axis=0),
                preferred_element_type=jnp.float32,
            )
            rest = res[:, part].astype(jnp.float32)
            states = rest + attn[:, part].astype(jnp.float32) + low_up
            target = rest + delta_v[:, part].astype(jnp.float32)
            gap = states - target
            adapted[:, part] = states.astype(jnp.bfloat16)
            squares = on_up(up, up)
            low_sums = 0
            for low_part in split3(squares):
                for j in range(3):
                    low_sums += jnp.dot(
                        low_parts[:, j * rank : (j + 1) * rank],
                        low_part,
                        preferred_element_type=jnp.float32,
                    )
            sums_ref[:, :rank] += on_up(res[:, part], up) + on_up(attn[:, part], up) + low_sums
            for k, product in enumerate((states * states, states * target, gap * gap)):
                sums_ref[:, rank + k : rank + k + 1] += jnp.sum(product, axis=1, keepdims=True)

        adapted_out = pltpu.make_async_copy(adapted, adapted_ref.at[:, here], out_sem.at[1])
        adapted_out.start()
        attn_out.wait()
        adapted_out.wait()

    anywhere = pl.BlockSpec(memory_space=pl.ANY)
    in_vmem = pl.BlockSpec(memory_space=pltpu.VMEM)
    operands = (*pieces, residual, delta, up_weight, low_rank, *(before or ()))
    return pl.pallas_call(
        kernel,
        out_shape=(
            jax.ShapeDtypeStruct((rows, cols), jnp.bfloat16),
            jax.ShapeDtypeStruct((rows, cols), jnp.bfloat16),
            jax.ShapeDtypeStruct((rows, 128), jnp.float32),
        ),
        in_specs=[anywhere] * (count + 3)
        + [in_vmem]
        + ([anywhere, anywhere, in_vmem] if before else []),
        out_specs=(anywhere, anywhere, in_vmem),
        input_output_aliases={count + 4: 0, count + 5: 1} if before else {},
        scratch_shapes=[pltpu.VMEM((rows, width), jnp.bfloat16) for _ in range(4)]
        + [
            pltpu.VMEM((rank, width), jnp.bfloat16),
            pltpu.SemaphoreType.DMA((count,)),
            pltpu.SemaphoreType.DMA((3,)),
            pltpu.SemaphoreType.DMA((2,)),
        ],
        compiler_params=pltpu.CompilerParams(vmem_limit_bytes=32 * 1024 * 1024),
        cost_estimate=pl.CostEstimate(
            flops=11_000_000_000, bytes_accessed=1000, transcendentals=0
        ),
    )(*operands)


def line_grads(sums, came, early_sums, low_t, weights, context, residual, delta, attn, up_weight):
    rows, cols = residual.shape
    rank = up_weight.shape[0]
    width = cols // INNER

    def kernel(*refs):
        sums_ref, came_ref, early_ref, low_ref, weight_ref = refs[:5]
        sources = refs[5:10]
        keep_ref, give_ref = refs[10:12]
        buffers, sem = refs[12:17], refs[17]
        place = lax.axis_index("dp") % INNER

        def loads(j):
            here = pl.ds(pl.multiple_of((place ^ j) * width, width), width)
            return [
                pltpu.make_async_copy(source.at[:, here], buffer.at[j % 2], sem.at[j % 2, i])
                for i, (source, buffer) in enumerate(zip(sources, buffers))
            ]

        for copy in loads(0):
            copy.start()
        sums = sums_ref[...] + came_ref[...]
        early = early_ref[...]
        low = low_ref[...]
        states_up, target_up = sums[:rank], early[:rank]
        norm_h = jnp.sqrt(sums[rank : rank + 1] + NORM_EPS)
        norm_g = jnp.sqrt(early[rank : rank + 1] + NORM_EPS)
        cosine = sums[rank + 1 : rank + 2] / (norm_h * norm_g)
        distance = jnp.sqrt(sums[rank + 2 : rank + 3] + NORM_EPS)
        weight_harm = weight_ref[0:1]
        weight_keep = weight_ref[1:2] / distance
        on_target = weight_harm / (norm_h * norm_g) - weight_keep
        on_states = weight_keep - weight_harm * cosine / (norm_h * norm_h)

        def stacked(value):
            return jnp.concatenate(split3(value), axis=0)

        def total(parts, values):
            product = jnp.dot(parts, values, preferred_element_type=jnp.float32)
            return product[:rank] + product[rank : 2 * rank] + product[2 * rank :]

        twice = ADAPTER_SCALE * low
        for_context = stacked(ADAPTER_SCALE * (on_target * target_up + on_states * states_up))
        for_rest = stacked(twice * (on_target + on_states))
        for_delta = stacked(twice * on_target)
        for_attn = stacked(twice * on_states)
        mixed = lax.dot_general(
            twice * on_states,
            twice,
            (((1,), (1,)), ((), ())),
            precision=HIGHEST,
            preferred_element_type=jnp.float32,
        )
        for_up = stacked(mixed)
        for j in range(INNER):
            if j + 1 < INNER:
                for copy in loads(j + 1):
                    copy.start()
            for copy in loads(j):
                copy.wait()
            ctx, rest, delta_v, attn_v, up = (buffer.at[j % 2] for buffer in buffers)
            out = give_ref if j % 2 else keep_ref
            out[j // 2, :rank, :] = total(for_context, ctx[...])
            out[j // 2, rank:, :] = (
                total(for_rest, rest[...])
                + total(for_delta, delta_v[...])
                + total(for_attn, attn_v[...])
                + total(for_up, up[...])
            )

    anywhere = pl.BlockSpec(memory_space=pl.ANY)
    in_vmem = pl.BlockSpec(memory_space=pltpu.VMEM)
    return pl.pallas_call(
        kernel,
        out_shape=[jax.ShapeDtypeStruct((2, 2 * rank, width), jnp.float32)] * 2,
        in_specs=[in_vmem] * 5 + [anywhere] * 5,
        out_specs=[in_vmem] * 2,
        scratch_shapes=[pltpu.VMEM((2, rows, width), jnp.bfloat16) for _ in range(4)]
        + [
            pltpu.VMEM((2, rank, width), jnp.bfloat16),
            pltpu.SemaphoreType.DMA((2, 5)),
        ],
        compiler_params=pltpu.CompilerParams(vmem_limit_bytes=56 * 1024 * 1024),
        cost_estimate=pl.CostEstimate(
            flops=11_000_000_000, bytes_accessed=1000, transcendentals=0
        ),
    )(sums, came, early_sums, low_t, weights, context, residual, delta, attn, up_weight)


def general_attention(context, output_weight):
    partial = dot_bf16(context, lax.all_gather(output_weight, "dp", axis=1, tiled=True))
    return lax.psum_scatter(partial, "tensor", scatter_dimension=1, tiled=True)


def line_sum_grads(keep, give):
    place = lax.axis_index("dp") % INNER
    rank = keep.shape[1] // 2
    keep = keep + send(give, inner_swap(1))
    both = keep[0] + send(keep[1], inner_swap(2))
    for bits in (1, 2):
        both = both + send(both, lambda z, q, t: (z ^ bits, q, t))
    grad_b = both[rank:]
    other = send(grad_b, other_tensor)
    across = send(both, inner_swap(2))
    across_other = send(grad_b, lambda z, q, t: (z, q ^ 2, 1 - t))

    def joined(bits, mine, got):
        upper = (place & bits) != 0
        return jnp.concatenate(
            [jnp.where(upper, got, mine), jnp.where(upper, mine, got)], axis=1
        )

    mine = jnp.stack([jnp.concatenate([both, other]), jnp.concatenate([across, across_other])])
    got = send(mine, inner_swap(1))
    mine = joined(2, joined(1, mine[0], got[0]), joined(1, mine[1], got[1]))
    grad_a = mine[:rank].T
    kept, other = mine[rank : 2 * rank], mine[2 * rank :]
    first = lax.axis_index("tensor") == 0
    grad_b = jnp.concatenate(
        [jnp.where(first, kept, other), jnp.where(first, other, kept)], axis=1
    )
    return grad_a, grad_b


def general_sum_grads(grad_a_t, grad_b):
    grad_a_t, grad_b = lax.psum((grad_a_t, grad_b), "dp")
    return grad_a_t.T, lax.all_gather(grad_b, "tensor", axis=1, tiled=True)


def solution(mesh):
    line = mesh.shape["dp"] == LAYERS * INNER and mesh.shape["tensor"] == 2

    def sum_tensor(value):
        if line:
            return value + send(value, other_tensor)
        return lax.psum(value, "tensor")

    def local(
        context,
        output_weight,
        adapter_down_weight,
        adapter_up_weight,
        residual,
        frozen_residual_delta,
        harmful_count,
        retain_count,
    ):
        seq_len = context.shape[0]
        tensor_rank = lax.axis_index("tensor")
        data_rank = lax.axis_index("dp")
        harm_total = jnp.sum(harmful_count).astype(jnp.float32)
        keep_total = jnp.sum(retain_count).astype(jnp.float32)
        harm_here = harmful_count[data_rank]
        keep_here = retain_count[data_rank]
        col_count = residual.shape[1]

        low_rank_t = sum_tensor(
            lax.dot_general(
                adapter_down_weight,
                context,
                (((0,), (1,)), ((), ())),
                preferred_element_type=jnp.float32,
            )
        )
        up_narrow = lax.dynamic_slice_in_dim(
            adapter_up_weight, tensor_rank * col_count, col_count, 1
        )
        up_columns = up_narrow.astype(jnp.float32)
        target = residual.astype(jnp.float32) + frozen_residual_delta.astype(jnp.float32)

        def on_up(values):
            return lax.dot_general(
                up_columns, values, (((1,), (1,)), ((), ())), precision=HIGHEST
            )

        rank = up_columns.shape[0]
        early_sums = sum_tensor(
            jnp.concatenate([on_up(target), jnp.sum(target * target, axis=1)[None]], axis=0)
        )
        target_up, sq_target = early_sums[:rank], early_sums[rank]
        positions = jnp.arange(seq_len, dtype=jnp.int32)
        harmful = (positions < harm_here).astype(jnp.float32)
        retained = (
            (positions >= harm_here) & (positions < harm_here + keep_here)
        ).astype(jnp.float32)
        weight_harm = REROUTE_WEIGHT / harm_total * harmful
        weight_keep = RETAIN_WEIGHT / keep_total * retained
        if line:
            weights = jnp.stack([weight_harm, weight_keep])
            low_rank = low_rank_t.T
            constant = (residual, frozen_residual_delta, up_narrow, low_rank)
            pieces, half_done = line_pieces(
                context,
                output_weight,
                (low_rank, early_sums, weights),
                lambda first: half_states(False, first, *constant, None),
            )
            adapted, attn, sums = half_states(True, pieces, *constant, half_done)
            sums = sums[:, : rank + 3].T
            keep, give = line_grads(
                sums,
                send(sums, other_tensor),
                early_sums,
                low_rank_t,
                weights,
                context,
                residual,
                frozen_residual_delta,
                attn,
                up_narrow,
            )
            return adapted, *line_sum_grads(keep, give)
        low_up = ADAPTER_SCALE * lax.dot_general(
            low_rank_t, up_columns, (((0,), (0,)), ((), ())), precision=HIGHEST
        )
        attn = general_attention(context, output_weight).astype(jnp.float32)
        states = residual.astype(jnp.float32) + attn + low_up
        adapted = states.astype(jnp.bfloat16)
        gap = states - target
        products = [states * states, states * target, gap * gap]
        sums = jnp.stack([jnp.sum(product, axis=1) for product in products])
        sums = jnp.concatenate([on_up(states), sums], axis=0)
        shared = sum_tensor(sums)
        states_up = shared[:rank]
        sq_state, cross_term, gap_sq = (shared[rank + i] for i in range(3))

        norm_h = jnp.sqrt(sq_state + NORM_EPS)
        norm_g = jnp.sqrt(sq_target + NORM_EPS)
        cosine = cross_term / (norm_h * norm_g)
        distance = jnp.sqrt(gap_sq + NORM_EPS)
        weight_keep = weight_keep / distance
        on_target = weight_harm / (norm_h * norm_g) - weight_keep
        on_states = weight_keep - weight_harm * cosine / (norm_h * norm_h)

        cotangent = on_target[:, None] * target + on_states[:, None] * states
        low_cot_t = ADAPTER_SCALE * (on_target * target_up + on_states * states_up)
        grad_a_t = jnp.dot(low_cot_t, context.astype(jnp.float32), precision=HIGHEST)
        grad_b = ADAPTER_SCALE * jnp.dot(low_rank_t, cotangent, precision=HIGHEST)
        grad_a, grad_b = general_sum_grads(grad_a_t, grad_b)
        return adapted, grad_a, grad_b

    return jax.shard_map(
        local,
        mesh=mesh,
        in_specs=(
            P("dp", "tensor"),
            P("tensor", "dp"),
            P("tensor", None),
            P(),
            P("dp", "tensor"),
            P("dp", "tensor"),
            P(),
            P(),
        ),
        out_specs=(P("dp", "tensor"), P("tensor", None), P()),
        check_vma=False,
    )
```

```python
import jax
import jax.numpy as jnp
from jax import lax
from jax.experimental import pallas as pl
from jax.experimental.pallas import tpu as pltpu
from jax.sharding import PartitionSpec as P

ADAPTER_SCALE = 2.0
NORM_EPS = 1e-06
REROUTE_WEIGHT = 65536.0
RETAIN_WEIGHT = 1024.0
COST = 100_000_000
INNER = 4
LAYERS = 4
HIGHEST = lax.Precision.HIGHEST


def after(value, *earlier):
    return lax.optimization_barrier((value,) + earlier)[0]


def routes(step):
    pairs = []
    for z in range(LAYERS):
        for q in range(INNER):
            for t in range(2):
                to = step(z, q, t)
                if to is not None:
                    pairs.append(((z * INNER + q) * 2 + t, (to[0] * INNER + to[1]) * 2 + to[2]))
    return pairs


def send(value, step):
    return lax.ppermute(value, ("dp", "tensor"), routes(step))


def inward(z, q, t):
    return {0: (1, q, t), 3: (2, q, t)}.get(z)


def outward(z, q, t):
    return {1: (0, q, t), 2: (3, q, t)}.get(z)


def mid_swap(z, q, t):
    return {1: (2, q, t), 2: (1, q, t)}.get(z)


def inner_swap(bits, layers=range(LAYERS)):
    return lambda z, q, t: (z, q ^ bits, t) if z in layers else None


def other_tensor(z, q, t):
    return (z, q, 1 - t)


def keeps_near(z, t):
    return (t == 0) == (z < 2)


def exchange_but_lent(z, q, t):
    return None if z in (0, 3) and keeps_near(z, t) else (z, q, 1 - t)


def lend_straight(z, q, t):
    return None if keeps_near(z, t) else outward(z, q, t)


def lend_across(z, q, t):
    return outward(z, q, 1 - t) if keeps_near(z, t) else None


def dot_bf16(a, b):
    return jnp.dot(a, b, preferred_element_type=jnp.float32).astype(jnp.bfloat16)


def at_end_layer():
    layer = lax.axis_index("dp") // INNER
    return (layer == 0) | (layer == LAYERS - 1)


def products(*jobs, load=()):
    operands = []

    def index(array):
        for i, known in enumerate(operands):
            if known is array:
                return i
        operands.append(array)
        return len(operands) - 1

    plan = []
    layers = []
    for layer, weights, ends, _ in jobs:
        choices = [weights] if ends is None else [weights, ends]
        if index(layer) not in layers:
            layers.append(index(layer))
        plan.append(
            (
                index(layer),
                [[(index(w), start, n) for w, start, n in choice] for choice in choices],
            )
        )
    depth = jobs[0][0].shape[1]
    rows = jobs[0][0].shape[0] // INNER
    widths = [sum(n for _, _, n in choices[0]) for _, choices in plan]
    cuts = [job[3] for job in jobs]
    out_count = sum(len(cut) for cut in cuts)
    columns = max(len(choice) for _, choices in plan for choice in choices)
    loads = [index(layer) for layer in load]
    kept = len(loads)

    def kernel(*refs):
        inputs = refs[: len(operands)]
        held = refs[len(operands) : len(operands) + kept]
        outs = refs[len(operands) + kept : len(operands) + kept + out_count]
        w_buf, w_sem, a_sem = refs[len(operands) + kept + out_count :]
        ends = at_end_layer()
        place = lax.axis_index("dp") % INNER

        def piece(p):
            return pl.ds(pl.multiple_of((place ^ p) * rows, rows), rows)

        def row_copy(i, p):
            return pltpu.make_async_copy(
                inputs[loads[i]].at[piece(p)], held[i].at[piece(p)], a_sem.at[i, p]
            )

        def weight_copies(j, choice):
            at = 0
            for i, (k, start, n) in enumerate(plan[j][1][choice]):
                source = inputs[k]
                if source.shape[1] != n:
                    source = source.at[:, pl.ds(start, n)]
                yield pltpu.make_async_copy(
                    source, w_buf.at[j % 2, :, pl.ds(at, n)], w_sem.at[j % 2, i]
                )
                at += n

        def weights(j, action):
            if len(plan[j][1]) == 1:
                for copy in weight_copies(j, 0):
                    action(copy)
                return

            @pl.when(ends)
            def _():
                for copy in weight_copies(j, 1):
                    action(copy)

            @pl.when(jnp.logical_not(ends))
            def _():
                for copy in weight_copies(j, 0):
                    action(copy)

        def begin(copy):
            copy.start()

        def finish(copy):
            copy.wait()

        weights(0, begin)
        for i in range(kept):
            for p in range(INNER):
                row_copy(i, p).start()
        out = 0
        for j, (layer, _) in enumerate(plan):
            weights(j, finish)
            if j + 1 < len(plan):
                weights(j + 1, begin)
            source = held[loads.index(layer)] if layer in loads else inputs[layer]
            for p in range(INNER):
                if layer in loads:
                    row_copy(loads.index(layer), p).wait()
                result = jnp.dot(
                    source[piece(p), :],
                    w_buf[j % 2, :, : widths[j]],
                    preferred_element_type=jnp.float32,
                ).astype(jnp.bfloat16)
                at = 0
                for k, width in enumerate(cuts[j]):
                    outs[out + k][p * rows : (p + 1) * rows, :] = result[:, at : at + width]
                    at += width
            out += len(cuts[j])

    in_vmem = pl.BlockSpec(memory_space=pltpu.VMEM)
    in_specs = [pl.BlockSpec(memory_space=pl.ANY)] * len(operands)
    for layer in layers:
        place_in = pltpu.HBM if layer in loads else pltpu.VMEM
        in_specs[layer] = pl.BlockSpec(memory_space=place_in)
        operands[layer] = pltpu.with_memory_space_constraint(operands[layer], place_in)
    resident = [pltpu.VMEM((INNER * rows, depth), jnp.bfloat16)] * kept
    return pl.pallas_call(
        kernel,
        out_shape=resident
        + [
            jax.ShapeDtypeStruct((INNER * rows, width), jnp.bfloat16)
            for cut in cuts
            for width in cut
        ],
        in_specs=in_specs,
        out_specs=[in_vmem] * (out_count + kept),
        scratch_shapes=[
            pltpu.VMEM((2, depth, max(widths)), jnp.bfloat16),
            pltpu.SemaphoreType.DMA((2, columns)),
            pltpu.SemaphoreType.DMA((max(kept, 1), INNER)),
        ],
        compiler_params=pltpu.CompilerParams(vmem_limit_bytes=22 * 1024 * 1024),
        cost_estimate=pl.CostEstimate(
            flops=COST, bytes_accessed=1000, transcendentals=0
        ),
    )(*operands)


def add_bf16(a, b):
    return (a.astype(jnp.float32) + b.astype(jnp.float32)).astype(jnp.bfloat16)


def to_owners(block, rows):
    pieces = [block[:rows]]
    for bits in range(1, INNER):
        pieces.append(send(block[bits * rows : (bits + 1) * rows], inner_swap(bits)))
    return pieces


def layer_rows(rows):
    groups = [[z * INNER + q for q in range(INNER)] for z in range(LAYERS)]
    return lax.all_gather(rows, "dp", axis_index_groups=groups, axis=0, tiled=True)


def line_pieces(context, output_weight, due, first_states):
    rows = context.shape[0]
    half = output_weight.shape[1] // 2
    quarter = half // 2
    block = 2 * half
    layer = lax.axis_index("dp") // INNER
    at_end = at_end_layer()
    near_half = (lax.axis_index("tensor") == 0) == (layer < 2)
    takes_lent = at_end & jnp.logical_not(near_half)

    def pin(*values):
        return lax.optimization_barrier(values)

    def swap(near_part, far_part, step=other_tensor):
        kept = jnp.where(near_half, near_part, far_part)
        return kept, send(jnp.where(near_half, far_part, near_part), step)

    def lend(part):
        return send(part, lend_straight), send(part, lend_across)

    def total(kept, came, lent):
        return add_bf16(
            jnp.where(takes_lent, lent[0], kept), jnp.where(takes_lent, lent[1], came)
        )

    def narrow(arrays):
        return [(array, 0, quarter) for array in arrays]

    quarters = [output_weight[:, i * quarter : (i + 1) * quarter] for i in range(4)]
    guest = send(context, inward)
    middle = send(output_weight, mid_swap)
    outer_end = send(output_weight, outward)
    own = layer_rows(context)
    near = [send(after(quarters[0], guest, due), inward)]
    guest, near[0], middle, outer_end, quarters, near_half, takes_lent = pin(
        guest, near[0], middle, outer_end, quarters, near_half, takes_lent
    )
    guests = layer_rows(guest)
    mid_quarters = [middle[:, i * quarter : (i + 1) * quarter] for i in range(2)]
    mid_a, mid_b = [(middle, 0, half)], [(middle, half, half)]

    far = [send(near[0], mid_swap)]
    near.append(send(quarters[1], inward))
    mid_end = [send(mid_quarters[0], outward)]
    resident, *part_own = products(
        (own, [(output_weight, 0, block)], None, [quarter, quarter, half]), load=(own,)
    )
    far[0], near[1], mid_end[0], resident, part_own, quarters, mid_quarters = pin(
        far[0], near[1], mid_end[0], resident, part_own, quarters, mid_quarters
    )

    far.append(send(near[1], mid_swap))
    near.append(send(quarters[2], inward))
    mid_end.append(send(mid_quarters[1], outward))
    part_mid_b, part_outer_a, part_mid_0 = products(
        (resident, mid_b + narrow(near[:2]), mid_b + [(outer_end, 0, half)], [half, half]),
        (resident, [(middle, 0, quarter)], narrow(mid_end[:1]), [quarter]),
    )
    far[1], near[2], mid_end[1], part_mid_b, part_outer_a, part_mid_0, quarters = pin(
        far[1], near[2], mid_end[1], part_mid_b, part_outer_a, part_mid_0, quarters
    )

    far.append(send(near[2], mid_swap))
    near.append(send(quarters[3], inward))
    swap_0 = swap(part_own[0], part_mid_0)
    swap_b = swap(part_own[2], part_mid_b, exchange_but_lent)
    _, part_mid_1 = products(
        (own, [(middle, quarter, quarter)], narrow(mid_end[1:]), [quarter]), load=(own,)
    )
    guests = after(guests, part_mid_1)
    guests, lent_b = products((guests, mid_b, None, [half]), load=(guests,))
    far[2], near[3], swap_0, swap_b, part_mid_1, guests, lent_b = pin(
        far[2], near[3], swap_0, swap_b, part_mid_1, guests, lent_b
    )

    far.append(send(near[3], mid_swap))
    lent_b = lend(lent_b)
    swap_1 = swap(part_own[1], part_mid_1)
    own, lent_c, part_far_a, part_outer_b = products(
        (guests, narrow(far[:2]), None, [half]),
        (
            own,
            narrow(far[:2]) + narrow(near[2:]),
            narrow(far[:2]) + [(outer_end, half, half)],
            [half, half],
        ),
        load=(own,),
    )
    far[3], lent_b, swap_1, own, lent_c, part_far_a, part_outer_b = pin(
        far[3], lent_b, swap_1, own, lent_c, part_far_a, part_outer_b
    )

    lent_c = lend(lent_c)
    swap_c = swap(part_outer_a, part_far_a, exchange_but_lent)
    first = [add_bf16(*swap_0), add_bf16(*swap_1), total(*swap_b, lent_b)]
    first = to_owners(jnp.concatenate(first, axis=1), rows)
    lent_d, part_far_b = products(
        (guests, narrow(far[2:]), None, [half]), (own, narrow(far[2:]), None, [half])
    )
    lent_c, swap_c, first, lent_d, part_far_b = pin(lent_c, swap_c, first, lent_d, part_far_b)

    lent_d = lend(lent_d)
    swap_d = swap(part_outer_b, part_far_b, exchange_but_lent)
    second = to_owners(total(*swap_c, lent_c), rows)
    half_done = first_states(first)
    lent_d, swap_d, second, half_done = pin(lent_d, swap_d, second, half_done)
    return second + to_owners(total(*swap_d, lent_d), rows), half_done


def split3(value):
    parts = []
    for _ in range(3):
        parts.append(value.astype(jnp.bfloat16))
        value = value - parts[-1].astype(jnp.float32)
    return parts


def half_states(second, pieces, residual, delta, up_weight, low_rank, before):
    rows, cols = residual.shape
    rank = up_weight.shape[0]
    width = cols // 2
    block = width // INNER
    thin = pieces[0].shape[1]
    count = len(pieces)

    def kernel(*refs):
        piece_refs = refs[:count]
        res_ref, delta_ref, up_ref, low_ref = refs[count : count + 4]
        prior_ref = refs[count + 6] if before else None
        adapted_ref, attn_ref, sums_ref = refs[-11:-8]
        attn, res, delta_v, adapted, up_v, sem, in_sem, out_sem = refs[-8:]
        data_rank = lax.axis_index("dp")
        layer = data_rank // INNER
        place = data_rank % INNER
        low = layer < 2
        keeps_near = (lax.axis_index("tensor") == 0) == low
        first = jnp.where(keeps_near, layer % 2, jnp.where(low, 0, 1))
        side = 1 - first if second else first
        here = pl.ds(pl.multiple_of(side * width, width), width)

        loads = [
            pltpu.make_async_copy(source.at[:, here], to, in_sem.at[i])
            for i, (source, to) in enumerate(((res_ref, res), (delta_ref, delta_v), (up_ref, up_v)))
        ]
        for i, piece in enumerate(piece_refs):
            at = (place ^ (i % INNER)) * block + (i // INNER) * thin
            to = attn.at[:, pl.ds(pl.multiple_of(at, thin), thin)]
            loads.append(pltpu.make_async_copy(piece, to, sem.at[i]))
        for copy in loads:
            copy.start()
        low_parts = jnp.concatenate(split3(ADAPTER_SCALE * low_ref[...].T), axis=1)
        if before:
            sums_ref[...] = prior_ref[...]
        else:
            sums_ref[...] = jnp.zeros_like(sums_ref)
        for copy in loads:
            copy.wait()
        attn_out = pltpu.make_async_copy(attn, attn_ref.at[:, here], out_sem.at[0])
        attn_out.start()

        def on_up(values, up):
            return lax.dot_general(
                values, up, (((1,), (1,)), ((), ())), preferred_element_type=jnp.float32
            )

        @pl.loop(0, INNER)
        def _(i):
            part = pl.ds(pl.multiple_of(i * block, block), block)
            up = up_v[:, part]
            low_up = jnp.dot(
                low_parts,
                jnp.concatenate([up] * 3, axis=0),
                preferred_element_type=jnp.float32,
            )
            rest = res[:, part].astype(jnp.float32)
            states = rest + attn[:, part].astype(jnp.float32) + low_up
            target = rest + delta_v[:, part].astype(jnp.float32)
            gap = states - target
            adapted[:, part] = states.astype(jnp.bfloat16)
            squares = on_up(up, up)
            low_sums = 0
            for low_part in split3(squares):
                for j in range(3):
                    low_sums += jnp.dot(
                        low_parts[:, j * rank : (j + 1) * rank],
                        low_part,
                        preferred_element_type=jnp.float32,
                    )
            sums_ref[:, :rank] += on_up(res[:, part], up) + on_up(attn[:, part], up) + low_sums
            for k, product in enumerate((states * states, states * target, gap * gap)):
                sums_ref[:, rank + k : rank + k + 1] += jnp.sum(product, axis=1, keepdims=True)

        adapted_out = pltpu.make_async_copy(adapted, adapted_ref.at[:, here], out_sem.at[1])
        adapted_out.start()
        attn_out.wait()
        adapted_out.wait()

    anywhere = pl.BlockSpec(memory_space=pl.ANY)
    in_vmem = pl.BlockSpec(memory_space=pltpu.VMEM)
    operands = (*pieces, residual, delta, up_weight, low_rank, *(before or ()))
    return pl.pallas_call(
        kernel,
        out_shape=(
            jax.ShapeDtypeStruct((rows, cols), jnp.bfloat16),
            jax.ShapeDtypeStruct((rows, cols), jnp.bfloat16),
            jax.ShapeDtypeStruct((rows, 128), jnp.float32),
        ),
        in_specs=[anywhere] * (count + 3)
        + [in_vmem]
        + ([anywhere, anywhere, in_vmem] if before else []),
        out_specs=(anywhere, anywhere, in_vmem),
        input_output_aliases={count + 4: 0, count + 5: 1} if before else {},
        scratch_shapes=[pltpu.VMEM((rows, width), jnp.bfloat16) for _ in range(4)]
        + [
            pltpu.VMEM((rank, width), jnp.bfloat16),
            pltpu.SemaphoreType.DMA((count,)),
            pltpu.SemaphoreType.DMA((3,)),
            pltpu.SemaphoreType.DMA((2,)),
        ],
        compiler_params=pltpu.CompilerParams(vmem_limit_bytes=32 * 1024 * 1024),
        cost_estimate=pl.CostEstimate(
            flops=COST, bytes_accessed=1000, transcendentals=0
        ),
    )(*operands)


def line_grads(sums, came, early_sums, low_t, weights, context, residual, delta, attn, up_weight):
    rows, cols = residual.shape
    rank = up_weight.shape[0]
    width = cols // INNER

    def kernel(*refs):
        sums_ref, came_ref, early_ref, low_ref, weight_ref = refs[:5]
        sources = refs[5:10]
        keep_ref, give_ref = refs[10:12]
        buffers, sem = refs[12:17], refs[17]
        place = lax.axis_index("dp") % INNER

        def loads(j):
            here = pl.ds(pl.multiple_of((place ^ j) * width, width), width)
            return [
                pltpu.make_async_copy(source.at[:, here], buffer.at[j % 2], sem.at[j % 2, i])
                for i, (source, buffer) in enumerate(zip(sources, buffers))
            ]

        for copy in loads(0):
            copy.start()
        sums = sums_ref[...] + came_ref[...]
        early = early_ref[...]
        low = low_ref[...]
        states_up, target_up = sums[:rank], early[:rank]
        norm_h = jnp.sqrt(sums[rank : rank + 1] + NORM_EPS)
        norm_g = jnp.sqrt(early[rank : rank + 1] + NORM_EPS)
        cosine = sums[rank + 1 : rank + 2] / (norm_h * norm_g)
        distance = jnp.sqrt(sums[rank + 2 : rank + 3] + NORM_EPS)
        weight_harm = weight_ref[0:1]
        weight_keep = weight_ref[1:2] / distance
        on_target = weight_harm / (norm_h * norm_g) - weight_keep
        on_states = weight_keep - weight_harm * cosine / (norm_h * norm_h)

        def stacked(value):
            return jnp.concatenate(split3(value), axis=0)

        def total(parts, values):
            product = jnp.dot(parts, values, preferred_element_type=jnp.float32)
            return product[:rank] + product[rank : 2 * rank] + product[2 * rank :]

        twice = ADAPTER_SCALE * low
        for_context = stacked(ADAPTER_SCALE * (on_target * target_up + on_states * states_up))
        for_rest = stacked(twice * (on_target + on_states))
        for_delta = stacked(twice * on_target)
        for_attn = stacked(twice * on_states)
        mixed = lax.dot_general(
            twice * on_states,
            twice,
            (((1,), (1,)), ((), ())),
            precision=HIGHEST,
            preferred_element_type=jnp.float32,
        )
        for_up = stacked(mixed)
        for j in range(INNER):
            if j + 1 < INNER:
                for copy in loads(j + 1):
                    copy.start()
            for copy in loads(j):
                copy.wait()
            ctx, rest, delta_v, attn_v, up = (buffer.at[j % 2] for buffer in buffers)
            out = give_ref if j % 2 else keep_ref
            out[j // 2, :rank, :] = total(for_context, ctx[...])
            out[j // 2, rank:, :] = (
                total(for_rest, rest[...])
                + total(for_delta, delta_v[...])
                + total(for_attn, attn_v[...])
                + total(for_up, up[...])
            )

    anywhere = pl.BlockSpec(memory_space=pl.ANY)
    in_vmem = pl.BlockSpec(memory_space=pltpu.VMEM)
    return pl.pallas_call(
        kernel,
        out_shape=[jax.ShapeDtypeStruct((2, 2 * rank, width), jnp.float32)] * 2,
        in_specs=[in_vmem] * 5 + [anywhere] * 5,
        out_specs=[in_vmem] * 2,
        scratch_shapes=[pltpu.VMEM((2, rows, width), jnp.bfloat16) for _ in range(4)]
        + [
            pltpu.VMEM((2, rank, width), jnp.bfloat16),
            pltpu.SemaphoreType.DMA((2, 5)),
        ],
        compiler_params=pltpu.CompilerParams(vmem_limit_bytes=56 * 1024 * 1024),
        cost_estimate=pl.CostEstimate(
            flops=COST, bytes_accessed=1000, transcendentals=0
        ),
    )(sums, came, early_sums, low_t, weights, context, residual, delta, attn, up_weight)


def general_attention(context, output_weight):
    partial = dot_bf16(context, lax.all_gather(output_weight, "dp", axis=1, tiled=True))
    return lax.psum_scatter(partial, "tensor", scatter_dimension=1, tiled=True)


def line_sum_grads(keep, give):
    place = lax.axis_index("dp") % INNER
    rank = keep.shape[1] // 2
    keep = keep + send(give, inner_swap(1))
    both = keep[0] + send(keep[1], inner_swap(2))
    for bits in (1, 2):
        both = both + send(both, lambda z, q, t: (z ^ bits, q, t))
    grad_b = both[rank:]
    other = send(grad_b, other_tensor)
    across = send(both, inner_swap(2))
    across_other = send(grad_b, lambda z, q, t: (z, q ^ 2, 1 - t))

    def joined(bits, mine, got):
        upper = (place & bits) != 0
        return jnp.concatenate(
            [jnp.where(upper, got, mine), jnp.where(upper, mine, got)], axis=1
        )

    mine = jnp.stack([jnp.concatenate([both, other]), jnp.concatenate([across, across_other])])
    got = send(mine, inner_swap(1))
    mine = joined(2, joined(1, mine[0], got[0]), joined(1, mine[1], got[1]))
    grad_a = mine[:rank].T
    kept, other = mine[rank : 2 * rank], mine[2 * rank :]
    first = lax.axis_index("tensor") == 0
    grad_b = jnp.concatenate(
        [jnp.where(first, kept, other), jnp.where(first, other, kept)], axis=1
    )
    return grad_a, grad_b


def general_sum_grads(grad_a_t, grad_b):
    grad_a_t, grad_b = lax.psum((grad_a_t, grad_b), "dp")
    return grad_a_t.T, lax.all_gather(grad_b, "tensor", axis=1, tiled=True)


def solution(mesh):
    line = mesh.shape["dp"] == LAYERS * INNER and mesh.shape["tensor"] == 2

    def sum_tensor(value):
        if line:
            return value + send(value, other_tensor)
        return lax.psum(value, "tensor")

    def local(
        context,
        output_weight,
        adapter_down_weight,
        adapter_up_weight,
        residual,
        frozen_residual_delta,
        harmful_count,
        retain_count,
    ):
        seq_len = context.shape[0]
        tensor_rank = lax.axis_index("tensor")
        data_rank = lax.axis_index("dp")
        harm_total = jnp.sum(harmful_count).astype(jnp.float32)
        keep_total = jnp.sum(retain_count).astype(jnp.float32)
        harm_here = harmful_count[data_rank]
        keep_here = retain_count[data_rank]
        col_count = residual.shape[1]

        low_rank_t = sum_tensor(
            lax.dot_general(
                adapter_down_weight,
                context,
                (((0,), (1,)), ((), ())),
                preferred_element_type=jnp.float32,
            )
        )
        up_narrow = lax.dynamic_slice_in_dim(
            adapter_up_weight, tensor_rank * col_count, col_count, 1
        )
        up_columns = up_narrow.astype(jnp.float32)
        target = residual.astype(jnp.float32) + frozen_residual_delta.astype(jnp.float32)

        def on_up(values):
            return lax.dot_general(
                up_columns, values, (((1,), (1,)), ((), ())), precision=HIGHEST
            )

        rank = up_columns.shape[0]
        early_sums = sum_tensor(
            jnp.concatenate([on_up(target), jnp.sum(target * target, axis=1)[None]], axis=0)
        )
        target_up, sq_target = early_sums[:rank], early_sums[rank]
        positions = jnp.arange(seq_len, dtype=jnp.int32)
        harmful = (positions < harm_here).astype(jnp.float32)
        retained = (
            (positions >= harm_here) & (positions < harm_here + keep_here)
        ).astype(jnp.float32)
        weight_harm = REROUTE_WEIGHT / harm_total * harmful
        weight_keep = RETAIN_WEIGHT / keep_total * retained
        if line:
            weights = jnp.stack([weight_harm, weight_keep])
            constant = (residual, frozen_residual_delta, up_narrow, low_rank_t)
            pieces, half_done = line_pieces(
                context,
                output_weight,
                (low_rank_t, early_sums, weights),
                lambda first: half_states(False, first, *constant, None),
            )
            adapted, attn, sums = half_states(True, pieces, *constant, half_done)
            sums = sums[:, : rank + 3].T
            keep, give = line_grads(
                sums,
                send(sums, other_tensor),
                early_sums,
                low_rank_t,
                weights,
                context,
                residual,
                frozen_residual_delta,
                attn,
                up_narrow,
            )
            return adapted, *line_sum_grads(keep, give)
        low_up = ADAPTER_SCALE * lax.dot_general(
            low_rank_t, up_columns, (((0,), (0,)), ((), ())), precision=HIGHEST
        )
        attn = general_attention(context, output_weight).astype(jnp.float32)
        states = residual.astype(jnp.float32) + attn + low_up
        adapted = states.astype(jnp.bfloat16)
        gap = states - target
        products = [states * states, states * target, gap * gap]
        sums = jnp.stack([jnp.sum(product, axis=1) for product in products])
        sums = jnp.concatenate([on_up(states), sums], axis=0)
        shared = sum_tensor(sums)
        states_up = shared[:rank]
        sq_state, cross_term, gap_sq = (shared[rank + i] for i in range(3))

        norm_h = jnp.sqrt(sq_state + NORM_EPS)
        norm_g = jnp.sqrt(sq_target + NORM_EPS)
        cosine = cross_term / (norm_h * norm_g)
        distance = jnp.sqrt(gap_sq + NORM_EPS)
        weight_keep = weight_keep / distance
        on_target = weight_harm / (norm_h * norm_g) - weight_keep
        on_states = weight_keep - weight_harm * cosine / (norm_h * norm_h)

        cotangent = on_target[:, None] * target + on_states[:, None] * states
        low_cot_t = ADAPTER_SCALE * (on_target * target_up + on_states * states_up)
        grad_a_t = jnp.dot(low_cot_t, context.astype(jnp.float32), precision=HIGHEST)
        grad_b = ADAPTER_SCALE * jnp.dot(low_rank_t, cotangent, precision=HIGHEST)
        grad_a, grad_b = general_sum_grads(grad_a_t, grad_b)
        return adapted, grad_a, grad_b

    return jax.shard_map(
        local,
        mesh=mesh,
        in_specs=(
            P("dp", "tensor"),
            P("tensor", "dp"),
            P("tensor", None),
            P(),
            P("dp", "tensor"),
            P("dp", "tensor"),
            P(),
            P(),
        ),
        out_specs=(P("dp", "tensor"), P("tensor", None), P()),
        check_vma=False,
    )
```

```python
import jax
import jax.numpy as jnp
from jax import lax
from jax.experimental import pallas as pl
from jax.experimental.pallas import tpu as pltpu
from jax.sharding import PartitionSpec as P

ADAPTER_SCALE = 2.0
NORM_EPS = 1e-06
REROUTE_WEIGHT = 65536.0
RETAIN_WEIGHT = 1024.0
COST = 100_000_000
INNER = 4
LAYERS = 4
HIGHEST = lax.Precision.HIGHEST


def after(value, *earlier):
    return lax.optimization_barrier((value,) + earlier)[0]


def routes(step):
    pairs = []
    for z in range(LAYERS):
        for q in range(INNER):
            for t in range(2):
                to = step(z, q, t)
                if to is not None:
                    pairs.append(((z * INNER + q) * 2 + t, (to[0] * INNER + to[1]) * 2 + to[2]))
    return pairs


def send(value, step):
    return lax.ppermute(value, ("dp", "tensor"), routes(step))


def inward(z, q, t):
    return {0: (1, q, t), 3: (2, q, t)}.get(z)


def outward(z, q, t):
    return {1: (0, q, t), 2: (3, q, t)}.get(z)


def mid_swap(z, q, t):
    return {1: (2, q, t), 2: (1, q, t)}.get(z)


def inner_swap(bits, layers=range(LAYERS)):
    return lambda z, q, t: (z, q ^ bits, t) if z in layers else None


def other_tensor(z, q, t):
    return (z, q, 1 - t)


def keeps_near(z, t):
    return (t == 0) == (z < 2)


def exchange_but_lent(z, q, t):
    return None if z in (0, 3) and keeps_near(z, t) else (z, q, 1 - t)


def lend_straight(z, q, t):
    return None if keeps_near(z, t) else outward(z, q, t)


def lend_across(z, q, t):
    return outward(z, q, 1 - t) if keeps_near(z, t) else None


def dot_bf16(a, b):
    return jnp.dot(a, b, preferred_element_type=jnp.float32).astype(jnp.bfloat16)


def at_end_layer():
    layer = lax.axis_index("dp") // INNER
    return (layer == 0) | (layer == LAYERS - 1)


def products(*jobs, load=(), cost=COST):
    operands = []

    def index(array):
        for i, known in enumerate(operands):
            if known is array:
                return i
        operands.append(array)
        return len(operands) - 1

    plan = []
    layers = []
    for layer, weights, ends, _ in jobs:
        choices = [weights] if ends is None else [weights, ends]
        if index(layer) not in layers:
            layers.append(index(layer))
        plan.append(
            (
                index(layer),
                [[(index(w), start, n) for w, start, n in choice] for choice in choices],
            )
        )
    depth = jobs[0][0].shape[1]
    rows = jobs[0][0].shape[0] // INNER
    widths = [sum(n for _, _, n in choices[0]) for _, choices in plan]
    cuts = [job[3] for job in jobs]
    out_count = sum(len(cut) for cut in cuts)
    columns = max(len(choice) for _, choices in plan for choice in choices)
    loads = [index(layer) for layer in load]
    kept = len(loads)

    def kernel(*refs):
        inputs = refs[: len(operands)]
        held = refs[len(operands) : len(operands) + kept]
        outs = refs[len(operands) + kept : len(operands) + kept + out_count]
        w_buf, w_sem, a_sem = refs[len(operands) + kept + out_count :]
        ends = at_end_layer()
        place = lax.axis_index("dp") % INNER

        def piece(p):
            return pl.ds(pl.multiple_of((place ^ p) * rows, rows), rows)

        def row_copy(i, p):
            return pltpu.make_async_copy(
                inputs[loads[i]].at[piece(p)], held[i].at[piece(p)], a_sem.at[i, p]
            )

        def weight_copies(j, choice):
            at = 0
            for i, (k, start, n) in enumerate(plan[j][1][choice]):
                source = inputs[k]
                if source.shape[1] != n:
                    source = source.at[:, pl.ds(start, n)]
                yield pltpu.make_async_copy(
                    source, w_buf.at[j % 2, :, pl.ds(at, n)], w_sem.at[j % 2, i]
                )
                at += n

        def weights(j, action):
            if len(plan[j][1]) == 1:
                for copy in weight_copies(j, 0):
                    action(copy)
                return

            @pl.when(ends)
            def _():
                for copy in weight_copies(j, 1):
                    action(copy)

            @pl.when(jnp.logical_not(ends))
            def _():
                for copy in weight_copies(j, 0):
                    action(copy)

        def begin(copy):
            copy.start()

        def finish(copy):
            copy.wait()

        weights(0, begin)
        for i in range(kept):
            for p in range(INNER):
                row_copy(i, p).start()
        out = 0
        for j, (layer, _) in enumerate(plan):
            weights(j, finish)
            if j + 1 < len(plan):
                weights(j + 1, begin)
            source = inputs[layer]
            if layer in loads:
                source = held[loads.index(layer)]
                for p in range(INNER):
                    row_copy(loads.index(layer), p).wait()
            for p in range(INNER):
                result = jnp.dot(
                    source[piece(p), :],
                    w_buf[j % 2, :, : widths[j]],
                    preferred_element_type=jnp.float32,
                ).astype(jnp.bfloat16)
                at = 0
                for k, width in enumerate(cuts[j]):
                    outs[out + k][p * rows : (p + 1) * rows, :] = result[:, at : at + width]
                    at += width
            out += len(cuts[j])

    in_vmem = pl.BlockSpec(memory_space=pltpu.VMEM)
    in_specs = [pl.BlockSpec(memory_space=pl.ANY)] * len(operands)
    for i, operand in enumerate(operands):
        place_in = pltpu.VMEM if i in layers and i not in loads else pltpu.HBM
        in_specs[i] = pl.BlockSpec(memory_space=place_in)
        operands[i] = pltpu.with_memory_space_constraint(operand, place_in)
    resident = [pltpu.VMEM((INNER * rows, depth), jnp.bfloat16)] * kept
    return pl.pallas_call(
        kernel,
        out_shape=resident
        + [
            jax.ShapeDtypeStruct((INNER * rows, width), jnp.bfloat16)
            for cut in cuts
            for width in cut
        ],
        in_specs=in_specs,
        out_specs=[in_vmem] * (out_count + kept),
        scratch_shapes=[
            pltpu.VMEM((2, depth, max(widths)), jnp.bfloat16),
            pltpu.SemaphoreType.DMA((2, columns)),
            pltpu.SemaphoreType.DMA((max(kept, 1), INNER)),
        ],
        compiler_params=pltpu.CompilerParams(vmem_limit_bytes=22 * 1024 * 1024),
        cost_estimate=pl.CostEstimate(
            flops=cost, bytes_accessed=1000, transcendentals=0
        ),
    )(*operands)


def add_bf16(a, b):
    return (a.astype(jnp.float32) + b.astype(jnp.float32)).astype(jnp.bfloat16)


def to_owners(block, rows):
    pieces = [block[:rows]]
    for bits in range(1, INNER):
        pieces.append(send(block[bits * rows : (bits + 1) * rows], inner_swap(bits)))
    return pieces


def layer_rows(rows):
    groups = [[z * INNER + q for q in range(INNER)] for z in range(LAYERS)]
    return lax.all_gather(rows, "dp", axis_index_groups=groups, axis=0, tiled=True)


def line_pieces(context, output_weight, due, first_states):
    rows = context.shape[0]
    half = output_weight.shape[1] // 2
    quarter = half // 2
    block = 2 * half
    layer = lax.axis_index("dp") // INNER
    at_end = at_end_layer()
    near_half = (lax.axis_index("tensor") == 0) == (layer < 2)
    takes_lent = at_end & jnp.logical_not(near_half)

    def pin(*values):
        return lax.optimization_barrier(values)

    def swap(near_part, far_part, step=other_tensor):
        kept = jnp.where(near_half, near_part, far_part)
        return kept, send(jnp.where(near_half, far_part, near_part), step)

    def lend(part):
        return send(part, lend_straight), send(part, lend_across)

    def total(kept, came, lent):
        return add_bf16(
            jnp.where(takes_lent, lent[0], kept), jnp.where(takes_lent, lent[1], came)
        )

    def narrow(arrays):
        return [(array, 0, quarter) for array in arrays]

    quarters = [output_weight[:, i * quarter : (i + 1) * quarter] for i in range(4)]
    guest = send(context, inward)
    middle = send(output_weight, mid_swap)
    outer_end = send(output_weight, outward)
    own = layer_rows(context)
    near = [send(after(quarters[0], guest, due), inward)]
    guest, near[0], middle, outer_end, quarters, near_half, takes_lent = pin(
        guest, near[0], middle, outer_end, quarters, near_half, takes_lent
    )
    guests = layer_rows(guest)
    mid_quarters = [middle[:, i * quarter : (i + 1) * quarter] for i in range(2)]
    mid_a, mid_b = [(middle, 0, half)], [(middle, half, half)]

    far = [send(near[0], mid_swap)]
    near.append(send(quarters[1], inward))
    mid_end = [send(mid_quarters[0], outward)]
    resident, *part_own = products(
        (own, [(output_weight, 0, block)], None, [quarter, quarter, half]), load=(own,)
    )
    far[0], near[1], mid_end[0], resident, part_own, quarters, mid_quarters = pin(
        far[0], near[1], mid_end[0], resident, part_own, quarters, mid_quarters
    )

    far.append(send(near[1], mid_swap))
    near.append(send(quarters[2], inward))
    mid_end.append(send(mid_quarters[1], outward))
    part_mid_b, part_outer_a, part_mid_0 = products(
        (resident, mid_b + narrow(near[:2]), mid_b + [(outer_end, 0, half)], [half, half]),
        (resident, [(middle, 0, quarter)], narrow(mid_end[:1]), [quarter]),
    )
    far[1], near[2], mid_end[1], part_mid_b, part_outer_a, part_mid_0, quarters = pin(
        far[1], near[2], mid_end[1], part_mid_b, part_outer_a, part_mid_0, quarters
    )

    far.append(send(near[2], mid_swap))
    near.append(send(quarters[3], inward))
    swap_0 = swap(part_own[0], part_mid_0)
    swap_b = swap(part_own[2], part_mid_b, exchange_but_lent)
    _, part_mid_1 = products(
        (own, [(middle, quarter, quarter)], narrow(mid_end[1:]), [quarter]),
        load=(own,),
        cost=100 * COST,
    )
    swap_1 = swap(part_own[1], part_mid_1)
    guests = after(guests, part_mid_1, swap_0)
    guests, lent_b = products((guests, mid_b, None, [half]), load=(guests,))
    far[2], near[3], swap_0, swap_1, swap_b, guests, lent_b = pin(
        far[2], near[3], swap_0, swap_1, swap_b, guests, lent_b
    )

    far.append(send(near[3], mid_swap))
    lent_b = lend(lent_b)
    own, lent_c, part_far_a, part_outer_b = products(
        (guests, narrow(far[:2]), None, [half]),
        (
            own,
            narrow(far[:2]) + narrow(near[2:]),
            narrow(far[:2]) + [(outer_end, half, half)],
            [half, half],
        ),
        load=(own,),
    )
    far[3], lent_b, own, lent_c, part_far_a, part_outer_b = pin(
        far[3], lent_b, own, lent_c, part_far_a, part_outer_b
    )

    lent_c = lend(lent_c)
    swap_c = swap(part_outer_a, part_far_a, exchange_but_lent)
    first = [add_bf16(*swap_0), add_bf16(*swap_1), total(*swap_b, lent_b)]
    first = to_owners(jnp.concatenate(first, axis=1), rows)
    lent_d, part_far_b = products(
        (guests, narrow(far[2:]), None, [half]), (own, narrow(far[2:]), None, [half])
    )
    lent_c, swap_c, first, lent_d, part_far_b = pin(lent_c, swap_c, first, lent_d, part_far_b)

    lent_d = lend(lent_d)
    swap_d = swap(part_outer_b, part_far_b, exchange_but_lent)
    second = to_owners(total(*swap_c, lent_c), rows)
    half_done = first_states(first)
    lent_d, swap_d, second, half_done = pin(lent_d, swap_d, second, half_done)
    return second + to_owners(total(*swap_d, lent_d), rows), half_done


def split3(value):
    parts = []
    for _ in range(3):
        parts.append(value.astype(jnp.bfloat16))
        value = value - parts[-1].astype(jnp.float32)
    return parts


def half_states(second, pieces, residual, delta, up_weight, low_rank, before):
    rows, cols = residual.shape
    rank = up_weight.shape[0]
    width = cols // 2
    block = width // INNER
    thin = pieces[0].shape[1]
    count = len(pieces)

    def kernel(*refs):
        piece_refs = refs[:count]
        res_ref, delta_ref, up_ref, low_ref = refs[count : count + 4]
        prior_ref = refs[count + 6] if before else None
        adapted_ref, attn_ref, sums_out = refs[-12:-9]
        attn, res, delta_v, adapted, up_v, sums_ref, sem, in_sem, out_sem = refs[-9:]
        data_rank = lax.axis_index("dp")
        layer = data_rank // INNER
        place = data_rank % INNER
        low = layer < 2
        keeps_near = (lax.axis_index("tensor") == 0) == low
        first = jnp.where(keeps_near, layer % 2, jnp.where(low, 0, 1))
        side = 1 - first if second else first
        here = pl.ds(pl.multiple_of(side * width, width), width)

        loads = [
            pltpu.make_async_copy(source.at[:, here], to, in_sem.at[i])
            for i, (source, to) in enumerate(((res_ref, res), (delta_ref, delta_v), (up_ref, up_v)))
        ]
        for i, piece in enumerate(piece_refs):
            at = (place ^ (i % INNER)) * block + (i // INNER) * thin
            to = attn.at[:, pl.ds(pl.multiple_of(at, thin), thin)]
            loads.append(pltpu.make_async_copy(piece, to, sem.at[i]))
        for copy in loads:
            copy.start()
        low_parts = jnp.concatenate(split3(ADAPTER_SCALE * low_ref[...].T), axis=1)
        if before:
            sums_ref[...] = prior_ref[...]
        else:
            sums_ref[...] = jnp.zeros_like(sums_ref)
        for copy in loads:
            copy.wait()
        attn_out = pltpu.make_async_copy(attn, attn_ref.at[:, here], out_sem.at[0])
        attn_out.start()

        def on_up(values, up):
            return lax.dot_general(
                values, up, (((1,), (1,)), ((), ())), preferred_element_type=jnp.float32
            )

        @pl.loop(0, INNER)
        def _(i):
            part = pl.ds(pl.multiple_of(i * block, block), block)
            up = up_v[:, part]
            low_up = jnp.dot(
                low_parts,
                jnp.concatenate([up] * 3, axis=0),
                preferred_element_type=jnp.float32,
            )
            rest = res[:, part].astype(jnp.float32)
            states = rest + attn[:, part].astype(jnp.float32) + low_up
            target = rest + delta_v[:, part].astype(jnp.float32)
            gap = states - target
            adapted[:, part] = states.astype(jnp.bfloat16)
            squares = on_up(up, up)
            low_sums = 0
            for low_part in split3(squares):
                for j in range(3):
                    low_sums += jnp.dot(
                        low_parts[:, j * rank : (j + 1) * rank],
                        low_part,
                        preferred_element_type=jnp.float32,
                    )
            sums_ref[:, :rank] += on_up(res[:, part], up) + on_up(attn[:, part], up) + low_sums
            for k, product in enumerate((states * states, states * target, gap * gap)):
                sums_ref[:, rank + k : rank + k + 1] += jnp.sum(product, axis=1, keepdims=True)

        adapted_out = pltpu.make_async_copy(adapted, adapted_ref.at[:, here], out_sem.at[1])
        adapted_out.start()
        sums_out[...] = sums_ref[...].T[:24] if before else sums_ref[...]
        attn_out.wait()
        adapted_out.wait()

    anywhere = pl.BlockSpec(memory_space=pl.ANY)
    in_vmem = pl.BlockSpec(memory_space=pltpu.VMEM)
    operands = (*pieces, residual, delta, up_weight, low_rank, *(before or ()))
    return pl.pallas_call(
        kernel,
        out_shape=(
            pltpu.HBM((rows, cols), jnp.bfloat16),
            pltpu.HBM((rows, cols), jnp.bfloat16),
            jax.ShapeDtypeStruct((24, rows) if before else (rows, 128), jnp.float32),
        ),
        in_specs=[anywhere] * (count + 3)
        + [in_vmem]
        + ([anywhere, anywhere, in_vmem] if before else []),
        out_specs=(anywhere, anywhere, in_vmem),
        input_output_aliases={count + 4: 0, count + 5: 1} if before else {},
        scratch_shapes=[pltpu.VMEM((rows, width), jnp.bfloat16) for _ in range(4)]
        + [
            pltpu.VMEM((rank, width), jnp.bfloat16),
            pltpu.VMEM((rows, 128), jnp.float32),
            pltpu.SemaphoreType.DMA((count,)),
            pltpu.SemaphoreType.DMA((3,)),
            pltpu.SemaphoreType.DMA((2,)),
        ],
        compiler_params=pltpu.CompilerParams(vmem_limit_bytes=32 * 1024 * 1024),
        cost_estimate=pl.CostEstimate(
            flops=COST, bytes_accessed=1000, transcendentals=0
        ),
    )(*operands)


def line_grads(sums, came, early_sums, low_t, weights, context, residual, delta, attn, up_weight):
    rows, cols = residual.shape
    rank = up_weight.shape[0]
    width = cols // INNER

    def kernel(*refs):
        sums_ref, came_ref, early_ref, low_ref, weight_ref = refs[:5]
        sources = refs[5:10]
        keep_ref, give_ref = refs[10:12]
        buffers, sem = refs[12:17], refs[17]
        place = lax.axis_index("dp") % INNER

        def loads(j):
            here = pl.ds(pl.multiple_of((place ^ j) * width, width), width)
            return [
                pltpu.make_async_copy(source.at[:, here], buffer.at[j % 2], sem.at[j % 2, i])
                for i, (source, buffer) in enumerate(zip(sources, buffers))
            ]

        for copy in loads(0):
            copy.start()
        sums = sums_ref[...] + came_ref[...]
        early = early_ref[...]
        low = low_ref[...]
        states_up, target_up = sums[:rank], early[:rank]
        norm_h = jnp.sqrt(sums[rank : rank + 1] + NORM_EPS)
        norm_g = jnp.sqrt(early[rank : rank + 1] + NORM_EPS)
        cosine = sums[rank + 1 : rank + 2] / (norm_h * norm_g)
        distance = jnp.sqrt(sums[rank + 2 : rank + 3] + NORM_EPS)
        weight_harm = weight_ref[0:1]
        weight_keep = weight_ref[1:2] / distance
        on_target = weight_harm / (norm_h * norm_g) - weight_keep
        on_states = weight_keep - weight_harm * cosine / (norm_h * norm_h)

        def stacked(value):
            return jnp.concatenate(split3(value), axis=0)

        def total(parts, values):
            product = jnp.dot(parts, values, preferred_element_type=jnp.float32)
            return product[:rank] + product[rank : 2 * rank] + product[2 * rank :]

        twice = ADAPTER_SCALE * low
        for_context = stacked(ADAPTER_SCALE * (on_target * target_up + on_states * states_up))
        for_rest = stacked(twice * (on_target + on_states))
        for_delta = stacked(twice * on_target)
        for_attn = stacked(twice * on_states)
        mixed = lax.dot_general(
            twice * on_states,
            twice,
            (((1,), (1,)), ((), ())),
            precision=HIGHEST,
            preferred_element_type=jnp.float32,
        )
        for_up = stacked(mixed)
        for j in range(INNER):
            if j + 1 < INNER:
                for copy in loads(j + 1):
                    copy.start()
            for copy in loads(j):
                copy.wait()
            ctx, rest, delta_v, attn_v, up = (buffer.at[j % 2] for buffer in buffers)
            out = give_ref if j % 2 else keep_ref
            out[j // 2, :rank, :] = total(for_context, ctx[...])
            out[j // 2, rank:, :] = (
                total(for_rest, rest[...])
                + total(for_delta, delta_v[...])
                + total(for_attn, attn_v[...])
                + total(for_up, up[...])
            )

    anywhere = pl.BlockSpec(memory_space=pl.ANY)
    in_vmem = pl.BlockSpec(memory_space=pltpu.VMEM)
    return pl.pallas_call(
        kernel,
        out_shape=[jax.ShapeDtypeStruct((2, 2 * rank, width), jnp.float32)] * 2,
        in_specs=[in_vmem] * 5 + [anywhere] * 5,
        out_specs=[in_vmem] * 2,
        scratch_shapes=[pltpu.VMEM((2, rows, width), jnp.bfloat16) for _ in range(4)]
        + [
            pltpu.VMEM((2, rank, width), jnp.bfloat16),
            pltpu.SemaphoreType.DMA((2, 5)),
        ],
        compiler_params=pltpu.CompilerParams(vmem_limit_bytes=56 * 1024 * 1024),
        cost_estimate=pl.CostEstimate(
            flops=COST, bytes_accessed=1000, transcendentals=0
        ),
    )(sums, came, early_sums, low_t, weights, context, residual, delta, attn, up_weight)


def general_attention(context, output_weight):
    partial = dot_bf16(context, lax.all_gather(output_weight, "dp", axis=1, tiled=True))
    return lax.psum_scatter(partial, "tensor", scatter_dimension=1, tiled=True)


def line_sum_grads(keep, give):
    place = lax.axis_index("dp") % INNER
    rank = keep.shape[1] // 2
    keep = keep + send(give, inner_swap(1))
    both = keep[0] + send(keep[1], inner_swap(2))
    for bits in (1, 2):
        both = both + send(both, lambda z, q, t: (z ^ bits, q, t))
    grad_b = both[rank:]
    other = send(grad_b, other_tensor)
    across = send(both, inner_swap(2))
    across_other = send(grad_b, lambda z, q, t: (z, q ^ 2, 1 - t))

    def joined(bits, mine, got):
        upper = (place & bits) != 0
        return jnp.concatenate(
            [jnp.where(upper, got, mine), jnp.where(upper, mine, got)], axis=1
        )

    mine = jnp.stack([jnp.concatenate([both, other]), jnp.concatenate([across, across_other])])
    got = send(mine, inner_swap(1))
    mine = joined(2, joined(1, mine[0], got[0]), joined(1, mine[1], got[1]))
    grad_a = mine[:rank].T
    kept, other = mine[rank : 2 * rank], mine[2 * rank :]
    first = lax.axis_index("tensor") == 0
    grad_b = jnp.concatenate(
        [jnp.where(first, kept, other), jnp.where(first, other, kept)], axis=1
    )
    return grad_a, grad_b


def general_sum_grads(grad_a_t, grad_b):
    grad_a_t, grad_b = lax.psum((grad_a_t, grad_b), "dp")
    return grad_a_t.T, lax.all_gather(grad_b, "tensor", axis=1, tiled=True)


def solution(mesh):
    line = mesh.shape["dp"] == LAYERS * INNER and mesh.shape["tensor"] == 2

    def sum_tensor(value):
        if line:
            return value + send(value, other_tensor)
        return lax.psum(value, "tensor")

    def local(
        context,
        output_weight,
        adapter_down_weight,
        adapter_up_weight,
        residual,
        frozen_residual_delta,
        harmful_count,
        retain_count,
    ):
        seq_len = context.shape[0]
        tensor_rank = lax.axis_index("tensor")
        data_rank = lax.axis_index("dp")
        harm_total = jnp.sum(harmful_count).astype(jnp.float32)
        keep_total = jnp.sum(retain_count).astype(jnp.float32)
        harm_here = harmful_count[data_rank]
        keep_here = retain_count[data_rank]
        col_count = residual.shape[1]

        low_rank_t = sum_tensor(
            lax.dot_general(
                adapter_down_weight,
                context,
                (((0,), (1,)), ((), ())),
                preferred_element_type=jnp.float32,
            )
        )
        up_narrow = lax.dynamic_slice_in_dim(
            adapter_up_weight, tensor_rank * col_count, col_count, 1
        )
        up_columns = up_narrow.astype(jnp.float32)
        target = residual.astype(jnp.float32) + frozen_residual_delta.astype(jnp.float32)

        def on_up(values):
            return lax.dot_general(
                up_columns, values, (((1,), (1,)), ((), ())), precision=HIGHEST
            )

        rank = up_columns.shape[0]
        early_sums = sum_tensor(
            jnp.concatenate([on_up(target), jnp.sum(target * target, axis=1)[None]], axis=0)
        )
        target_up, sq_target = early_sums[:rank], early_sums[rank]
        positions = jnp.arange(seq_len, dtype=jnp.int32)
        harmful = (positions < harm_here).astype(jnp.float32)
        retained = (
            (positions >= harm_here) & (positions < harm_here + keep_here)
        ).astype(jnp.float32)
        weight_harm = REROUTE_WEIGHT / harm_total * harmful
        weight_keep = RETAIN_WEIGHT / keep_total * retained
        if line:
            weights = jnp.stack([weight_harm, weight_keep])
            constant = (residual, frozen_residual_delta, up_narrow, low_rank_t)
            pieces, half_done = line_pieces(
                context,
                output_weight,
                (low_rank_t, early_sums, weights),
                lambda first: half_states(False, first, *constant, None),
            )
            adapted, attn, sums = half_states(True, pieces, *constant, half_done)
            keep, give = line_grads(
                sums,
                send(sums, other_tensor),
                early_sums,
                low_rank_t,
                weights,
                context,
                residual,
                frozen_residual_delta,
                attn,
                up_narrow,
            )
            return adapted, *line_sum_grads(keep, give)
        low_up = ADAPTER_SCALE * lax.dot_general(
            low_rank_t, up_columns, (((0,), (0,)), ((), ())), precision=HIGHEST
        )
        attn = general_attention(context, output_weight).astype(jnp.float32)
        states = residual.astype(jnp.float32) + attn + low_up
        adapted = states.astype(jnp.bfloat16)
        gap = states - target
        products = [states * states, states * target, gap * gap]
        sums = jnp.stack([jnp.sum(product, axis=1) for product in products])
        sums = jnp.concatenate([on_up(states), sums], axis=0)
        shared = sum_tensor(sums)
        states_up = shared[:rank]
        sq_state, cross_term, gap_sq = (shared[rank + i] for i in range(3))

        norm_h = jnp.sqrt(sq_state + NORM_EPS)
        norm_g = jnp.sqrt(sq_target + NORM_EPS)
        cosine = cross_term / (norm_h * norm_g)
        distance = jnp.sqrt(gap_sq + NORM_EPS)
        weight_keep = weight_keep / distance
        on_target = weight_harm / (norm_h * norm_g) - weight_keep
        on_states = weight_keep - weight_harm * cosine / (norm_h * norm_h)

        cotangent = on_target[:, None] * target + on_states[:, None] * states
        low_cot_t = ADAPTER_SCALE * (on_target * target_up + on_states * states_up)
        grad_a_t = jnp.dot(low_cot_t, context.astype(jnp.float32), precision=HIGHEST)
        grad_b = ADAPTER_SCALE * jnp.dot(low_rank_t, cotangent, precision=HIGHEST)
        grad_a, grad_b = general_sum_grads(grad_a_t, grad_b)
        return adapted, grad_a, grad_b

    return jax.shard_map(
        local,
        mesh=mesh,
        in_specs=(
            P("dp", "tensor"),
            P("tensor", "dp"),
            P("tensor", None),
            P(),
            P("dp", "tensor"),
            P("dp", "tensor"),
            P(),
            P(),
        ),
        out_specs=(P("dp", "tensor"), P("tensor", None), P()),
        check_vma=False,
    )
```

```python
import jax
import jax.numpy as jnp
from jax import lax
from jax.experimental import pallas as pl
from jax.experimental.pallas import tpu as pltpu
from jax.sharding import PartitionSpec as P

ADAPTER_SCALE = 2.0
NORM_EPS = 1e-06
REROUTE_WEIGHT = 65536.0
RETAIN_WEIGHT = 1024.0
COST = 100_000_000
INNER = 4
LAYERS = 4
HIGHEST = lax.Precision.HIGHEST


def after(value, *earlier):
    return lax.optimization_barrier((value,) + earlier)[0]


def routes(step):
    pairs = []
    for z in range(LAYERS):
        for q in range(INNER):
            for t in range(2):
                to = step(z, q, t)
                if to is not None:
                    pairs.append(((z * INNER + q) * 2 + t, (to[0] * INNER + to[1]) * 2 + to[2]))
    return pairs


def send(value, step):
    return lax.ppermute(value, ("dp", "tensor"), routes(step))


def inward(z, q, t):
    return {0: (1, q, t), 3: (2, q, t)}.get(z)


def outward(z, q, t):
    return {1: (0, q, t), 2: (3, q, t)}.get(z)


def mid_swap(z, q, t):
    return {1: (2, q, t), 2: (1, q, t)}.get(z)


def inner_swap(bits, layers=range(LAYERS)):
    return lambda z, q, t: (z, q ^ bits, t) if z in layers else None


def other_tensor(z, q, t):
    return (z, q, 1 - t)


def keeps_near(z, t):
    return (t == 0) == (z < 2)


def exchange_but_lent(z, q, t):
    return None if z in (0, 3) and keeps_near(z, t) else (z, q, 1 - t)


def lend_straight(z, q, t):
    return None if keeps_near(z, t) else outward(z, q, t)


def lend_across(z, q, t):
    return outward(z, q, 1 - t) if keeps_near(z, t) else None


def dot_bf16(a, b):
    return jnp.dot(a, b, preferred_element_type=jnp.float32).astype(jnp.bfloat16)


def at_end_layer():
    layer = lax.axis_index("dp") // INNER
    return (layer == 0) | (layer == LAYERS - 1)


def products(*jobs, load=(), cost=COST):
    operands = []

    def index(array):
        for i, known in enumerate(operands):
            if known is array:
                return i
        operands.append(array)
        return len(operands) - 1

    plan = []
    layers = []
    for layer, weights, ends, _ in jobs:
        choices = [weights] if ends is None else [weights, ends]
        if index(layer) not in layers:
            layers.append(index(layer))
        plan.append(
            (
                index(layer),
                [[(index(w), start, n) for w, start, n in choice] for choice in choices],
            )
        )
    depth = jobs[0][0].shape[1]
    rows = jobs[0][0].shape[0] // INNER
    widths = [sum(n for _, _, n in choices[0]) for _, choices in plan]
    cuts = [job[3] for job in jobs]
    out_count = sum(len(cut) for cut in cuts)
    columns = max(len(choice) for _, choices in plan for choice in choices)
    loads = [index(layer) for layer in load]
    kept = len(loads)

    def kernel(*refs):
        inputs = refs[: len(operands)]
        held = refs[len(operands) : len(operands) + kept]
        outs = refs[len(operands) + kept : len(operands) + kept + out_count]
        w_buf, w_sem, a_sem = refs[len(operands) + kept + out_count :]
        ends = at_end_layer()
        place = lax.axis_index("dp") % INNER

        def piece(p):
            return pl.ds(pl.multiple_of((place ^ p) * rows, rows), rows)

        def row_copy(i, p):
            return pltpu.make_async_copy(
                inputs[loads[i]].at[piece(p)], held[i].at[piece(p)], a_sem.at[i, p]
            )

        def weight_copies(j, choice):
            at = 0
            for i, (k, start, n) in enumerate(plan[j][1][choice]):
                source = inputs[k]
                if source.shape[1] != n:
                    source = source.at[:, pl.ds(start, n)]
                yield pltpu.make_async_copy(
                    source, w_buf.at[j % 2, :, pl.ds(at, n)], w_sem.at[j % 2, i]
                )
                at += n

        def weights(j, action):
            if len(plan[j][1]) == 1:
                for copy in weight_copies(j, 0):
                    action(copy)
                return

            @pl.when(ends)
            def _():
                for copy in weight_copies(j, 1):
                    action(copy)

            @pl.when(jnp.logical_not(ends))
            def _():
                for copy in weight_copies(j, 0):
                    action(copy)

        def begin(copy):
            copy.start()

        def finish(copy):
            copy.wait()

        weights(0, begin)
        for i in range(kept):
            for p in range(INNER):
                row_copy(i, p).start()
        out = 0
        for j, (layer, _) in enumerate(plan):
            weights(j, finish)
            if j + 1 < len(plan):
                weights(j + 1, begin)
            source = inputs[layer]
            if layer in loads:
                source = held[loads.index(layer)]
                for p in range(INNER):
                    row_copy(loads.index(layer), p).wait()
            for p in range(INNER):
                result = jnp.dot(
                    source[piece(p), :],
                    w_buf[j % 2, :, : widths[j]],
                    preferred_element_type=jnp.float32,
                ).astype(jnp.bfloat16)
                at = 0
                for k, width in enumerate(cuts[j]):
                    outs[out + k][p * rows : (p + 1) * rows, :] = result[:, at : at + width]
                    at += width
            out += len(cuts[j])

    in_vmem = pl.BlockSpec(memory_space=pltpu.VMEM)
    in_specs = [pl.BlockSpec(memory_space=pl.ANY)] * len(operands)
    for i, operand in enumerate(operands):
        place_in = pltpu.VMEM if i in layers and i not in loads else pltpu.HBM
        in_specs[i] = pl.BlockSpec(memory_space=place_in)
        operands[i] = pltpu.with_memory_space_constraint(operand, place_in)
    resident = [pltpu.VMEM((INNER * rows, depth), jnp.bfloat16)] * kept
    return pl.pallas_call(
        kernel,
        out_shape=resident
        + [
            jax.ShapeDtypeStruct((INNER * rows, width), jnp.bfloat16)
            for cut in cuts
            for width in cut
        ],
        in_specs=in_specs,
        out_specs=[in_vmem] * (out_count + kept),
        scratch_shapes=[
            pltpu.VMEM((2, depth, max(widths)), jnp.bfloat16),
            pltpu.SemaphoreType.DMA((2, columns)),
            pltpu.SemaphoreType.DMA((max(kept, 1), INNER)),
        ],
        compiler_params=pltpu.CompilerParams(vmem_limit_bytes=22 * 1024 * 1024),
        cost_estimate=pl.CostEstimate(
            flops=cost, bytes_accessed=1000, transcendentals=0
        ),
    )(*operands)


def add_bf16(a, b):
    return (a.astype(jnp.float32) + b.astype(jnp.float32)).astype(jnp.bfloat16)


def to_owners(block, rows):
    pieces = [block[:rows]]
    for bits in range(1, INNER):
        pieces.append(send(block[bits * rows : (bits + 1) * rows], inner_swap(bits)))
    return pieces


def layer_rows(rows):
    groups = [[z * INNER + q for q in range(INNER)] for z in range(LAYERS)]
    return lax.all_gather(rows, "dp", axis_index_groups=groups, axis=0, tiled=True)


def line_pieces(context, output_weight, due, add_states):
    rows = context.shape[0]
    half = output_weight.shape[1] // 2
    quarter = half // 2
    block = 2 * half
    layer = lax.axis_index("dp") // INNER
    at_end = at_end_layer()
    near_half = (lax.axis_index("tensor") == 0) == (layer < 2)
    takes_lent = at_end & jnp.logical_not(near_half)

    def pin(*values):
        return lax.optimization_barrier(values)

    def swap(near_part, far_part, step=other_tensor):
        kept = jnp.where(near_half, near_part, far_part)
        return kept, send(jnp.where(near_half, far_part, near_part), step)

    def lend(part):
        return send(part, lend_straight), send(part, lend_across)

    def total(kept, came, lent):
        return add_bf16(
            jnp.where(takes_lent, lent[0], kept), jnp.where(takes_lent, lent[1], came)
        )

    def narrow(arrays):
        return [(array, 0, quarter) for array in arrays]

    quarters = [output_weight[:, i * quarter : (i + 1) * quarter] for i in range(4)]
    guest = send(context, inward)
    middle = send(output_weight, mid_swap)
    outer_end = send(output_weight, outward)
    own = layer_rows(context)
    near = [send(after(quarters[0], guest, due), inward)]
    guest, near[0], middle, outer_end, quarters, near_half, takes_lent = pin(
        guest, near[0], middle, outer_end, quarters, near_half, takes_lent
    )
    guests = layer_rows(guest)
    mid_quarters = [middle[:, i * quarter : (i + 1) * quarter] for i in range(2)]
    mid_a, mid_b = [(middle, 0, half)], [(middle, half, half)]

    far = [send(near[0], mid_swap)]
    near.append(send(quarters[1], inward))
    mid_end = [send(mid_quarters[0], outward)]
    resident, *part_own = products(
        (own, [(output_weight, 0, block)], None, [quarter, quarter, half]), load=(own,)
    )
    far[0], near[1], mid_end[0], resident, part_own, quarters, mid_quarters = pin(
        far[0], near[1], mid_end[0], resident, part_own, quarters, mid_quarters
    )

    far.append(send(near[1], mid_swap))
    near.append(send(quarters[2], inward))
    mid_end.append(send(mid_quarters[1], outward))
    part_mid_b, part_outer_a, part_mid_0 = products(
        (resident, mid_b + narrow(near[:2]), mid_b + [(outer_end, 0, half)], [half, half]),
        (resident, [(middle, 0, quarter)], narrow(mid_end[:1]), [quarter]),
    )
    far[1], near[2], mid_end[1], part_mid_b, part_outer_a, part_mid_0, quarters = pin(
        far[1], near[2], mid_end[1], part_mid_b, part_outer_a, part_mid_0, quarters
    )

    far.append(send(near[2], mid_swap))
    near.append(send(quarters[3], inward))
    swap_0 = swap(part_own[0], part_mid_0)
    (part_mid_1,) = products(
        (resident, [(middle, quarter, quarter)], narrow(mid_end[1:]), [quarter]),
        cost=100 * COST,
    )
    swap_1 = swap(part_own[1], part_mid_1)
    guests = after(guests, part_mid_1, swap_0)
    guests, lent_b = products((guests, mid_b, None, [half]), load=(guests,))
    far[2], near[3], swap_0, swap_1, guests, lent_b, part_own, part_mid_b = pin(
        far[2], near[3], swap_0, swap_1, guests, lent_b, part_own, part_mid_b
    )

    far.append(send(near[3], mid_swap))
    lent_b = lend(lent_b)
    swap_b = swap(part_own[2], part_mid_b, exchange_but_lent)
    own, lent_c, part_far_a, part_outer_b = products(
        (guests, narrow(far[:2]), None, [half]),
        (
            own,
            narrow(far[:2]) + narrow(near[2:]),
            narrow(far[:2]) + [(outer_end, half, half)],
            [half, half],
        ),
        load=(own,),
    )
    far[3], lent_b, swap_b, own, lent_c, part_far_a, part_outer_b = pin(
        far[3], lent_b, swap_b, own, lent_c, part_far_a, part_outer_b
    )

    lent_c = lend(lent_c)
    swap_c = swap(part_outer_a, part_far_a, exchange_but_lent)
    first = [add_bf16(*swap_0), add_bf16(*swap_1), total(*swap_b, lent_b)]
    first = to_owners(jnp.concatenate(first, axis=1), rows)
    lent_d, part_far_b = products(
        (guests, narrow(far[2:]), None, [half]), (own, narrow(far[2:]), None, [half])
    )
    lent_c, swap_c, first, lent_d, part_far_b = pin(lent_c, swap_c, first, lent_d, part_far_b)

    lent_d = lend(lent_d)
    swap_d = swap(part_outer_b, part_far_b, exchange_but_lent)
    second = to_owners(total(*swap_c, lent_c), rows)
    done = add_states(False, 0, first, None, False)
    lent_d, swap_d, second, done = pin(lent_d, swap_d, second, done)

    third = to_owners(total(*swap_d, lent_d), rows)
    done = add_states(True, 0, second, done, False)
    third, done = pin(third, done)
    return add_states(True, half, third, done, True)


def split3(value):
    parts = []
    for _ in range(3):
        parts.append(value.astype(jnp.bfloat16))
        value = value - parts[-1].astype(jnp.float32)
    return parts


def part_states(second, start, pieces, residual, delta, up_weight, low_rank, before, last):
    rows, cols = residual.shape
    rank = up_weight.shape[0]
    block = cols // (2 * INNER)
    width = pieces[0].shape[1]

    def kernel(*refs):
        piece_refs = refs[:INNER]
        res_ref, delta_ref, up_ref, low_ref = refs[INNER : INNER + 4]
        prior_ref = refs[INNER + 6] if before else None
        adapted_ref, attn_ref, sums_out = refs[-12:-9]
        attn, res, delta_v, adapted, up_v, sums_ref, sem, in_sem, out_sem = refs[-9:]
        data_rank = lax.axis_index("dp")
        layer = data_rank // INNER
        place = data_rank % INNER
        low = layer < 2
        near_half = (lax.axis_index("tensor") == 0) == low
        first = jnp.where(near_half, layer % 2, jnp.where(low, 0, 1))
        side = 1 - first if second else first

        def window(ref, j):
            at = (side * INNER + (place ^ j)) * block + start
            return ref.at[:, pl.ds(pl.multiple_of(at, width), width)]

        def part(ref, j):
            return ref.at[:, pl.ds(j * width, width)]

        loads = []
        for j in range(INNER):
            for i, (source, to) in enumerate(((res_ref, res), (delta_ref, delta_v), (up_ref, up_v))):
                loads.append(
                    pltpu.make_async_copy(window(source, j), part(to, j), in_sem.at[i, j])
                )
            loads.append(pltpu.make_async_copy(piece_refs[j], part(attn, j), sem.at[j]))
        for copy in loads:
            copy.start()
        low_parts = jnp.concatenate(split3(ADAPTER_SCALE * low_ref[...].T), axis=1)
        if before:
            sums_ref[...] = prior_ref[...]
        else:
            sums_ref[...] = jnp.zeros_like(sums_ref)
        for copy in loads:
            copy.wait()
        stores = [
            pltpu.make_async_copy(part(attn, j), window(attn_ref, j), out_sem.at[0, j])
            for j in range(INNER)
        ]
        for copy in stores:
            copy.start()

        def on_up(values, up):
            return lax.dot_general(
                values, up, (((1,), (1,)), ((), ())), preferred_element_type=jnp.float32
            )

        @pl.loop(0, INNER)
        def _(j):
            here = pl.ds(pl.multiple_of(j * width, width), width)
            up = up_v[:, here]
            low_up = jnp.dot(
                low_parts,
                jnp.concatenate([up] * 3, axis=0),
                preferred_element_type=jnp.float32,
            )
            rest = res[:, here].astype(jnp.float32)
            states = rest + attn[:, here].astype(jnp.float32) + low_up
            target = rest + delta_v[:, here].astype(jnp.float32)
            gap = states - target
            adapted[:, here] = states.astype(jnp.bfloat16)
            squares = on_up(up, up)
            low_sums = 0
            for low_part in split3(squares):
                for k in range(3):
                    low_sums += jnp.dot(
                        low_parts[:, k * rank : (k + 1) * rank],
                        low_part,
                        preferred_element_type=jnp.float32,
                    )
            sums_ref[:, :rank] += on_up(res[:, here], up) + on_up(attn[:, here], up) + low_sums
            for k, product in enumerate((states * states, states * target, gap * gap)):
                sums_ref[:, rank + k : rank + k + 1] += jnp.sum(product, axis=1, keepdims=True)

        for j in range(INNER):
            stores.append(
                pltpu.make_async_copy(part(adapted, j), window(adapted_ref, j), out_sem.at[1, j])
            )
            stores[-1].start()
        sums_out[...] = sums_ref[...].T[:24] if last else sums_ref[...]
        for copy in stores:
            copy.wait()

    anywhere = pl.BlockSpec(memory_space=pl.ANY)
    in_vmem = pl.BlockSpec(memory_space=pltpu.VMEM)
    operands = (*pieces, residual, delta, up_weight, low_rank, *(before or ()))
    return pl.pallas_call(
        kernel,
        out_shape=(
            pltpu.HBM((rows, cols), jnp.bfloat16),
            pltpu.HBM((rows, cols), jnp.bfloat16),
            jax.ShapeDtypeStruct((24, rows) if last else (rows, 128), jnp.float32),
        ),
        in_specs=[anywhere] * (INNER + 3)
        + [in_vmem]
        + ([anywhere, anywhere, in_vmem] if before else []),
        out_specs=(anywhere, anywhere, in_vmem),
        input_output_aliases={INNER + 4: 0, INNER + 5: 1} if before else {},
        scratch_shapes=[pltpu.VMEM((rows, INNER * width), jnp.bfloat16) for _ in range(4)]
        + [
            pltpu.VMEM((rank, INNER * width), jnp.bfloat16),
            pltpu.VMEM((rows, 128), jnp.float32),
            pltpu.SemaphoreType.DMA((INNER,)),
            pltpu.SemaphoreType.DMA((3, INNER)),
            pltpu.SemaphoreType.DMA((2, INNER)),
        ],
        compiler_params=pltpu.CompilerParams(vmem_limit_bytes=32 * 1024 * 1024),
        cost_estimate=pl.CostEstimate(flops=COST, bytes_accessed=1000, transcendentals=0),
    )(*operands)


def hold(*arrays):
    count = len(arrays)

    def kernel(*refs):
        copies = [
            pltpu.make_async_copy(refs[i], refs[count + i], refs[-1].at[i]) for i in range(count)
        ]
        for copy in copies:
            copy.start()
        for copy in copies:
            copy.wait()

    arrays = [pltpu.with_memory_space_constraint(array, pltpu.HBM) for array in arrays]
    return pl.pallas_call(
        kernel,
        out_shape=[pltpu.VMEM(array.shape, array.dtype) for array in arrays],
        in_specs=[pl.BlockSpec(memory_space=pltpu.HBM)] * count,
        out_specs=[pl.BlockSpec(memory_space=pltpu.VMEM)] * count,
        scratch_shapes=[pltpu.SemaphoreType.DMA((count,))],
        compiler_params=pltpu.CompilerParams(vmem_limit_bytes=16 * 1024 * 1024),
        cost_estimate=pl.CostEstimate(flops=100 * COST, bytes_accessed=1000, transcendentals=0),
    )(*arrays)


def line_grads(sums, came, early_sums, low_t, weights, context, residual, delta, attn, up_weight):
    rows, cols = residual.shape
    rank = up_weight.shape[0]
    width = cols // INNER

    def kernel(*refs):
        sums_ref, came_ref, early_ref, low_ref, weight_ref = refs[:5]
        ctx_ref, res_ref, delta_ref, attn_in, up_in = refs[5:10]
        keep_ref, give_ref, attn_ref, up_ref, sem = refs[10:]
        place = lax.axis_index("dp") % INNER
        loads = [
            pltpu.make_async_copy(attn_in, attn_ref, sem.at[0]),
            pltpu.make_async_copy(up_in, up_ref, sem.at[1]),
        ]
        for copy in loads:
            copy.start()
        sums = sums_ref[...] + came_ref[...]
        early = early_ref[...]
        low = low_ref[...]
        states_up, target_up = sums[:rank], early[:rank]
        norm_h = jnp.sqrt(sums[rank : rank + 1] + NORM_EPS)
        norm_g = jnp.sqrt(early[rank : rank + 1] + NORM_EPS)
        cosine = sums[rank + 1 : rank + 2] / (norm_h * norm_g)
        distance = jnp.sqrt(sums[rank + 2 : rank + 3] + NORM_EPS)
        weight_harm = weight_ref[0:1]
        weight_keep = weight_ref[1:2] / distance
        on_target = weight_harm / (norm_h * norm_g) - weight_keep
        on_states = weight_keep - weight_harm * cosine / (norm_h * norm_h)

        def stacked(value):
            return jnp.concatenate(split3(value), axis=0)

        def total(parts, values):
            product = jnp.dot(parts, values, preferred_element_type=jnp.float32)
            return product[:rank] + product[rank : 2 * rank] + product[2 * rank :]

        twice = ADAPTER_SCALE * low
        for_context = stacked(ADAPTER_SCALE * (on_target * target_up + on_states * states_up))
        for_rest = stacked(twice * (on_target + on_states))
        for_delta = stacked(twice * on_target)
        for_attn = stacked(twice * on_states)
        mixed = lax.dot_general(
            twice * on_states,
            twice,
            (((1,), (1,)), ((), ())),
            precision=HIGHEST,
            preferred_element_type=jnp.float32,
        )
        for_up = stacked(mixed)
        for j in range(INNER):
            here = pl.ds(pl.multiple_of((place ^ j) * width, width), width)
            out = give_ref if j % 2 else keep_ref
            out[j // 2, :rank, :] = total(for_context, ctx_ref[:, here])
            part = total(for_rest, res_ref[:, here]) + total(for_delta, delta_ref[:, here])
            if j == 0:
                for copy in loads:
                    copy.wait()
            part += total(for_attn, attn_ref[:, here]) + total(for_up, up_ref[:, here])
            out[j // 2, rank:, :] = part

    anywhere = pl.BlockSpec(memory_space=pl.ANY)
    in_vmem = pl.BlockSpec(memory_space=pltpu.VMEM)
    return pl.pallas_call(
        kernel,
        out_shape=[jax.ShapeDtypeStruct((2, 2 * rank, width), jnp.float32)] * 2,
        in_specs=[in_vmem] * 8 + [anywhere] * 2,
        out_specs=[in_vmem] * 2,
        scratch_shapes=[
            pltpu.VMEM((rows, cols), jnp.bfloat16),
            pltpu.VMEM((rank, cols), jnp.bfloat16),
            pltpu.SemaphoreType.DMA((2,)),
        ],
        compiler_params=pltpu.CompilerParams(vmem_limit_bytes=24 * 1024 * 1024),
        cost_estimate=pl.CostEstimate(flops=COST, bytes_accessed=1000, transcendentals=0),
    )(
        sums, came, early_sums, low_t, weights,
        *(pltpu.with_memory_space_constraint(x, pltpu.VMEM) for x in (context, residual, delta)),
        attn, up_weight,
    )


def general_attention(context, output_weight):
    partial = dot_bf16(context, lax.all_gather(output_weight, "dp", axis=1, tiled=True))
    return lax.psum_scatter(partial, "tensor", scatter_dimension=1, tiled=True)


def line_sum_grads(keep, give):
    place = lax.axis_index("dp") % INNER
    rank = keep.shape[1] // 2
    keep = keep + send(give, inner_swap(1))
    both = keep[0] + send(keep[1], inner_swap(2))
    for bits in (1, 2):
        both = both + send(both, lambda z, q, t: (z ^ bits, q, t))
    grad_b = both[rank:]
    other = send(grad_b, other_tensor)
    across = send(both, inner_swap(2))
    across_other = send(grad_b, lambda z, q, t: (z, q ^ 2, 1 - t))

    def joined(bits, mine, got):
        upper = (place & bits) != 0
        return jnp.concatenate(
            [jnp.where(upper, got, mine), jnp.where(upper, mine, got)], axis=1
        )

    mine = jnp.stack([jnp.concatenate([both, other]), jnp.concatenate([across, across_other])])
    got = send(mine, inner_swap(1))
    mine = joined(2, joined(1, mine[0], got[0]), joined(1, mine[1], got[1]))
    grad_a = mine[:rank].T
    kept, other = mine[rank : 2 * rank], mine[2 * rank :]
    first = lax.axis_index("tensor") == 0
    grad_b = jnp.concatenate(
        [jnp.where(first, kept, other), jnp.where(first, other, kept)], axis=1
    )
    return grad_a, grad_b


def general_sum_grads(grad_a_t, grad_b):
    grad_a_t, grad_b = lax.psum((grad_a_t, grad_b), "dp")
    return grad_a_t.T, lax.all_gather(grad_b, "tensor", axis=1, tiled=True)


def solution(mesh):
    line = mesh.shape["dp"] == LAYERS * INNER and mesh.shape["tensor"] == 2

    def sum_tensor(value):
        if line:
            return value + send(value, other_tensor)
        return lax.psum(value, "tensor")

    def local(
        context,
        output_weight,
        adapter_down_weight,
        adapter_up_weight,
        residual,
        frozen_residual_delta,
        harmful_count,
        retain_count,
    ):
        seq_len = context.shape[0]
        tensor_rank = lax.axis_index("tensor")
        data_rank = lax.axis_index("dp")
        harm_total = jnp.sum(harmful_count).astype(jnp.float32)
        keep_total = jnp.sum(retain_count).astype(jnp.float32)
        harm_here = harmful_count[data_rank]
        keep_here = retain_count[data_rank]
        col_count = residual.shape[1]

        low_rank_t = sum_tensor(
            lax.dot_general(
                adapter_down_weight,
                context,
                (((0,), (1,)), ((), ())),
                preferred_element_type=jnp.float32,
            )
        )
        up_narrow = lax.dynamic_slice_in_dim(
            adapter_up_weight, tensor_rank * col_count, col_count, 1
        )
        up_columns = up_narrow.astype(jnp.float32)
        target = residual.astype(jnp.float32) + frozen_residual_delta.astype(jnp.float32)

        def on_up(values):
            return lax.dot_general(
                up_columns, values, (((1,), (1,)), ((), ())), precision=HIGHEST
            )

        rank = up_columns.shape[0]
        early_sums = sum_tensor(
            jnp.concatenate([on_up(target), jnp.sum(target * target, axis=1)[None]], axis=0)
        )
        target_up, sq_target = early_sums[:rank], early_sums[rank]
        positions = jnp.arange(seq_len, dtype=jnp.int32)
        harmful = (positions < harm_here).astype(jnp.float32)
        retained = (
            (positions >= harm_here) & (positions < harm_here + keep_here)
        ).astype(jnp.float32)
        weight_harm = REROUTE_WEIGHT / harm_total * harmful
        weight_keep = RETAIN_WEIGHT / keep_total * retained
        if line:
            weights = jnp.stack([weight_harm, weight_keep])
            constant = (residual, frozen_residual_delta, up_narrow, low_rank_t)
            adapted, attn, sums = line_pieces(
                context,
                output_weight,
                (low_rank_t, early_sums, weights),
                lambda second, start, pieces, before, last: part_states(
                    second, start, pieces, *constant, before, last
                ),
            )
            held = hold(*lax.optimization_barrier((context, residual, frozen_residual_delta, sums))[:3])
            keep, give = line_grads(
                sums,
                send(sums, other_tensor),
                early_sums,
                low_rank_t,
                weights,
                *held,
                attn,
                up_narrow,
            )
            return adapted, *line_sum_grads(keep, give)
        low_up = ADAPTER_SCALE * lax.dot_general(
            low_rank_t, up_columns, (((0,), (0,)), ((), ())), precision=HIGHEST
        )
        attn = general_attention(context, output_weight).astype(jnp.float32)
        states = residual.astype(jnp.float32) + attn + low_up
        adapted = states.astype(jnp.bfloat16)
        gap = states - target
        products = [states * states, states * target, gap * gap]
        sums = jnp.stack([jnp.sum(product, axis=1) for product in products])
        sums = jnp.concatenate([on_up(states), sums], axis=0)
        shared = sum_tensor(sums)
        states_up = shared[:rank]
        sq_state, cross_term, gap_sq = (shared[rank + i] for i in range(3))

        norm_h = jnp.sqrt(sq_state + NORM_EPS)
        norm_g = jnp.sqrt(sq_target + NORM_EPS)
        cosine = cross_term / (norm_h * norm_g)
        distance = jnp.sqrt(gap_sq + NORM_EPS)
        weight_keep = weight_keep / distance
        on_target = weight_harm / (norm_h * norm_g) - weight_keep
        on_states = weight_keep - weight_harm * cosine / (norm_h * norm_h)

        cotangent = on_target[:, None] * target + on_states[:, None] * states
        low_cot_t = ADAPTER_SCALE * (on_target * target_up + on_states * states_up)
        grad_a_t = jnp.dot(low_cot_t, context.astype(jnp.float32), precision=HIGHEST)
        grad_b = ADAPTER_SCALE * jnp.dot(low_rank_t, cotangent, precision=HIGHEST)
        grad_a, grad_b = general_sum_grads(grad_a_t, grad_b)
        return adapted, grad_a, grad_b

    return jax.shard_map(
        local,
        mesh=mesh,
        in_specs=(
            P("dp", "tensor"),
            P("tensor", "dp"),
            P("tensor", None),
            P(),
            P("dp", "tensor"),
            P("dp", "tensor"),
            P(),
            P(),
        ),
        out_specs=(P("dp", "tensor"), P("tensor", None), P()),
        check_vma=False,
    )
```

```python
import functools

import jax
import jax.numpy as jnp
from jax import lax
from jax.experimental import pallas as pl
from jax.experimental.pallas import tpu as pltpu
from jax.sharding import PartitionSpec as P

ADAPTER_SCALE = 2.0
NORM_EPS = 1e-06
REROUTE_WEIGHT = 65536.0
RETAIN_WEIGHT = 1024.0
COST = 100_000_000
INNER = 4
LAYERS = 4
HIGHEST = lax.Precision.HIGHEST


def after(value, *earlier):
    return lax.optimization_barrier((value,) + earlier)[0]


def routes(step):
    pairs = []
    for z in range(LAYERS):
        for q in range(INNER):
            for t in range(2):
                to = step(z, q, t)
                if to is not None:
                    pairs.append(((z * INNER + q) * 2 + t, (to[0] * INNER + to[1]) * 2 + to[2]))
    return pairs


def send(value, step):
    return lax.ppermute(value, ("dp", "tensor"), routes(step))


def inward(z, q, t):
    return {0: (1, q, t), 3: (2, q, t)}.get(z)


def outward(z, q, t):
    return {1: (0, q, t), 2: (3, q, t)}.get(z)


def mid_swap(z, q, t):
    return {1: (2, q, t), 2: (1, q, t)}.get(z)


def inner_swap(bits, layers=range(LAYERS)):
    return lambda z, q, t: (z, q ^ bits, t) if z in layers else None


def other_tensor(z, q, t):
    return (z, q, 1 - t)


def keeps_near(z, t):
    return (t == 0) == (z < 2)


def exchange_but_lent(z, q, t):
    return None if z in (0, 3) and keeps_near(z, t) else (z, q, 1 - t)


def lend_straight(z, q, t):
    return None if keeps_near(z, t) else outward(z, q, t)


def lend_across(z, q, t):
    return outward(z, q, 1 - t) if keeps_near(z, t) else None


def dot_bf16(a, b):
    return jnp.dot(a, b, preferred_element_type=jnp.float32).astype(jnp.bfloat16)


def at_end_layer():
    layer = lax.axis_index("dp") // INNER
    return (layer == 0) | (layer == LAYERS - 1)


def products(*jobs, load=(), mids_only=(), cost=COST):
    operands = []

    def index(array):
        for i, known in enumerate(operands):
            if known is array:
                return i
        operands.append(array)
        return len(operands) - 1

    plan = []
    layers = []
    for layer, weights, ends, _ in jobs:
        choices = [weights] if ends is None else [weights, ends]
        if index(layer) not in layers:
            layers.append(index(layer))
        plan.append(
            (
                index(layer),
                [[(index(w), start, n) for w, start, n in choice] for choice in choices],
            )
        )
    depth = jobs[0][0].shape[1]
    rows = jobs[0][0].shape[0] // INNER
    widths = [sum(n for _, _, n in choices[0]) for _, choices in plan]
    cuts = [job[3] for job in jobs]
    out_count = sum(len(cut) for cut in cuts)
    columns = max(len(choice) for _, choices in plan for choice in choices)
    loads = [index(layer) for layer in load]
    kept = len(loads)

    def kernel(*refs):
        inputs = refs[: len(operands)]
        held = refs[len(operands) : len(operands) + kept]
        outs = refs[len(operands) + kept : len(operands) + kept + out_count]
        w_buf, w_sem, a_sem = refs[len(operands) + kept + out_count :]
        ends = at_end_layer()
        place = lax.axis_index("dp") % INNER

        def piece(p):
            return pl.ds(pl.multiple_of((place ^ p) * rows, rows), rows)

        def row_copy(i, p):
            return pltpu.make_async_copy(
                inputs[loads[i]].at[piece(p)], held[i].at[piece(p)], a_sem.at[i, p]
            )

        def weight_copies(j, choice):
            at = 0
            for i, (k, start, n) in enumerate(plan[j][1][choice]):
                source = inputs[k]
                if source.shape[1] != n:
                    source = source.at[:, pl.ds(start, n)]
                yield pltpu.make_async_copy(
                    source, w_buf.at[j % 2, :, pl.ds(at, n)], w_sem.at[j % 2, i]
                )
                at += n

        def weights(j, action):
            def first_choice():
                for copy in weight_copies(j, 0):
                    action(copy)

            if len(plan[j][1]) == 1:
                unless_left_out(j, first_choice)
                return

            @pl.when(ends)
            def _():
                for copy in weight_copies(j, 1):
                    action(copy)

            @pl.when(jnp.logical_not(ends))
            def _():
                for copy in weight_copies(j, 0):
                    action(copy)

        def unless_left_out(j, work):
            if j in mids_only:
                pl.when(jnp.logical_not(ends))(work)
            else:
                work()

        def begin(copy):
            copy.start()

        def finish(copy):
            copy.wait()

        def load_rows(i):
            for p in range(INNER):
                row_copy(i, p).start()

        def multiply(j, out):
            layer = plan[j][0]
            source = inputs[layer]
            if layer in loads:
                source = held[loads.index(layer)]
                for p in range(INNER):
                    row_copy(loads.index(layer), p).wait()
            for p in range(INNER):
                result = jnp.dot(
                    source[piece(p), :],
                    w_buf[j % 2, :, : widths[j]],
                    preferred_element_type=jnp.float32,
                ).astype(jnp.bfloat16)
                at = 0
                for k, width in enumerate(cuts[j]):
                    outs[out + k][p * rows : (p + 1) * rows, :] = result[:, at : at + width]
                    at += width

        weights(0, begin)
        for i, layer in enumerate(loads):
            owner = [j for j, (used, _) in enumerate(plan) if used == layer]
            unless_left_out(owner[0], functools.partial(load_rows, i))
        out = 0
        for j in range(len(plan)):
            weights(j, finish)
            if j + 1 < len(plan):
                weights(j + 1, begin)
            unless_left_out(j, functools.partial(multiply, j, out))
            out += len(cuts[j])

    in_vmem = pl.BlockSpec(memory_space=pltpu.VMEM)
    in_specs = [pl.BlockSpec(memory_space=pl.ANY)] * len(operands)
    for i, operand in enumerate(operands):
        place_in = pltpu.VMEM if i in layers and i not in loads else pltpu.HBM
        in_specs[i] = pl.BlockSpec(memory_space=place_in)
        operands[i] = pltpu.with_memory_space_constraint(operand, place_in)
    resident = [pltpu.VMEM((INNER * rows, depth), jnp.bfloat16)] * kept
    return pl.pallas_call(
        kernel,
        out_shape=resident
        + [
            jax.ShapeDtypeStruct((INNER * rows, width), jnp.bfloat16)
            for cut in cuts
            for width in cut
        ],
        in_specs=in_specs,
        out_specs=[in_vmem] * (out_count + kept),
        scratch_shapes=[
            pltpu.VMEM((2, depth, max(widths)), jnp.bfloat16),
            pltpu.SemaphoreType.DMA((2, columns)),
            pltpu.SemaphoreType.DMA((max(kept, 1), INNER)),
        ],
        compiler_params=pltpu.CompilerParams(vmem_limit_bytes=22 * 1024 * 1024),
        cost_estimate=pl.CostEstimate(
            flops=cost, bytes_accessed=1000, transcendentals=0
        ),
    )(*operands)


def add_bf16(a, b):
    return (a.astype(jnp.float32) + b.astype(jnp.float32)).astype(jnp.bfloat16)


def to_owners(block, rows):
    pieces = [block[:rows]]
    for bits in range(1, INNER):
        pieces.append(send(block[bits * rows : (bits + 1) * rows], inner_swap(bits)))
    return pieces


def layer_rows(rows):
    groups = [[z * INNER + q for q in range(INNER)] for z in range(LAYERS)]
    return lax.all_gather(rows, "dp", axis_index_groups=groups, axis=0, tiled=True)


def line_pieces(context, output_weight, due, add_states):
    rows = context.shape[0]
    half = output_weight.shape[1] // 2
    quarter = half // 2
    block = 2 * half
    layer = lax.axis_index("dp") // INNER
    at_end = at_end_layer()
    near_half = (lax.axis_index("tensor") == 0) == (layer < 2)
    takes_lent = at_end & jnp.logical_not(near_half)

    def pin(*values):
        return lax.optimization_barrier(values)

    def swap(near_part, far_part, step=other_tensor):
        kept = jnp.where(near_half, near_part, far_part)
        return kept, send(jnp.where(near_half, far_part, near_part), step)

    def lend(part):
        return send(part, lend_straight), send(part, lend_across)

    def total(kept, came, lent):
        return add_bf16(
            jnp.where(takes_lent, lent[0], kept), jnp.where(takes_lent, lent[1], came)
        )

    def narrow(arrays):
        return [(array, 0, quarter) for array in arrays]

    quarters = [output_weight[:, i * quarter : (i + 1) * quarter] for i in range(4)]
    guest = send(context, inward)
    middle = send(output_weight, mid_swap)
    outer_end = send(output_weight, outward)
    own = layer_rows(context)
    near = [send(after(quarters[0], guest, due), inward)]
    guest, near[0], middle, outer_end, quarters, near_half, takes_lent = pin(
        guest, near[0], middle, outer_end, quarters, near_half, takes_lent
    )
    guests = layer_rows(guest)
    mid_quarters = [middle[:, :quarter]]
    mid_a, mid_b = [(middle, 0, half)], [(middle, half, half)]

    far = [send(near[0], mid_swap)]
    near.append(send(quarters[1], inward))
    mid_end = [send(mid_quarters[0], outward)]
    resident, *part_own = products(
        (own, [(output_weight, 0, block)], None, [quarter, quarter, half]), load=(own,)
    )
    mid_quarters.append(after(middle, part_own[0])[:, quarter : 2 * quarter])
    far[0], near[1], mid_end[0], resident, part_own, quarters, mid_quarters = pin(
        far[0], near[1], mid_end[0], resident, part_own, quarters, mid_quarters
    )

    far.append(send(near[1], mid_swap))
    near.append(send(quarters[2], inward))
    mid_end.append(send(mid_quarters[1], outward))
    part_mid_b, part_outer_a, part_mid_0 = products(
        (resident, mid_b + narrow(near[:2]), mid_b + [(outer_end, 0, half)], [half, half]),
        (resident, [(middle, 0, quarter)], narrow(mid_end[:1]), [quarter]),
    )
    far[1], near[2], mid_end[1], part_mid_b, part_outer_a, part_mid_0, quarters = pin(
        far[1], near[2], mid_end[1], part_mid_b, part_outer_a, part_mid_0, quarters
    )

    far.append(send(near[2], mid_swap))
    near.append(send(quarters[3], inward))
    swap_0 = swap(part_own[0], part_mid_0)
    (part_mid_1,) = products(
        (resident, [(middle, quarter, quarter)], narrow(mid_end[1:]), [quarter]),
        cost=100 * COST,
    )
    swap_1 = swap(part_own[1], part_mid_1)
    guests = after(guests, part_mid_1, swap_0)
    guests, lent_b = products((guests, mid_b, None, [half]), load=(guests,), mids_only=(0,))
    far[2], near[3], swap_0, swap_1, guests, lent_b, part_own, part_mid_b = pin(
        far[2], near[3], swap_0, swap_1, guests, lent_b, part_own, part_mid_b
    )

    far.append(send(near[3], mid_swap))
    lent_b = lend(lent_b)
    swap_b = swap(part_own[2], part_mid_b, exchange_but_lent)
    own, lent_c, part_far_a = products(
        (guests, narrow(far[:2]), None, [half]),
        (own, narrow(far[:2]), None, [half]),
        load=(own,),
        mids_only=(0,),
    )
    far[3], lent_b, swap_b, own, lent_c, part_far_a, near = pin(
        far[3], lent_b, swap_b, own, lent_c, part_far_a, near
    )

    lent_c = lend(lent_c)
    swap_c = swap(part_outer_a, part_far_a, exchange_but_lent)
    first = [add_bf16(*swap_0), add_bf16(*swap_1), total(*swap_b, lent_b)]
    first = to_owners(jnp.concatenate(first, axis=1), rows)
    lent_d, part_far_b, part_outer_b = products(
        (guests, narrow(far[2:]), None, [half]),
        (
            own,
            narrow(far[2:]) + narrow(near[2:]),
            narrow(far[2:]) + [(outer_end, half, half)],
            [half, half],
        ),
        mids_only=(0,),
    )
    lent_c, swap_c, first, lent_d, part_far_b, part_outer_b = pin(
        lent_c, swap_c, first, lent_d, part_far_b, part_outer_b
    )

    lent_d = lend(lent_d)
    swap_d = swap(part_outer_b, part_far_b, exchange_but_lent)
    second = to_owners(total(*swap_c, lent_c), rows)
    done = add_states(False, 0, first, None, False)
    lent_d, swap_d, second, done = pin(lent_d, swap_d, second, done)

    third = to_owners(total(*swap_d, lent_d), rows)
    done = add_states(True, 0, second, done, False)
    third, done = pin(third, done)
    return add_states(True, half, third, done, True)


def split3(value):
    parts = []
    for _ in range(3):
        parts.append(value.astype(jnp.bfloat16))
        value = value - parts[-1].astype(jnp.float32)
    return parts


def part_states(second, start, pieces, residual, delta, up_weight, low_rank, before, last):
    rows, cols = residual.shape
    rank = up_weight.shape[0]
    block = cols // (2 * INNER)
    width = pieces[0].shape[1]

    def kernel(*refs):
        piece_refs = refs[:INNER]
        res_ref, delta_ref, up_ref, low_ref = refs[INNER : INNER + 4]
        prior_ref = refs[INNER + 6] if before else None
        adapted_ref, attn_ref, sums_out = refs[-12:-9]
        attn, res, delta_v, adapted, up_v, sums_ref, sem, in_sem, out_sem = refs[-9:]
        data_rank = lax.axis_index("dp")
        layer = data_rank // INNER
        place = data_rank % INNER
        low = layer < 2
        near_half = (lax.axis_index("tensor") == 0) == low
        first = jnp.where(near_half, layer % 2, jnp.where(low, 0, 1))
        side = 1 - first if second else first

        def window(ref, j):
            at = (side * INNER + (place ^ j)) * block + start
            return ref.at[:, pl.ds(pl.multiple_of(at, width), width)]

        def part(ref, j):
            return ref.at[:, pl.ds(j * width, width)]

        loads = []
        for j in range(INNER):
            for i, (source, to) in enumerate(((res_ref, res), (delta_ref, delta_v), (up_ref, up_v))):
                loads.append(
                    pltpu.make_async_copy(window(source, j), part(to, j), in_sem.at[i, j])
                )
            loads.append(pltpu.make_async_copy(piece_refs[j], part(attn, j), sem.at[j]))
        for copy in loads:
            copy.start()
        low_parts = jnp.concatenate(split3(ADAPTER_SCALE * low_ref[...].T), axis=1)
        if before:
            sums_ref[...] = prior_ref[...]
        else:
            sums_ref[...] = jnp.zeros_like(sums_ref)
        for copy in loads:
            copy.wait()
        stores = [
            pltpu.make_async_copy(part(attn, j), window(attn_ref, j), out_sem.at[0, j])
            for j in range(INNER)
        ]
        for copy in stores:
            copy.start()

        def on_up(values, up):
            return lax.dot_general(
                values, up, (((1,), (1,)), ((), ())), preferred_element_type=jnp.float32
            )

        @pl.loop(0, INNER)
        def _(j):
            here = pl.ds(pl.multiple_of(j * width, width), width)
            up = up_v[:, here]
            low_up = jnp.dot(
                low_parts,
                jnp.concatenate([up] * 3, axis=0),
                preferred_element_type=jnp.float32,
            )
            rest = res[:, here].astype(jnp.float32)
            states = rest + attn[:, here].astype(jnp.float32) + low_up
            target = rest + delta_v[:, here].astype(jnp.float32)
            gap = states - target
            adapted[:, here] = states.astype(jnp.bfloat16)
            squares = on_up(up, up)
            low_sums = 0
            for low_part in split3(squares):
                for k in range(3):
                    low_sums += jnp.dot(
                        low_parts[:, k * rank : (k + 1) * rank],
                        low_part,
                        preferred_element_type=jnp.float32,
                    )
            sums_ref[:, :rank] += on_up(res[:, here], up) + on_up(attn[:, here], up) + low_sums
            for k, product in enumerate((states * states, states * target, gap * gap)):
                sums_ref[:, rank + k : rank + k + 1] += jnp.sum(product, axis=1, keepdims=True)

        for j in range(INNER):
            stores.append(
                pltpu.make_async_copy(part(adapted, j), window(adapted_ref, j), out_sem.at[1, j])
            )
            stores[-1].start()
        sums_out[...] = sums_ref[...].T[:24] if last else sums_ref[...]
        for copy in stores:
            copy.wait()

    anywhere = pl.BlockSpec(memory_space=pl.ANY)
    in_vmem = pl.BlockSpec(memory_space=pltpu.VMEM)
    operands = (*pieces, residual, delta, up_weight, low_rank, *(before or ()))
    return pl.pallas_call(
        kernel,
        out_shape=(
            pltpu.HBM((rows, cols), jnp.bfloat16),
            pltpu.HBM((rows, cols), jnp.bfloat16),
            jax.ShapeDtypeStruct((24, rows) if last else (rows, 128), jnp.float32),
        ),
        in_specs=[anywhere] * (INNER + 3)
        + [in_vmem]
        + ([anywhere, anywhere, in_vmem] if before else []),
        out_specs=(anywhere, anywhere, in_vmem),
        input_output_aliases={INNER + 4: 0, INNER + 5: 1} if before else {},
        scratch_shapes=[pltpu.VMEM((rows, INNER * width), jnp.bfloat16) for _ in range(4)]
        + [
            pltpu.VMEM((rank, INNER * width), jnp.bfloat16),
            pltpu.VMEM((rows, 128), jnp.float32),
            pltpu.SemaphoreType.DMA((INNER,)),
            pltpu.SemaphoreType.DMA((3, INNER)),
            pltpu.SemaphoreType.DMA((2, INNER)),
        ],
        compiler_params=pltpu.CompilerParams(vmem_limit_bytes=32 * 1024 * 1024),
        cost_estimate=pl.CostEstimate(flops=COST, bytes_accessed=1000, transcendentals=0),
    )(*operands)


def hold(*arrays):
    count = len(arrays)

    def kernel(*refs):
        copies = [
            pltpu.make_async_copy(refs[i], refs[count + i], refs[-1].at[i]) for i in range(count)
        ]
        for copy in copies:
            copy.start()
        for copy in copies:
            copy.wait()

    arrays = [pltpu.with_memory_space_constraint(array, pltpu.HBM) for array in arrays]
    return pl.pallas_call(
        kernel,
        out_shape=[pltpu.VMEM(array.shape, array.dtype) for array in arrays],
        in_specs=[pl.BlockSpec(memory_space=pltpu.HBM)] * count,
        out_specs=[pl.BlockSpec(memory_space=pltpu.VMEM)] * count,
        scratch_shapes=[pltpu.SemaphoreType.DMA((count,))],
        compiler_params=pltpu.CompilerParams(vmem_limit_bytes=16 * 1024 * 1024),
        cost_estimate=pl.CostEstimate(flops=100 * COST, bytes_accessed=1000, transcendentals=0),
    )(*arrays)


def line_grads(sums, came, early_sums, low_t, weights, context, residual, delta, attn, up_weight):
    rows, cols = residual.shape
    rank = up_weight.shape[0]
    width = cols // INNER

    def kernel(*refs):
        sums_ref, came_ref, early_ref, low_ref, weight_ref = refs[:5]
        ctx_ref, res_ref, delta_ref, attn_in, up_in = refs[5:10]
        keep_ref, give_ref, attn_ref, up_ref, sem = refs[10:]
        place = lax.axis_index("dp") % INNER
        loads = [
            pltpu.make_async_copy(attn_in, attn_ref, sem.at[0]),
            pltpu.make_async_copy(up_in, up_ref, sem.at[1]),
        ]
        for copy in loads:
            copy.start()
        sums = sums_ref[...] + came_ref[...]
        early = early_ref[...]
        low = low_ref[...]
        states_up, target_up = sums[:rank], early[:rank]
        norm_h = jnp.sqrt(sums[rank : rank + 1] + NORM_EPS)
        norm_g = jnp.sqrt(early[rank : rank + 1] + NORM_EPS)
        cosine = sums[rank + 1 : rank + 2] / (norm_h * norm_g)
        distance = jnp.sqrt(sums[rank + 2 : rank + 3] + NORM_EPS)
        weight_harm = weight_ref[0:1]
        weight_keep = weight_ref[1:2] / distance
        on_target = weight_harm / (norm_h * norm_g) - weight_keep
        on_states = weight_keep - weight_harm * cosine / (norm_h * norm_h)

        def stacked(value):
            return jnp.concatenate(split3(value), axis=0)

        def total(parts, values):
            product = jnp.dot(parts, values, preferred_element_type=jnp.float32)
            return product[:rank] + product[rank : 2 * rank] + product[2 * rank :]

        twice = ADAPTER_SCALE * low
        for_context = stacked(ADAPTER_SCALE * (on_target * target_up + on_states * states_up))
        for_rest = stacked(twice * (on_target + on_states))
        for_delta = stacked(twice * on_target)
        for_attn = stacked(twice * on_states)
        mixed = lax.dot_general(
            twice * on_states,
            twice,
            (((1,), (1,)), ((), ())),
            precision=HIGHEST,
            preferred_element_type=jnp.float32,
        )
        for_up = stacked(mixed)
        for j in range(INNER):
            here = pl.ds(pl.multiple_of((place ^ j) * width, width), width)
            out = give_ref if j % 2 else keep_ref
            out[j // 2, :rank, :] = total(for_context, ctx_ref[:, here])
            part = total(for_rest, res_ref[:, here]) + total(for_delta, delta_ref[:, here])
            if j == 0:
                for copy in loads:
                    copy.wait()
            part += total(for_attn, attn_ref[:, here]) + total(for_up, up_ref[:, here])
            out[j // 2, rank:, :] = part

    anywhere = pl.BlockSpec(memory_space=pl.ANY)
    in_vmem = pl.BlockSpec(memory_space=pltpu.VMEM)
    return pl.pallas_call(
        kernel,
        out_shape=[jax.ShapeDtypeStruct((2, 2 * rank, width), jnp.float32)] * 2,
        in_specs=[in_vmem] * 8 + [anywhere] * 2,
        out_specs=[in_vmem] * 2,
        scratch_shapes=[
            pltpu.VMEM((rows, cols), jnp.bfloat16),
            pltpu.VMEM((rank, cols), jnp.bfloat16),
            pltpu.SemaphoreType.DMA((2,)),
        ],
        compiler_params=pltpu.CompilerParams(vmem_limit_bytes=24 * 1024 * 1024),
        cost_estimate=pl.CostEstimate(flops=COST, bytes_accessed=1000, transcendentals=0),
    )(
        sums, came, early_sums, low_t, weights,
        *(pltpu.with_memory_space_constraint(x, pltpu.VMEM) for x in (context, residual, delta)),
        attn, up_weight,
    )


def general_attention(context, output_weight):
    partial = dot_bf16(context, lax.all_gather(output_weight, "dp", axis=1, tiled=True))
    return lax.psum_scatter(partial, "tensor", scatter_dimension=1, tiled=True)


def line_sum_grads(keep, give):
    place = lax.axis_index("dp") % INNER
    rank = keep.shape[1] // 2
    keep = keep + send(give, inner_swap(1))
    both = keep[0] + send(keep[1], inner_swap(2))
    for bits in (1, 2):
        both = both + send(both, lambda z, q, t: (z ^ bits, q, t))
    grad_b = both[rank:]
    other = send(grad_b, other_tensor)
    across = send(both, inner_swap(2))
    across_other = send(grad_b, lambda z, q, t: (z, q ^ 2, 1 - t))

    def joined(bits, mine, got):
        upper = (place & bits) != 0
        return jnp.concatenate(
            [jnp.where(upper, got, mine), jnp.where(upper, mine, got)], axis=1
        )

    mine = jnp.stack([jnp.concatenate([both, other]), jnp.concatenate([across, across_other])])
    got = send(mine, inner_swap(1))
    mine = joined(2, joined(1, mine[0], got[0]), joined(1, mine[1], got[1]))
    grad_a = mine[:rank].T
    kept, other = mine[rank : 2 * rank], mine[2 * rank :]
    first = lax.axis_index("tensor") == 0
    grad_b = jnp.concatenate(
        [jnp.where(first, kept, other), jnp.where(first, other, kept)], axis=1
    )
    return grad_a, grad_b


def general_sum_grads(grad_a_t, grad_b):
    grad_a_t, grad_b = lax.psum((grad_a_t, grad_b), "dp")
    return grad_a_t.T, lax.all_gather(grad_b, "tensor", axis=1, tiled=True)


def solution(mesh):
    line = mesh.shape["dp"] == LAYERS * INNER and mesh.shape["tensor"] == 2

    def sum_tensor(value):
        if line:
            return value + send(value, other_tensor)
        return lax.psum(value, "tensor")

    def local(
        context,
        output_weight,
        adapter_down_weight,
        adapter_up_weight,
        residual,
        frozen_residual_delta,
        harmful_count,
        retain_count,
    ):
        seq_len = context.shape[0]
        tensor_rank = lax.axis_index("tensor")
        data_rank = lax.axis_index("dp")
        harm_total = jnp.sum(harmful_count).astype(jnp.float32)
        keep_total = jnp.sum(retain_count).astype(jnp.float32)
        harm_here = harmful_count[data_rank]
        keep_here = retain_count[data_rank]
        col_count = residual.shape[1]

        low_rank_t = sum_tensor(
            lax.dot_general(
                adapter_down_weight,
                context,
                (((0,), (1,)), ((), ())),
                preferred_element_type=jnp.float32,
            )
        )
        up_narrow = lax.dynamic_slice_in_dim(
            adapter_up_weight, tensor_rank * col_count, col_count, 1
        )
        up_columns = up_narrow.astype(jnp.float32)
        target = residual.astype(jnp.float32) + frozen_residual_delta.astype(jnp.float32)

        def on_up(values):
            return lax.dot_general(
                up_columns, values, (((1,), (1,)), ((), ())), precision=HIGHEST
            )

        rank = up_columns.shape[0]
        early_sums = sum_tensor(
            jnp.concatenate([on_up(target), jnp.sum(target * target, axis=1)[None]], axis=0)
        )
        target_up, sq_target = early_sums[:rank], early_sums[rank]
        positions = jnp.arange(seq_len, dtype=jnp.int32)
        harmful = (positions < harm_here).astype(jnp.float32)
        retained = (
            (positions >= harm_here) & (positions < harm_here + keep_here)
        ).astype(jnp.float32)
        weight_harm = REROUTE_WEIGHT / harm_total * harmful
        weight_keep = RETAIN_WEIGHT / keep_total * retained
        if line:
            weights = jnp.stack([weight_harm, weight_keep])
            constant = (residual, frozen_residual_delta, up_narrow, low_rank_t)
            adapted, attn, sums = line_pieces(
                context,
                output_weight,
                (low_rank_t, early_sums, weights),
                lambda second, start, pieces, before, last: part_states(
                    second, start, pieces, *constant, before, last
                ),
            )
            held = hold(*lax.optimization_barrier((context, residual, frozen_residual_delta, sums))[:3])
            keep, give = line_grads(
                sums,
                send(sums, other_tensor),
                early_sums,
                low_rank_t,
                weights,
                *held,
                attn,
                up_narrow,
            )
            return adapted, *line_sum_grads(keep, give)
        low_up = ADAPTER_SCALE * lax.dot_general(
            low_rank_t, up_columns, (((0,), (0,)), ((), ())), precision=HIGHEST
        )
        attn = general_attention(context, output_weight).astype(jnp.float32)
        states = residual.astype(jnp.float32) + attn + low_up
        adapted = states.astype(jnp.bfloat16)
        gap = states - target
        products = [states * states, states * target, gap * gap]
        sums = jnp.stack([jnp.sum(product, axis=1) for product in products])
        sums = jnp.concatenate([on_up(states), sums], axis=0)
        shared = sum_tensor(sums)
        states_up = shared[:rank]
        sq_state, cross_term, gap_sq = (shared[rank + i] for i in range(3))

        norm_h = jnp.sqrt(sq_state + NORM_EPS)
        norm_g = jnp.sqrt(sq_target + NORM_EPS)
        cosine = cross_term / (norm_h * norm_g)
        distance = jnp.sqrt(gap_sq + NORM_EPS)
        weight_keep = weight_keep / distance
        on_target = weight_harm / (norm_h * norm_g) - weight_keep
        on_states = weight_keep - weight_harm * cosine / (norm_h * norm_h)

        cotangent = on_target[:, None] * target + on_states[:, None] * states
        low_cot_t = ADAPTER_SCALE * (on_target * target_up + on_states * states_up)
        grad_a_t = jnp.dot(low_cot_t, context.astype(jnp.float32), precision=HIGHEST)
        grad_b = ADAPTER_SCALE * jnp.dot(low_rank_t, cotangent, precision=HIGHEST)
        grad_a, grad_b = general_sum_grads(grad_a_t, grad_b)
        return adapted, grad_a, grad_b

    return jax.shard_map(
        local,
        mesh=mesh,
        in_specs=(
            P("dp", "tensor"),
            P("tensor", "dp"),
            P("tensor", None),
            P(),
            P("dp", "tensor"),
            P("dp", "tensor"),
            P(),
            P(),
        ),
        out_specs=(P("dp", "tensor"), P("tensor", None), P()),
        check_vma=False,
    )
```

```python
import functools

import jax
import jax.numpy as jnp
from jax import lax
from jax.experimental import pallas as pl
from jax.experimental.pallas import tpu as pltpu
from jax.sharding import PartitionSpec as P

ADAPTER_SCALE = 2.0
NORM_EPS = 1e-06
REROUTE_WEIGHT = 65536.0
RETAIN_WEIGHT = 1024.0
COST = 100_000_000
INNER = 4
LAYERS = 4
HIGHEST = lax.Precision.HIGHEST


def after(value, *earlier):
    return lax.optimization_barrier((value,) + earlier)[0]


def routes(step):
    pairs = []
    for z in range(LAYERS):
        for q in range(INNER):
            for t in range(2):
                to = step(z, q, t)
                if to is not None:
                    pairs.append(((z * INNER + q) * 2 + t, (to[0] * INNER + to[1]) * 2 + to[2]))
    return pairs


def send(value, step):
    return lax.ppermute(value, ("dp", "tensor"), routes(step))


def inward(z, q, t):
    return {0: (1, q, t), 3: (2, q, t)}.get(z)


def outward(z, q, t):
    return {1: (0, q, t), 2: (3, q, t)}.get(z)


def mid_swap(z, q, t):
    return {1: (2, q, t), 2: (1, q, t)}.get(z)


def inner_swap(bits, layers=range(LAYERS)):
    return lambda z, q, t: (z, q ^ bits, t) if z in layers else None


def other_tensor(z, q, t):
    return (z, q, 1 - t)


def keeps_near(z, t):
    return (t == 0) == (z < 2)


def exchange_but_lent(z, q, t):
    return None if z in (0, 3) and keeps_near(z, t) else (z, q, 1 - t)


def lend_straight(z, q, t):
    return None if keeps_near(z, t) else outward(z, q, t)


def lend_across(z, q, t):
    return outward(z, q, 1 - t) if keeps_near(z, t) else None


def dot_bf16(a, b):
    return jnp.dot(a, b, preferred_element_type=jnp.float32).astype(jnp.bfloat16)


def at_end_layer():
    layer = lax.axis_index("dp") // INNER
    return (layer == 0) | (layer == LAYERS - 1)


def products(*jobs, load=(), mids_only=(), cost=COST):
    operands = []

    def index(array):
        for i, known in enumerate(operands):
            if known is array:
                return i
        operands.append(array)
        return len(operands) - 1

    plan = []
    layers = []
    for layer, weights, ends, _ in jobs:
        choices = [weights] if ends is None else [weights, ends]
        if index(layer) not in layers:
            layers.append(index(layer))
        plan.append(
            (
                index(layer),
                [[(index(w), start, n) for w, start, n in choice] for choice in choices],
            )
        )
    depth = jobs[0][0].shape[1]
    rows = jobs[0][0].shape[0] // INNER
    widths = [sum(n for _, _, n in choices[0]) for _, choices in plan]
    cuts = [job[3] for job in jobs]
    out_count = sum(len(cut) for cut in cuts)
    columns = max(len(choice) for _, choices in plan for choice in choices)
    loads = [index(layer) for layer in load]
    kept = len(loads)

    def kernel(*refs):
        inputs = refs[: len(operands)]
        held = refs[len(operands) : len(operands) + kept]
        outs = refs[len(operands) + kept : len(operands) + kept + out_count]
        w_buf, w_sem, a_sem = refs[len(operands) + kept + out_count :]
        ends = at_end_layer()
        place = lax.axis_index("dp") % INNER

        def piece(p):
            return pl.ds(pl.multiple_of((place ^ p) * rows, rows), rows)

        def row_copy(i, p):
            return pltpu.make_async_copy(
                inputs[loads[i]].at[piece(p)], held[i].at[piece(p)], a_sem.at[i, p]
            )

        def weight_copies(j, choice):
            at = 0
            for i, (k, start, n) in enumerate(plan[j][1][choice]):
                source = inputs[k]
                if source.shape[1] != n:
                    source = source.at[:, pl.ds(start, n)]
                yield pltpu.make_async_copy(
                    source, w_buf.at[j % 2, :, pl.ds(at, n)], w_sem.at[j % 2, i]
                )
                at += n

        def weights(j, action):
            def first_choice():
                for copy in weight_copies(j, 0):
                    action(copy)

            if len(plan[j][1]) == 1:
                unless_left_out(j, first_choice)
                return

            @pl.when(ends)
            def _():
                for copy in weight_copies(j, 1):
                    action(copy)

            @pl.when(jnp.logical_not(ends))
            def _():
                for copy in weight_copies(j, 0):
                    action(copy)

        def unless_left_out(j, work):
            if j in mids_only:
                pl.when(jnp.logical_not(ends))(work)
            else:
                work()

        def begin(copy):
            copy.start()

        def finish(copy):
            copy.wait()

        def load_rows(i):
            for p in range(INNER):
                row_copy(i, p).start()

        def multiply(j, out):
            layer = plan[j][0]
            source = inputs[layer]
            if layer in loads:
                source = held[loads.index(layer)]
                for p in range(INNER):
                    row_copy(loads.index(layer), p).wait()
            for p in range(INNER):
                result = jnp.dot(
                    source[piece(p), :],
                    w_buf[j % 2, :, : widths[j]],
                    preferred_element_type=jnp.float32,
                ).astype(jnp.bfloat16)
                at = 0
                for k, width in enumerate(cuts[j]):
                    outs[out + k][p * rows : (p + 1) * rows, :] = result[:, at : at + width]
                    at += width

        weights(0, begin)
        for i, layer in enumerate(loads):
            owner = [j for j, (used, _) in enumerate(plan) if used == layer]
            unless_left_out(owner[0], functools.partial(load_rows, i))
        out = 0
        for j in range(len(plan)):
            weights(j, finish)
            if j + 1 < len(plan):
                weights(j + 1, begin)
            unless_left_out(j, functools.partial(multiply, j, out))
            out += len(cuts[j])

    in_vmem = pl.BlockSpec(memory_space=pltpu.VMEM)
    in_specs = [pl.BlockSpec(memory_space=pl.ANY)] * len(operands)
    for i, operand in enumerate(operands):
        place_in = pltpu.VMEM if i in layers and i not in loads else pltpu.HBM
        in_specs[i] = pl.BlockSpec(memory_space=place_in)
        operands[i] = pltpu.with_memory_space_constraint(operand, place_in)
    resident = [pltpu.VMEM((INNER * rows, depth), jnp.bfloat16)] * kept
    return pl.pallas_call(
        kernel,
        out_shape=resident
        + [
            jax.ShapeDtypeStruct((INNER * rows, width), jnp.bfloat16)
            for cut in cuts
            for width in cut
        ],
        in_specs=in_specs,
        out_specs=[in_vmem] * (out_count + kept),
        scratch_shapes=[
            pltpu.VMEM((2, depth, max(widths)), jnp.bfloat16),
            pltpu.SemaphoreType.DMA((2, columns)),
            pltpu.SemaphoreType.DMA((max(kept, 1), INNER)),
        ],
        compiler_params=pltpu.CompilerParams(vmem_limit_bytes=22 * 1024 * 1024),
        cost_estimate=pl.CostEstimate(
            flops=cost, bytes_accessed=1000, transcendentals=0
        ),
    )(*operands)


def add_bf16(a, b):
    return (a.astype(jnp.float32) + b.astype(jnp.float32)).astype(jnp.bfloat16)


def to_owners(block, rows):
    pieces = [block[:rows]]
    for bits in range(1, INNER):
        pieces.append(send(block[bits * rows : (bits + 1) * rows], inner_swap(bits)))
    return pieces


def layer_rows(rows):
    groups = [[z * INNER + q for q in range(INNER)] for z in range(LAYERS)]
    return lax.all_gather(rows, "dp", axis_index_groups=groups, axis=0, tiled=True)


def line_pieces(context, output_weight, due, add_states):
    rows = context.shape[0]
    half = output_weight.shape[1] // 2
    quarter = half // 2
    block = 2 * half
    layer = lax.axis_index("dp") // INNER
    at_end = at_end_layer()
    near_half = (lax.axis_index("tensor") == 0) == (layer < 2)
    takes_lent = at_end & jnp.logical_not(near_half)

    def pin(*values):
        return lax.optimization_barrier(values)

    def swap(near_part, far_part, step=other_tensor):
        kept = jnp.where(near_half, near_part, far_part)
        return kept, send(jnp.where(near_half, far_part, near_part), step)

    def lend(part):
        return send(part, lend_straight), send(part, lend_across)

    def total(kept, came, lent):
        return add_bf16(
            jnp.where(takes_lent, lent[0], kept), jnp.where(takes_lent, lent[1], came)
        )

    def narrow(arrays):
        return [(array, 0, quarter) for array in arrays]

    quarters = [output_weight[:, i * quarter : (i + 1) * quarter] for i in range(4)]
    guest = send(context, inward)
    middle = send(output_weight, mid_swap)
    outer_end = send(output_weight, outward)
    own = layer_rows(context)
    near = [send(after(quarters[0], guest, due), inward)]
    guest, near[0], middle, outer_end, quarters, near_half, takes_lent = pin(
        guest, near[0], middle, outer_end, quarters, near_half, takes_lent
    )
    guests = layer_rows(guest)
    mid_quarters = [middle[:, :quarter]]
    mid_a, mid_b = [(middle, 0, half)], [(middle, half, half)]

    far = [send(near[0], mid_swap)]
    near.append(send(quarters[1], inward))
    mid_end = [send(mid_quarters[0], outward)]
    resident, *part_own = products(
        (own, [(output_weight, 0, block)], None, [quarter, quarter, half]), load=(own,)
    )
    mid_quarters.append(after(middle, part_own[0])[:, quarter : 2 * quarter])
    far[0], near[1], mid_end[0], resident, part_own, quarters, mid_quarters = pin(
        far[0], near[1], mid_end[0], resident, part_own, quarters, mid_quarters
    )

    far.append(send(near[1], mid_swap))
    near.append(send(quarters[2], inward))
    mid_end.append(send(mid_quarters[1], outward))
    part_mid_b, part_outer_a, part_mid_0 = products(
        (resident, mid_b + narrow(near[:2]), mid_b + [(outer_end, 0, half)], [half, half]),
        (resident, [(middle, 0, quarter)], narrow(mid_end[:1]), [quarter]),
    )
    far[1], near[2], mid_end[1], part_mid_b, part_outer_a, part_mid_0, quarters = pin(
        far[1], near[2], mid_end[1], part_mid_b, part_outer_a, part_mid_0, quarters
    )

    far.append(send(near[2], mid_swap))
    near.append(send(quarters[3], inward))
    swap_0 = swap(part_own[0], part_mid_0)
    (part_mid_1,) = products(
        (resident, [(middle, quarter, quarter)], narrow(mid_end[1:]), [quarter]),
        cost=100 * COST,
    )
    swap_1 = swap(part_own[1], part_mid_1)
    guests = after(guests, part_mid_1, swap_0)
    guests, lent_b = products((guests, mid_b, None, [half]), load=(guests,), mids_only=(0,))
    far[2], near[3], swap_0, swap_1, guests, lent_b, part_own, part_mid_b = pin(
        far[2], near[3], swap_0, swap_1, guests, lent_b, part_own, part_mid_b
    )

    far.append(send(near[3], mid_swap))
    lent_b = lend(lent_b)
    swap_b = swap(part_own[2], part_mid_b, exchange_but_lent)
    own, lent_c, part_far_a = products(
        (guests, narrow(far[:2]), None, [half]),
        (own, narrow(far[:2]), None, [half]),
        load=(own,),
        mids_only=(0,),
    )
    far[3], lent_b, swap_b, own, lent_c, part_far_a, near = pin(
        far[3], lent_b, swap_b, own, lent_c, part_far_a, near
    )

    lent_c = lend(lent_c)
    swap_c = swap(part_outer_a, part_far_a, exchange_but_lent)
    first = [add_bf16(*swap_0), add_bf16(*swap_1), total(*swap_b, lent_b)]
    first = to_owners(jnp.concatenate(first, axis=1), rows)
    lent_d, part_far_b, part_outer_b = products(
        (guests, narrow(far[2:]), None, [half]),
        (
            own,
            narrow(far[2:]) + narrow(near[2:]),
            narrow(far[2:]) + [(outer_end, half, half)],
            [half, half],
        ),
        mids_only=(0,),
    )
    lent_c, swap_c, first, lent_d, part_far_b, part_outer_b = pin(
        lent_c, swap_c, first, lent_d, part_far_b, part_outer_b
    )

    lent_d = lend(lent_d)
    swap_d = swap(part_outer_b, part_far_b, exchange_but_lent)
    second = to_owners(total(*swap_c, lent_c), rows)
    done = add_states(False, 0, first, None, False)
    lent_d, swap_d, second, done = pin(lent_d, swap_d, second, done)

    third = to_owners(total(*swap_d, lent_d), rows)
    done = add_states(True, 0, second, done, False)
    third, done = pin(third, done)
    return add_states(True, half, third, done, True)


def split3(value):
    parts = []
    for _ in range(3):
        parts.append(value.astype(jnp.bfloat16))
        value = value - parts[-1].astype(jnp.float32)
    return parts


def part_states(second, start, pieces, residual, delta, up_weight, low_rank, before, last):
    rows, cols = residual.shape
    rank = up_weight.shape[0]
    block = cols // (2 * INNER)
    width = pieces[0].shape[1]

    def kernel(*refs):
        piece_refs = refs[:INNER]
        res_ref, delta_ref, up_ref, low_ref = refs[INNER : INNER + 4]
        prior_ref = refs[INNER + 6] if before else None
        adapted_ref, attn_ref, sums_out = refs[-12:-9]
        attn, res, delta_v, adapted, up_v, sums_ref, sem, in_sem, out_sem = refs[-9:]
        data_rank = lax.axis_index("dp")
        layer = data_rank // INNER
        place = data_rank % INNER
        low = layer < 2
        near_half = (lax.axis_index("tensor") == 0) == low
        first = jnp.where(near_half, layer % 2, jnp.where(low, 0, 1))
        side = 1 - first if second else first

        def window(ref, j):
            at = (side * INNER + (place ^ j)) * block + start
            return ref.at[:, pl.ds(pl.multiple_of(at, width), width)]

        def part(ref, j):
            return ref.at[:, pl.ds(j * width, width)]

        loads = []
        for j in range(INNER):
            for i, (source, to) in enumerate(((res_ref, res), (delta_ref, delta_v), (up_ref, up_v))):
                loads.append(
                    pltpu.make_async_copy(window(source, j), part(to, j), in_sem.at[i, j])
                )
            loads.append(pltpu.make_async_copy(piece_refs[j], part(attn, j), sem.at[j]))
        for copy in loads:
            copy.start()
        low_parts = jnp.concatenate(split3(ADAPTER_SCALE * low_ref[...].T), axis=1)
        if before:
            sums_ref[...] = prior_ref[...]
        else:
            sums_ref[...] = jnp.zeros_like(sums_ref)
        for copy in loads:
            copy.wait()
        stores = [
            pltpu.make_async_copy(part(attn, j), window(attn_ref, j), out_sem.at[0, j])
            for j in range(INNER)
        ]
        for copy in stores:
            copy.start()

        def on_up(values, up):
            return lax.dot_general(
                values, up, (((1,), (1,)), ((), ())), preferred_element_type=jnp.float32
            )

        @pl.loop(0, INNER)
        def _(j):
            here = pl.ds(pl.multiple_of(j * width, width), width)
            up = up_v[:, here]
            low_up = jnp.dot(
                low_parts,
                jnp.concatenate([up] * 3, axis=0),
                preferred_element_type=jnp.float32,
            )
            rest = res[:, here].astype(jnp.float32)
            states = rest + attn[:, here].astype(jnp.float32) + low_up
            target = rest + delta_v[:, here].astype(jnp.float32)
            gap = states - target
            adapted[:, here] = states.astype(jnp.bfloat16)
            squares = on_up(up, up)
            low_sums = 0
            for low_part in split3(squares):
                for k in range(3):
                    low_sums += jnp.dot(
                        low_parts[:, k * rank : (k + 1) * rank],
                        low_part,
                        preferred_element_type=jnp.float32,
                    )
            sums_ref[:, :rank] += on_up(res[:, here], up) + on_up(attn[:, here], up) + low_sums
            for k, product in enumerate((states * states, states * target, gap * gap)):
                sums_ref[:, rank + k : rank + k + 1] += jnp.sum(product, axis=1, keepdims=True)

        for j in range(INNER):
            stores.append(
                pltpu.make_async_copy(part(adapted, j), window(adapted_ref, j), out_sem.at[1, j])
            )
            stores[-1].start()
        sums_out[...] = sums_ref[...].T[:24] if last else sums_ref[...]
        for copy in stores:
            copy.wait()

    anywhere = pl.BlockSpec(memory_space=pl.ANY)
    in_vmem = pl.BlockSpec(memory_space=pltpu.VMEM)
    operands = (*pieces, residual, delta, up_weight, low_rank, *(before or ()))
    return pl.pallas_call(
        kernel,
        out_shape=(
            pltpu.HBM((rows, cols), jnp.bfloat16),
            pltpu.HBM((rows, cols), jnp.bfloat16),
            jax.ShapeDtypeStruct((24, rows) if last else (rows, 128), jnp.float32),
        ),
        in_specs=[anywhere] * (INNER + 3)
        + [in_vmem]
        + ([anywhere, anywhere, in_vmem] if before else []),
        out_specs=(anywhere, anywhere, in_vmem),
        input_output_aliases={INNER + 4: 0, INNER + 5: 1} if before else {},
        scratch_shapes=[pltpu.VMEM((rows, INNER * width), jnp.bfloat16) for _ in range(4)]
        + [
            pltpu.VMEM((rank, INNER * width), jnp.bfloat16),
            pltpu.VMEM((rows, 128), jnp.float32),
            pltpu.SemaphoreType.DMA((INNER,)),
            pltpu.SemaphoreType.DMA((3, INNER)),
            pltpu.SemaphoreType.DMA((2, INNER)),
        ],
        compiler_params=pltpu.CompilerParams(vmem_limit_bytes=32 * 1024 * 1024),
        cost_estimate=pl.CostEstimate(flops=COST, bytes_accessed=1000, transcendentals=0),
    )(*operands)


def hold(*arrays):
    count = len(arrays)

    def kernel(*refs):
        copies = [
            pltpu.make_async_copy(refs[i], refs[count + i], refs[-1].at[i]) for i in range(count)
        ]
        for copy in copies:
            copy.start()
        for copy in copies:
            copy.wait()

    arrays = [pltpu.with_memory_space_constraint(array, pltpu.HBM) for array in arrays]
    return pl.pallas_call(
        kernel,
        out_shape=[pltpu.VMEM(array.shape, array.dtype) for array in arrays],
        in_specs=[pl.BlockSpec(memory_space=pltpu.HBM)] * count,
        out_specs=[pl.BlockSpec(memory_space=pltpu.VMEM)] * count,
        scratch_shapes=[pltpu.SemaphoreType.DMA((count,))],
        compiler_params=pltpu.CompilerParams(vmem_limit_bytes=16 * 1024 * 1024),
        cost_estimate=pl.CostEstimate(flops=100 * COST, bytes_accessed=1000, transcendentals=0),
    )(*arrays)


def line_grads(sums, came, early_sums, low_t, weights, context, residual, delta, attn, up_weight):
    rows, cols = residual.shape
    rank = up_weight.shape[0]
    width = cols // INNER

    def kernel(*refs):
        sums_ref, came_ref, early_ref, low_ref, weight_ref = refs[:5]
        ctx_ref, res_ref, delta_ref, attn_in, up_in = refs[5:10]
        keep_ref, give_ref, attn_ref, up_ref, sem = refs[10:]
        place = lax.axis_index("dp") % INNER
        loads = [
            pltpu.make_async_copy(attn_in, attn_ref, sem.at[0]),
            pltpu.make_async_copy(up_in, up_ref, sem.at[1]),
        ]
        for copy in loads:
            copy.start()
        sums = sums_ref[...] + came_ref[...]
        early = early_ref[...]
        low = low_ref[...]
        states_up, target_up = sums[:rank], early[:rank]
        norm_h = jnp.sqrt(sums[rank : rank + 1] + NORM_EPS)
        norm_g = jnp.sqrt(early[rank : rank + 1] + NORM_EPS)
        cosine = sums[rank + 1 : rank + 2] / (norm_h * norm_g)
        distance = jnp.sqrt(sums[rank + 2 : rank + 3] + NORM_EPS)
        weight_harm = weight_ref[0:1]
        weight_keep = weight_ref[1:2] / distance
        on_target = weight_harm / (norm_h * norm_g) - weight_keep
        on_states = weight_keep - weight_harm * cosine / (norm_h * norm_h)

        def stacked(value):
            return jnp.concatenate(split3(value), axis=0)

        def total(parts, values):
            product = jnp.dot(parts, values, preferred_element_type=jnp.float32)
            return product[:rank] + product[rank : 2 * rank] + product[2 * rank :]

        twice = ADAPTER_SCALE * low
        for_context = stacked(ADAPTER_SCALE * (on_target * target_up + on_states * states_up))
        for_rest = stacked(twice * (on_target + on_states))
        for_delta = stacked(twice * on_target)
        for_attn = stacked(twice * on_states)
        mixed = lax.dot_general(
            twice * on_states,
            twice,
            (((1,), (1,)), ((), ())),
            precision=HIGHEST,
            preferred_element_type=jnp.float32,
        )
        for_up = stacked(mixed)
        for j in range(INNER):
            here = pl.ds(pl.multiple_of((place ^ j) * width, width), width)
            out = give_ref if j % 2 else keep_ref
            out[j // 2, :rank, :] = total(for_context, ctx_ref[:, here])
            part = total(for_rest, res_ref[:, here]) + total(for_delta, delta_ref[:, here])
            if j == 0:
                for copy in loads:
                    copy.wait()
            part += total(for_attn, attn_ref[:, here]) + total(for_up, up_ref[:, here])
            out[j // 2, rank:, :] = part

    anywhere = pl.BlockSpec(memory_space=pl.ANY)
    in_vmem = pl.BlockSpec(memory_space=pltpu.VMEM)
    return pl.pallas_call(
        kernel,
        out_shape=[jax.ShapeDtypeStruct((2, 2 * rank, width), jnp.float32)] * 2,
        in_specs=[in_vmem] * 8 + [anywhere] * 2,
        out_specs=[in_vmem] * 2,
        scratch_shapes=[
            pltpu.VMEM((rows, cols), jnp.bfloat16),
            pltpu.VMEM((rank, cols), jnp.bfloat16),
            pltpu.SemaphoreType.DMA((2,)),
        ],
        compiler_params=pltpu.CompilerParams(vmem_limit_bytes=24 * 1024 * 1024),
        cost_estimate=pl.CostEstimate(flops=COST, bytes_accessed=1000, transcendentals=0),
    )(
        sums, came, early_sums, low_t, weights,
        *(pltpu.with_memory_space_constraint(x, pltpu.VMEM) for x in (context, residual, delta)),
        attn, up_weight,
    )


def general_attention(context, output_weight):
    partial = dot_bf16(context, lax.all_gather(output_weight, "dp", axis=1, tiled=True))
    return lax.psum_scatter(partial, "tensor", scatter_dimension=1, tiled=True)


def line_sum_grads(keep, give):
    place = lax.axis_index("dp") % INNER
    rank = keep.shape[1] // 2
    keep = keep + send(give, inner_swap(1))
    both = keep[0] + send(keep[1], inner_swap(2))
    for bits in (1, 2):
        both = both + send(both, lambda z, q, t: (z ^ bits, q, t))
    both = lax.optimization_barrier(both.astype(jnp.bfloat16))
    grad_b = both[rank:]
    other = send(grad_b, other_tensor)
    across = send(both, inner_swap(2))
    across_other = send(grad_b, lambda z, q, t: (z, q ^ 2, 1 - t))

    def joined(bits, mine, got):
        upper = (place & bits) != 0
        return jnp.concatenate(
            [jnp.where(upper, got, mine), jnp.where(upper, mine, got)], axis=1
        )

    mine = jnp.stack([jnp.concatenate([both, other]), jnp.concatenate([across, across_other])])
    got = send(mine, inner_swap(1))
    mine = joined(2, joined(1, mine[0], got[0]), joined(1, mine[1], got[1]))
    mine = mine.astype(jnp.float32)
    grad_a = mine[:rank].T
    kept, other = mine[rank : 2 * rank], mine[2 * rank :]
    first = lax.axis_index("tensor") == 0
    grad_b = jnp.concatenate(
        [jnp.where(first, kept, other), jnp.where(first, other, kept)], axis=1
    )
    return grad_a, grad_b


def general_sum_grads(grad_a_t, grad_b):
    grad_a_t, grad_b = lax.psum((grad_a_t, grad_b), "dp")
    return grad_a_t.T, lax.all_gather(grad_b, "tensor", axis=1, tiled=True)


def solution(mesh):
    line = mesh.shape["dp"] == LAYERS * INNER and mesh.shape["tensor"] == 2

    def sum_tensor(value):
        if line:
            return value + send(value, other_tensor)
        return lax.psum(value, "tensor")

    def local(
        context,
        output_weight,
        adapter_down_weight,
        adapter_up_weight,
        residual,
        frozen_residual_delta,
        harmful_count,
        retain_count,
    ):
        seq_len = context.shape[0]
        tensor_rank = lax.axis_index("tensor")
        data_rank = lax.axis_index("dp")
        harm_total = jnp.sum(harmful_count).astype(jnp.float32)
        keep_total = jnp.sum(retain_count).astype(jnp.float32)
        harm_here = harmful_count[data_rank]
        keep_here = retain_count[data_rank]
        col_count = residual.shape[1]

        low_rank_t = sum_tensor(
            lax.dot_general(
                adapter_down_weight,
                context,
                (((0,), (1,)), ((), ())),
                preferred_element_type=jnp.float32,
            )
        )
        up_narrow = lax.dynamic_slice_in_dim(
            adapter_up_weight, tensor_rank * col_count, col_count, 1
        )
        up_columns = up_narrow.astype(jnp.float32)
        target = residual.astype(jnp.float32) + frozen_residual_delta.astype(jnp.float32)

        def on_up(values):
            return lax.dot_general(
                up_columns, values, (((1,), (1,)), ((), ())), precision=HIGHEST
            )

        rank = up_columns.shape[0]
        early_sums = sum_tensor(
            jnp.concatenate([on_up(target), jnp.sum(target * target, axis=1)[None]], axis=0)
        )
        target_up, sq_target = early_sums[:rank], early_sums[rank]
        positions = jnp.arange(seq_len, dtype=jnp.int32)
        harmful = (positions < harm_here).astype(jnp.float32)
        retained = (
            (positions >= harm_here) & (positions < harm_here + keep_here)
        ).astype(jnp.float32)
        weight_harm = REROUTE_WEIGHT / harm_total * harmful
        weight_keep = RETAIN_WEIGHT / keep_total * retained
        if line:
            weights = jnp.stack([weight_harm, weight_keep])
            constant = (residual, frozen_residual_delta, up_narrow, low_rank_t)
            adapted, attn, sums = line_pieces(
                context,
                output_weight,
                (low_rank_t, early_sums, weights),
                lambda second, start, pieces, before, last: part_states(
                    second, start, pieces, *constant, before, last
                ),
            )
            held = hold(*lax.optimization_barrier((context, residual, frozen_residual_delta, sums))[:3])
            keep, give = line_grads(
                sums,
                send(sums, other_tensor),
                early_sums,
                low_rank_t,
                weights,
                *held,
                attn,
                up_narrow,
            )
            return adapted, *line_sum_grads(keep, give)
        low_up = ADAPTER_SCALE * lax.dot_general(
            low_rank_t, up_columns, (((0,), (0,)), ((), ())), precision=HIGHEST
        )
        attn = general_attention(context, output_weight).astype(jnp.float32)
        states = residual.astype(jnp.float32) + attn + low_up
        adapted = states.astype(jnp.bfloat16)
        gap = states - target
        products = [states * states, states * target, gap * gap]
        sums = jnp.stack([jnp.sum(product, axis=1) for product in products])
        sums = jnp.concatenate([on_up(states), sums], axis=0)
        shared = sum_tensor(sums)
        states_up = shared[:rank]
        sq_state, cross_term, gap_sq = (shared[rank + i] for i in range(3))

        norm_h = jnp.sqrt(sq_state + NORM_EPS)
        norm_g = jnp.sqrt(sq_target + NORM_EPS)
        cosine = cross_term / (norm_h * norm_g)
        distance = jnp.sqrt(gap_sq + NORM_EPS)
        weight_keep = weight_keep / distance
        on_target = weight_harm / (norm_h * norm_g) - weight_keep
        on_states = weight_keep - weight_harm * cosine / (norm_h * norm_h)

        cotangent = on_target[:, None] * target + on_states[:, None] * states
        low_cot_t = ADAPTER_SCALE * (on_target * target_up + on_states * states_up)
        grad_a_t = jnp.dot(low_cot_t, context.astype(jnp.float32), precision=HIGHEST)
        grad_b = ADAPTER_SCALE * jnp.dot(low_rank_t, cotangent, precision=HIGHEST)
        grad_a, grad_b = general_sum_grads(grad_a_t, grad_b)
        return adapted, grad_a, grad_b

    return jax.shard_map(
        local,
        mesh=mesh,
        in_specs=(
            P("dp", "tensor"),
            P("tensor", "dp"),
            P("tensor", None),
            P(),
            P("dp", "tensor"),
            P("dp", "tensor"),
            P(),
            P(),
        ),
        out_specs=(P("dp", "tensor"), P("tensor", None), P()),
        check_vma=False,
    )
```
